512 devices in a mesh: seq: 32 (over y, z_hi, core), clip: 16 (over z_lo, x).
Axes of the slice: x: 4, y: 4, z: 16 (z_hi: 4, z_lo: 4; z = z_hi * 4 + z_lo), core: 2. Of those that a mesh axis runs over, the one named last changes fastest.
Arguments:
- hidden: bfloat16 [16, 32, 128, 1152], P('clip', 'seq'), may hold values from -56 to 56
- exponent: int32 [16, 32], P('clip', 'seq'), may hold values from 2 to 7
- modulation: float32 [16, 2, 3, 1152], P('clip'), may hold values from -3 to 3
- out_grad: bfloat16 [16, 32, 128, 1152], P('clip', 'seq'), may hold values from -6 to 6
- w_qkv: bfloat16 [1152, 3456], P('clip'), may hold values from -0.1875 to 0.1875
- w_out: bfloat16 [1152, 1152], P('clip'), may hold values from -0.1875 to 0.1875
- qk_gain: float32 [2, 72], replicated, may hold values from 0.25 to 1.75
Outputs:
- d_hidden: bfloat16 [16, 32, 128, 1152], P('clip', 'seq')
- grad_out_proj: float32 [1152, 1152], P('seq')
The draws below stay inside these ranges and needn't reach their ends.
All inputs are finite; a program needn't handle non-finite values.
Results may differ from the reference program's by a relative error of at most 0.03.
Values may be sent and summed in bfloat16 or wider, within the bound.
No kernel may reach another device: no remote copies, remote signals or barrier semaphores. Data moves between devices by JAX's collectives and lax.ppermute only.
A program may use at most 128 MiB of HBM per device.

```python
import jax
import jax.numpy as jnp
from jax import lax

D = 1152
HD = 72
FRAMES = 16
S = 128
CLIPS = 2
GROUPS = 16
INNER = 1152
SP_DEV = 4
N_SEQ = 32
N_CLIP = 16


def draw_hidden(key, part):
    key = jax.random.fold_in(key, 7)
    base_key, row_key, column_key = jax.random.split(key, 3)
    shape_all = (GROUPS, CLIPS * FRAMES, S, D)
    column_scale = jnp.exp(jax.random.uniform(column_key, (D,), jnp.float32, jnp.log(0.35), jnp.log(3.5)))
    base_values = jax.random.truncated_normal(base_key, -4.0, 4.0, shape_all, jnp.float32)
    row_scale = jnp.exp(jax.random.uniform(row_key, (GROUPS, CLIPS * FRAMES, S, 1), jnp.float32, jnp.log(0.4), jnp.log(4.0)))
    return (base_values * row_scale * column_scale).astype(jnp.bfloat16)


def with_ends(entries, key, least, high):
    longest = entries.shape.index(max(entries.shape))
    spots = []
    for shift in (0, 1):
        where = [jax.random.randint(jax.random.fold_in(key, axis), (), 0, length) for axis, length in enumerate(entries.shape)]
        where[longest] = (where[longest] + shift) % entries.shape[longest]
        spots.append(tuple(where))
    return entries.at[spots[0]].set(least).at[spots[1]].set(high)


def block_scale(rng, dims, pieces, least, high):
    level, own = 1.0, jax.random.fold_in(rng, 6)
    for axis_at, shards_of in pieces:
        draws = jnp.exp(jax.random.uniform(jax.random.fold_in(own, axis_at), (shards_of,), jnp.float32, least / len(pieces), high / len(pieces)))
        level = level * jnp.repeat(draws, dims[axis_at] // shards_of).reshape([-1 if axis == axis_at else 1 for axis in range(len(dims))])
    return level


def normal_values(rng, shape, scale, bound, cuts=(), kind=jnp.bfloat16):
    drawn = scale * jax.random.normal(rng, shape, jnp.float32)
    if cuts:
        drawn = drawn * block_scale(rng, shape, cuts, -0.22, 0.18)
    return jnp.clip(drawn, -bound, bound).astype(kind)


def setup_inputs(seed: int = 0) -> dict:
    splits = jax.random.split(jax.random.key(seed), 8)
    hidden = draw_hidden(jax.random.fold_in(splits[7], 71), 0)
    exponent = with_ends(jax.random.randint(splits[1], (GROUPS, CLIPS * FRAMES), 2, 8), jax.random.fold_in(splits[1], 1), 2, 7).astype(jnp.int32)
    modulation = normal_values(splits[2], (GROUPS, CLIPS, 3, D), 0.5, 3.0, ((0, 16),), jnp.float32)
    out_grad = normal_values(splits[3], (GROUPS, CLIPS * FRAMES, S, D), 1.0, 6.0, ((0, 16), (1, 32)))
    w_qkv = normal_values(splits[4], (D, 3 * INNER), D ** -0.5, 0.1875, ((0, 16),))
    w_out = normal_values(splits[5], (INNER, D), INNER ** -0.5, 0.1875, ((0, 16),))
    qk_gain = jnp.clip(1.0 + 0.15 * jax.random.normal(splits[6], (2, HD), jnp.float32), 0.25, 1.75)
    return dict(hidden=hidden, exponent=exponent, modulation=modulation, out_grad=out_grad, w_qkv=w_qkv, w_out=w_out, qk_gain=qk_gain)


def rotary_tables(frame_count, head_dim, head_count):
    position = lax.broadcasted_iota(jnp.int32, (frame_count, head_dim), 0).astype(jnp.float32)
    column = lax.broadcasted_iota(jnp.int32, (frame_count, head_dim), 1)
    exponent_part = (2 * (column // 2)).astype(jnp.float32) / head_dim
    frequency = jnp.power(10000.0, -exponent_part)
    angles = position * frequency
    return (jnp.tile(jnp.cos(angles), (1, head_count)), jnp.tile(jnp.sin(angles), (1, head_count)))

def rotate(values):
    shifted_up = jnp.roll(values, -1, axis=-1)
    shifted_down = jnp.roll(values, 1, axis=-1)
    parity = lax.broadcasted_iota(jnp.int32, values.shape, values.ndim - 1) % 2
    return jnp.where(parity == 0, -shifted_up, shifted_down)

def product(form, left, right):
    return jnp.einsum(form, left.astype(jnp.float32), right.astype(jnp.float32))

def branch_pass(row_grid, cotangent, clip_mod, w_qkv, w_out, qk_gain):
    clip_count, frame_count, item_count, model_dim = row_grid.shape
    inner_dim = w_out.shape[0]
    head_dim = qk_gain.shape[1]
    head_count = inner_dim // head_dim
    head_shape = (clip_count, frame_count, item_count, head_count, head_dim)
    shift_row = clip_mod[:, 0][:, None, None, :]
    scale_row = clip_mod[:, 1][:, None, None, :]
    gate_row = clip_mod[:, 2][:, None, None, :]
    row_mean = lax.optimization_barrier(jnp.mean(row_grid, axis=-1, keepdims=True))
    centred = row_grid - row_mean
    norm_factor = lax.rsqrt(lax.optimization_barrier(jnp.mean(centred * centred, axis=-1, keepdims=True)) + 1e-06)
    normed = centred * norm_factor
    modded = (normed * (1.0 + scale_row) + shift_row).astype(jnp.bfloat16)
    packed = jnp.dot(modded.reshape(-1, model_dim), w_qkv, preferred_element_type=jnp.float32).astype(jnp.bfloat16)
    query_raw = packed[:, :inner_dim].astype(jnp.float32)
    key_raw = packed[:, inner_dim:2 * inner_dim].astype(jnp.float32)
    value_rows = packed[:, 2 * inner_dim:]
    cosine_table, sine_table = rotary_tables(frame_count, head_dim, head_count)
    cosine_table = cosine_table[None, :, None, :]
    sine_table = sine_table[None, :, None, :]

    def prepare(raw_rows, gain_values):
        grouped = raw_rows.reshape(-1, head_count, head_dim)
        root_factor = lax.rsqrt(lax.optimization_barrier(jnp.mean(grouped * grouped, axis=-1, keepdims=True)) + 1e-06)
        normal_rows = (grouped * root_factor * gain_values).reshape(clip_count, frame_count, item_count, inner_dim)
        turned = normal_rows * cosine_table + rotate(normal_rows) * sine_table
        return (turned.astype(jnp.bfloat16), root_factor)
    query_hat, query_factor = prepare(query_raw, qk_gain[0])
    key_hat, key_factor = prepare(key_raw, qk_gain[1])
    query_grid = query_hat.reshape(head_shape)
    key_grid = key_hat.reshape(head_shape)
    value_grid = value_rows.reshape(head_shape)
    temper = head_dim ** (-0.5)
    scores = product('cfnhd,cgnhd->cnhfg', query_grid, key_grid) * temper
    exp_scores = jnp.exp(scores)
    prob_full = exp_scores / lax.optimization_barrier(jnp.sum(exp_scores, axis=-1, keepdims=True))
    prob_half = prob_full.astype(jnp.bfloat16)
    attended = product('cnhfg,cgnhd->cfnhd', prob_half, value_grid).astype(jnp.bfloat16)
    attended = attended.reshape(clip_count, frame_count, item_count, inner_dim)
    branch_grad = (gate_row * cotangent.astype(jnp.float32)).astype(jnp.bfloat16)
    grad_attended = jnp.dot(branch_grad.reshape(-1, model_dim), w_out.T, preferred_element_type=jnp.float32).astype(jnp.bfloat16)
    grad_grid = grad_attended.reshape(head_shape)
    grad_prob = product('cfnhd,cgnhd->cnhfg', grad_grid, value_grid)
    grad_value = product('cnhfg,cfnhd->cgnhd', prob_half, grad_grid).astype(jnp.bfloat16)
    grad_score = (prob_full * (grad_prob - lax.optimization_barrier(jnp.sum(prob_full * grad_prob, axis=-1, keepdims=True))) * temper).astype(jnp.bfloat16)
    grad_qhat = product('cnhfg,cgnhd->cfnhd', grad_score, key_grid)
    grad_khat = product('cnhfg,cfnhd->cgnhd', grad_score, query_grid)

    def restore(grad_turned, raw_rows, root_factor, gain_values):
        grad_turned = grad_turned.reshape(clip_count, frame_count, item_count, inner_dim)
        grad_normal = grad_turned * cosine_table - rotate(grad_turned) * sine_table
        scaled_grad = grad_normal.reshape(-1, head_count, head_dim) * gain_values
        grouped = raw_rows.reshape(-1, head_count, head_dim)
        grad_raw = root_factor * scaled_grad - grouped * root_factor ** 3 * lax.optimization_barrier(jnp.mean(grouped * scaled_grad, axis=-1, keepdims=True))
        return grad_raw.reshape(-1, inner_dim).astype(jnp.bfloat16)
    grad_packed = jnp.concatenate([restore(grad_qhat, query_raw, query_factor, qk_gain[0]), restore(grad_khat, key_raw, key_factor, qk_gain[1]), grad_value.reshape(-1, inner_dim)], axis=1)
    grad_modded = jnp.dot(grad_packed, w_qkv.T, preferred_element_type=jnp.float32)
    grad_normed = grad_modded.reshape(clip_count, frame_count, item_count, model_dim) * (1.0 + scale_row)
    grad_rows = norm_factor * (grad_normed - lax.optimization_barrier(jnp.mean(grad_normed, axis=-1, keepdims=True)) - normed * lax.optimization_barrier(jnp.mean(grad_normed * normed, axis=-1, keepdims=True)))
    return (grad_rows.astype(jnp.bfloat16), attended, branch_grad)

def reference(hidden, exponent, modulation, out_grad, w_qkv, w_out, qk_gain):

    def one_group(grad_total, group_data):
        group_hidden, group_exponent, group_mod, group_cot = group_data
        power_scale = jnp.exp2(group_exponent.astype(jnp.float32))
        scaled = jnp.clip(group_hidden.astype(jnp.float32) * power_scale[:, None, None], -448.0, 448.0).astype(jnp.bfloat16)
        restored = lax.optimization_barrier(scaled).astype(jnp.float32) * (1.0 / power_scale)[:, None, None]
        frames_all = restored.shape[0]
        clip_count = group_mod.shape[0]
        frame_count = frames_all // clip_count
        row_grid = restored.reshape(clip_count, frame_count, S, D)
        cot_grid = group_cot.reshape(clip_count, frame_count, S, D)
        grad_rows, attended, branch_grad = branch_pass(row_grid, cot_grid, group_mod, w_qkv, w_out, qk_gain)
        attended_blocks = attended.reshape(frames_all, N_SEQ, SP_DEV, INNER).astype(jnp.float32)
        grad_blocks = branch_grad.reshape(frames_all, N_SEQ, SP_DEV, D).astype(jnp.float32)
        device_terms = jnp.einsum('fsui,fsud->sid', attended_blocks, grad_blocks)
        rounded = lax.optimization_barrier(device_terms.astype(jnp.bfloat16)).astype(jnp.float32)
        grad_total = grad_total + lax.optimization_barrier(jnp.sum(rounded, axis=0))
        group_out = (group_cot.astype(jnp.float32) + grad_rows.reshape(frames_all, S, D).astype(jnp.float32)).astype(jnp.bfloat16)
        return (grad_total, group_out)
    zero_grad = jnp.zeros((INNER, D), jnp.float32)
    grad_total, d_hidden = lax.scan(one_group, zero_grad, (hidden, exponent, modulation, out_grad))
    return (d_hidden, grad_total / (CLIPS * N_CLIP))
```

```python
import jax
import jax.numpy as jnp
from jax import lax
from jax.experimental import pallas as pl
from jax.experimental.pallas import tpu as pltpu
from jax.sharding import Mesh
from jax.sharding import PartitionSpec as P

FINE = (("yh", 2), ("yl", 2), ("zh", 4), ("c", 2), ("zl", 4), ("x", 4))
SEQ = ("yh", "yl", "zh", "c")
CLIP = ("zl", "x")
D = 1152
HD = 72
HALF = 576
WIDE = 640
PEERS = 8
TOK = 16
ROWS = PEERS * TOK
ALL = 2 * ROWS
F32 = jnp.float32
BF16 = jnp.bfloat16
EPS = 1e-06
TEMPER = HD ** (-0.5)
PARAMS = pltpu.CompilerParams(vmem_limit_bytes=56 * 1024 * 1024)


def cost(flops, nbytes):
    return pl.CostEstimate(flops=flops, bytes_accessed=nbytes, transcendentals=0)


def normalise(hidden, power, inverse):
    scaled = jnp.clip(hidden.astype(F32) * power, -448.0, 448.0)
    rows = scaled * inverse
    centred = rows - jnp.mean(rows, axis=-1, keepdims=True)
    factor = lax.rsqrt(jnp.mean(centred * centred, axis=-1, keepdims=True) + EPS)
    return centred * factor, factor


def home_forward(power_ref, hidden_ref, grad_ref, mod_ref, out_ref):
    normed, _ = normalise(hidden_ref[...], power_ref[0], power_ref[1])
    modded = (normed * (1.0 + mod_ref[1:2, :]) + mod_ref[0:1, :]).astype(BF16)
    branch = (mod_ref[2:3, :] * grad_ref[...].astype(F32)).astype(BF16)
    out_ref[:, 0:TOK, :] = modded.reshape(PEERS, TOK, D)
    out_ref[:, TOK : 2 * TOK, :] = branch.reshape(PEERS, TOK, D)


def home_backward(power_ref, hidden_ref, grad_ref, mod_ref, back_ref, out_ref):
    normed, factor = normalise(hidden_ref[...], power_ref[0], power_ref[1])
    d_normed = back_ref[...].astype(F32) * (1.0 + mod_ref[1:2, :])
    d_rows = factor * (
        d_normed
        - jnp.mean(d_normed, axis=-1, keepdims=True)
        - normed * jnp.mean(d_normed * normed, axis=-1, keepdims=True)
    )
    out_ref[...] = (grad_ref[...].astype(F32) + d_rows.astype(BF16).astype(F32)).astype(BF16)


def nt(left, right):
    return lax.dot_general(left, right, (((1,), (1,)), ((), ())), preferred_element_type=F32)


def nn(left, right):
    return lax.dot_general(left, right, (((1,), (0,)), ((), ())), preferred_element_type=F32)


def tn(left, right):
    return lax.dot_general(left, right, (((0,), (0,)), ((), ())), preferred_element_type=F32)


def swap_pairs(values):
    parity = lax.broadcasted_iota(jnp.int32, (values.shape[0], 128), 1) % 2
    tiles = []
    for start in range(0, values.shape[1], 128):
        tile = values[:, start : start + 128]
        tiles.append(jnp.where(parity == 0, pltpu.roll(tile, 127, 1), pltpu.roll(tile, 1, 1)))
    return jnp.concatenate(tiles, axis=1)


def head_members():
    entry = lax.broadcasted_iota(jnp.int32, (WIDE, 128), 0)
    first = lax.broadcasted_iota(jnp.int32, (WIDE, 128), 1) * HD
    return ((entry >= first) & (entry < first + HD) & (entry < HALF)).astype(F32).astype(BF16)


def split_dot(dot, values, members):
    high = values.astype(BF16)
    low = (values - high.astype(F32)).astype(BF16)
    return dot(high, members) + dot(low, members)


def window(head):
    start = head * HD // 128 * 128
    end = -(-(head + 1) * HD // 128) * 128
    column = lax.broadcasted_iota(jnp.int32, (ALL, end - start), 1) + start
    return start, end, (column >= head * HD) & (column < (head + 1) * HD)


def keep(values, mask):
    return jnp.where(mask, values, jnp.zeros_like(values))


def same_token():
    row = lax.broadcasted_iota(jnp.int32, (ALL, ALL), 0) % TOK
    column = lax.broadcasted_iota(jnp.int32, (ALL, ALL), 1) % TOK
    return row == column


def probabilities(q_hat_ref, k_hat_ref, head, same):
    start, end, mask = window(head)
    scores = nt(keep(q_hat_ref[:, start:end], mask), k_hat_ref[:, start:end]) * TEMPER
    exps = jnp.where(same, jnp.exp(scores), 0.0)
    return exps / jnp.sum(exps, axis=-1, keepdims=True)


def gather_rows(own_ref, other_ref, first):
    return jnp.concatenate(
        [ref[:, first : first + TOK, :].reshape(ROWS, D) for ref in (own_ref, other_ref)], axis=0
    )


def widen(values):
    return jnp.concatenate([values, jnp.zeros((ALL, WIDE - HALF), values.dtype)], axis=1)


def chip_forward(
    own_ref, other_ref, w_ref, tab_ref, part_ref, q_ref, k_ref, v_ref, qh_ref, kh_ref, qf_ref, kf_ref, att_ref
):
    modded = gather_rows(own_ref, other_ref, 0)
    members = head_members()
    for place, (raw_ref, hat_ref, factor_ref) in enumerate(((q_ref, qh_ref, qf_ref), (k_ref, kh_ref, kf_ref))):
        raw = widen(nn(modded, w_ref[place]).astype(BF16))
        raw_ref[...] = raw
        raw = raw.astype(F32)
        factor = lax.rsqrt(split_dot(nn, raw * raw, members) / HD + EPS)
        factor_ref[...] = factor
        turned = raw * tab_ref[2 * place] + swap_pairs(raw) * tab_ref[2 * place + 1]
        hat_ref[...] = (split_dot(nt, factor, members) * turned).astype(BF16)
    v_ref[...] = widen(nn(modded, w_ref[2]).astype(BF16))
    same = same_token()
    att_ref[...] = jnp.zeros_like(att_ref)
    for head in range(8):
        start, end, mask = window(head)
        probs = probabilities(qh_ref, kh_ref, head, same).astype(BF16)
        found = nn(probs, v_ref[:, start:end]).astype(BF16)
        att_ref[:, start:end] = jnp.where(mask, found, att_ref[:, start:end])
    branch = gather_rows(own_ref, other_ref, TOK)
    part_ref[...] = tn(att_ref[...], branch)[:HALF].astype(BF16)


def chip_backward(
    own_ref, other_ref, w_ref, wo_ref, tab_ref, q_ref, k_ref, v_ref, qh_ref, kh_ref, qf_ref, kf_ref,
    mine_ref, theirs_ref, do_ref, dv_ref, dqh_ref, dkh_ref,
):
    branch = gather_rows(own_ref, other_ref, TOK)
    do_ref[...] = widen(nt(branch, wo_ref[...]).astype(BF16))
    same = same_token()
    members = head_members()
    for ref in (dv_ref, dqh_ref, dkh_ref):
        ref[...] = jnp.zeros_like(ref)
    for head in range(8):
        start, end, mask = window(head)
        probs = probabilities(qh_ref, kh_ref, head, same)
        d_out = do_ref[:, start:end]
        d_probs = nt(keep(d_out, mask), v_ref[:, start:end])
        d_value = tn(probs.astype(BF16), d_out)
        spread = probs * d_probs
        d_scores = ((spread - probs * jnp.sum(spread, axis=-1, keepdims=True)) * TEMPER).astype(BF16)
        d_q = nn(d_scores, kh_ref[:, start:end])
        d_k = tn(d_scores, qh_ref[:, start:end])
        dv_ref[:, start:end] = jnp.where(mask, d_value.astype(BF16), dv_ref[:, start:end])
        dqh_ref[:, start:end] = jnp.where(mask, d_q, dqh_ref[:, start:end])
        dkh_ref[:, start:end] = jnp.where(mask, d_k, dkh_ref[:, start:end])
    total = nt(dv_ref[:, :HALF], w_ref[2])
    for place, (raw_ref, factor_ref, turned_ref) in enumerate(
        ((q_ref, qf_ref, dqh_ref), (k_ref, kf_ref, dkh_ref))
    ):
        raw = raw_ref[...].astype(F32)
        factor = factor_ref[...]
        turned = turned_ref[...]
        scaled = turned * tab_ref[2 * place] + swap_pairs(turned) * tab_ref[2 * place + 1]
        inner = split_dot(nn, raw * scaled, members) / HD
        wide = split_dot(nt, factor, members)
        pulled = split_dot(nt, factor * factor * factor * inner, members)
        d_raw = (wide * scaled - raw * pulled).astype(BF16)
        total = total + nt(d_raw[:, :HALF], w_ref[place])
    mine_ref[...] = total[:ROWS].reshape(PEERS, TOK, D)
    theirs_ref[...] = total[ROWS:].reshape(PEERS, TOK, D).astype(BF16)


def turn_tables(qk_gain, core):
    frame = 2 * jnp.arange(PEERS, dtype=jnp.int32)
    position = jnp.concatenate([frame + core, frame + 1 - core]).astype(F32)
    column = jnp.arange(HD, dtype=jnp.int32)
    frequency = jnp.power(10000.0, -((2 * (column // 2)).astype(F32) / HD))
    angles = position[:, None] * frequency[None, :]
    cosine, sine = jnp.cos(angles), jnp.sin(angles)
    even = column % 2 == 0
    swapped = qk_gain.reshape(2, HD // 2, 2)[:, :, ::-1].reshape(2, HD)

    def spread(table):
        table = jnp.pad(jnp.tile(table, (1, 1, HALF // HD)), ((0, 0), (0, 0), (0, WIDE - HALF)))
        return jnp.broadcast_to(table[:, :, None, :], (4, 2 * PEERS, TOK, WIDE)).reshape(4, ALL, WIDE)

    straight = [qk_gain[i] * cosine for i in range(2)]
    ahead = [jnp.where(even, -sine, sine) * swapped[i] for i in range(2)]
    back = [jnp.where(even, sine, -sine) * qk_gain[i] for i in range(2)]
    return (
        spread(jnp.stack([straight[0], ahead[0], straight[1], ahead[1]])),
        spread(jnp.stack([straight[0], back[0], straight[1], back[1]])),
    )


def on_device(hidden, exponent, modulation, out_grad, w_qkv, w_out, qk_gain):
    core = lax.axis_index("c")
    zh = lax.axis_index("zh")
    rows, cotangent = hidden[0, 0], out_grad[0, 0]
    shift_by = exponent[0, 0]
    power = jnp.stack(
        [
            lax.shift_left(jnp.int32(1), shift_by).astype(F32),
            lax.shift_left(jnp.int32(1), 24 - shift_by).astype(F32) * 2.0**-24,
        ]
    )
    mod = lax.dynamic_index_in_dim(modulation[0], lax.axis_index("yh"), 0, keepdims=False)

    qkv_heads = w_qkv.reshape(HD, 3, 4, 2, 2 * HD)
    qkv_mine = lax.dynamic_index_in_dim(qkv_heads, core, 3, keepdims=False).reshape(HD, 3 * HALF)
    qkv_full = lax.all_gather(qkv_mine, CLIP, axis=0, tiled=True)
    out_full = lax.all_gather(w_out, CLIP, axis=0, tiled=True)
    w_in = jnp.stack([qkv_full[:, i * HALF : (i + 1) * HALF] for i in range(3)])
    w_back = lax.dynamic_index_in_dim(out_full.reshape(4, 2, 2 * HD, D), core, 1, keepdims=False).reshape(HALF, D)

    smem = pl.BlockSpec(memory_space=pltpu.SMEM)
    vmem = pl.BlockSpec(memory_space=pltpu.VMEM)
    sent = pl.pallas_call(
        home_forward,
        out_shape=jax.ShapeDtypeStruct((PEERS, 2 * TOK, D), BF16),
        in_specs=[smem, vmem, vmem, vmem],
        out_specs=vmem,
        compiler_params=PARAMS,
        cost_estimate=cost(20 * ROWS * D, 8 * ROWS * D),
    )(power, rows, cotangent, mod)
    own = lax.all_to_all(sent, ("yl", "zh"), 0, 0, tiled=True)
    other = lax.ppermute(own, "c", [(0, 1), (1, 0)])

    tables, tables_back = turn_tables(qk_gain, core)
    wide = jax.ShapeDtypeStruct((ALL, WIDE), BF16)
    factors = jax.ShapeDtypeStruct((ALL, 128), F32)
    part, *kept = pl.pallas_call(
        chip_forward,
        out_shape=[jax.ShapeDtypeStruct((HALF, D), BF16)] + [wide] * 5 + [factors] * 2,
        in_specs=[vmem] * 4,
        out_specs=[vmem] * 8,
        scratch_shapes=[pltpu.VMEM((ALL, WIDE), BF16)],
        compiler_params=PARAMS,
        cost_estimate=cost(2 * ALL * D * 4 * HALF, 12 * 10**6),
    )(own, other, w_in, tables)

    pieces = part.reshape(4, 4, 36, D).reshape(16, 36, D)
    plane = lax.all_to_all(pieces, ("yh", "yl", "x"), 0, 0, tiled=True)
    plane = jnp.sum(plane.astype(F32), axis=0).astype(BF16)
    plane = jnp.pad(plane, ((0, 12), (0, 0))).reshape(16, 3, D)

    mine, theirs = pl.pallas_call(
        chip_backward,
        out_shape=[jax.ShapeDtypeStruct((PEERS, TOK, D), F32), jax.ShapeDtypeStruct((PEERS, TOK, D), BF16)],
        in_specs=[vmem] * 12,
        out_specs=[vmem] * 2,
        scratch_shapes=[
            pltpu.VMEM((ALL, WIDE), BF16),
            pltpu.VMEM((ALL, WIDE), BF16),
            pltpu.VMEM((ALL, WIDE), F32),
            pltpu.VMEM((ALL, WIDE), F32),
        ],
        compiler_params=PARAMS,
        cost_estimate=cost(2 * ALL * D * 4 * HALF, 14 * 10**6),
    )(own, other, w_in, w_back, tables_back, *kept)
    arrived = lax.ppermute(theirs, "c", [(0, 1), (1, 0)])
    summed = (mine + arrived.astype(F32)).astype(BF16)
    back = lax.all_to_all(summed, ("yl", "zh"), 0, 0, tiled=True).reshape(ROWS, D)
    d_hidden = pl.pallas_call(
        home_backward,
        out_shape=jax.ShapeDtypeStruct((ROWS, D), BF16),
        in_specs=[smem, vmem, vmem, vmem, vmem],
        out_specs=vmem,
        compiler_params=PARAMS,
        cost_estimate=cost(30 * ROWS * D, 8 * ROWS * D),
    )(power, rows, cotangent, mod, back)

    levels = lax.all_to_all(plane, ("zh", "zl"), 0, 0, tiled=True)
    level = jnp.sum(levels.astype(F32), axis=0).astype(BF16)
    spread = lax.all_to_all(jnp.broadcast_to(level[None], (8, 3, D)), ("c", "x"), 0, 0, tiled=True)
    wanted = lax.dynamic_index_in_dim(spread.reshape(4, 2, 3, D), core, 1, keepdims=False)
    wanted = jnp.broadcast_to(wanted[:, None], (4, 4, 3, D)).reshape(16, 3, D)
    final = lax.all_to_all(wanted, ("zh", "zl"), 0, 0, tiled=True).reshape(48, D)[:36]
    return d_hidden[None, None], final.astype(F32) / 32.0


def solution(mesh):
    fine = Mesh(mesh.devices.reshape([size for _, size in FINE]), [name for name, _ in FINE])
    placed = (
        P(CLIP, SEQ, None, None),
        P(CLIP, SEQ),
        P(CLIP, None, None, None),
        P(CLIP, SEQ, None, None),
        P(CLIP, None),
        P(CLIP, None),
        P(),
    )
    return jax.shard_map(
        on_device,
        mesh=fine,
        in_specs=placed,
        out_specs=(P(CLIP, SEQ, None, None), P(SEQ, None)),
        check_vma=False,
    )
```

```python
import jax
import jax.numpy as jnp
from jax import lax
from jax.experimental import pallas as pl
from jax.experimental.pallas import tpu as pltpu
from jax.sharding import Mesh
from jax.sharding import PartitionSpec as P

FINE = (("yh", 2), ("yl", 2), ("zh", 4), ("c", 2), ("zl", 4), ("x", 4))
SEQ = ("yh", "yl", "zh", "c")
CLIP = ("zl", "x")
D = 1152
HD = 72
PART = 288
WIDE = 384
HEADS = 4
ZS = 4
TOK = 32
ROWS = ZS * TOK
ALL = 4 * ROWS
BLOCK = 256
F32 = jnp.float32
BF16 = jnp.bfloat16
EPS = 1e-06
TEMPER = HD ** (-0.5)
PARAMS = pltpu.CompilerParams(vmem_limit_bytes=56 * 1024 * 1024)


def cost(flops, nbytes):
    return pl.CostEstimate(flops=flops, bytes_accessed=nbytes, transcendentals=0)


def normalise(hidden, power, inverse):
    scaled = jnp.clip(hidden.astype(F32) * power, -448.0, 448.0)
    rows = scaled * inverse
    centred = rows - jnp.mean(rows, axis=-1, keepdims=True)
    factor = lax.rsqrt(jnp.mean(centred * centred, axis=-1, keepdims=True) + EPS)
    return centred * factor, factor


def home_forward(power_ref, x_ref, hidden_ref, grad_ref, mod_ref, out_ref, branch_ref, turned_ref):
    normed, _ = normalise(hidden_ref[...], power_ref[0], power_ref[1])
    modded = normed * (1.0 + mod_ref[1:2, :]) + mod_ref[0:1, :]
    for x in range(4):

        @pl.when(x_ref[0] == x)
        def _(x=x):
            for place, block in enumerate(block_order(x)):
                turned_ref[:, place * HD : (place + 1) * HD] = modded[:, block * HD : (block + 1) * HD]

    out_ref[...] = turned_ref[...].astype(BF16).reshape(ZS, TOK, D)
    branch_ref[...] = (mod_ref[2:3, :] * grad_ref[...].astype(F32)).astype(BF16).reshape(ZS, TOK, D)


def home_backward(power_ref, x_ref, hidden_ref, grad_ref, mod_ref, back_ref, out_ref, turned_ref):
    normed, factor = normalise(hidden_ref[...], power_ref[0], power_ref[1])
    back = back_ref[...].astype(F32)
    for x in range(4):

        @pl.when(x_ref[0] == x)
        def _(x=x):
            for place, block in enumerate(block_order(x)):
                turned_ref[:, block * HD : (block + 1) * HD] = back[:, place * HD : (place + 1) * HD]

    d_normed = turned_ref[...] * (1.0 + mod_ref[1:2, :])
    d_rows = factor * (
        d_normed
        - jnp.mean(d_normed, axis=-1, keepdims=True)
        - normed * jnp.mean(d_normed * normed, axis=-1, keepdims=True)
    )
    out_ref[...] = (grad_ref[...].astype(F32) + d_rows.astype(BF16).astype(F32)).astype(BF16)


def block_order(x):
    return [4 * zl + (x + step) % 4 for step in range(4) for zl in range(4)]


def pick_weights(place_ref, w_qkv_ref, w_out_ref, out_ref, unit_ref):
    qkv = w_qkv_ref[...].astype(F32)
    out = w_out_ref[...].astype(F32)
    for place in range(4):

        @pl.when(place_ref[0] == place)
        def _(place=place):
            yl, core = place // 2, place % 2
            for part in range(3):
                for high in range(2):
                    first = part * D + HD * (4 * (2 * high + yl) + 2 * core)
                    to = part * PART + high * 2 * HD
                    unit_ref[:, to : to + 2 * HD] = qkv[:, first : first + 2 * HD]
            unit_ref[:, 3 * PART :] = out[:, place * PART : (place + 1) * PART]

    unit = unit_ref[...].astype(BF16)
    for copy in range(4):
        out_ref[copy] = unit


def out_rows(x_ref, *refs):
    *block_refs, send_ref, rows_ref, sem = refs
    copies = [
        pltpu.make_async_copy(ref.at[:, pl.ds(768, 384)], rows_ref.at[step], sem.at[step])
        for step, ref in enumerate(block_refs)
    ]
    for copy in copies:
        copy.start()
    for copy in copies:
        copy.wait()
    blocks = [rows_ref[step].astype(F32)[:, 96:384] for step in range(4)]
    for x in range(4):

        @pl.when(x_ref[0] == x)
        def _(x=x):
            for place in range(4):
                yl, core = place // 2, place % 2
                pieces = []
                for high in range(2):
                    for low in range(2):
                        first = (2 * high + yl) * HD
                        pieces.append(blocks[(2 * core + low - x) % 4][first : first + HD])
                send_ref[place] = jnp.concatenate(pieces, axis=0).astype(BF16)


def nt(left, right):
    return lax.dot_general(left, right, (((1,), (1,)), ((), ())), preferred_element_type=F32)


def nn(left, right):
    return lax.dot_general(left, right, (((1,), (0,)), ((), ())), preferred_element_type=F32)


def tn(left, right):
    return lax.dot_general(left, right, (((0,), (0,)), ((), ())), preferred_element_type=F32)


def swap_pairs(values):
    parity = lax.broadcasted_iota(jnp.int32, (values.shape[0], 128), 1) % 2
    tiles = []
    for start in range(0, values.shape[1], 128):
        tile = values[:, start : start + 128]
        tiles.append(jnp.where(parity == 0, pltpu.roll(tile, 127, 1), pltpu.roll(tile, 1, 1)))
    return jnp.concatenate(tiles, axis=1)


def head_members():
    entry = lax.broadcasted_iota(jnp.int32, (WIDE, 128), 0)
    first = lax.broadcasted_iota(jnp.int32, (WIDE, 128), 1) * HD
    return ((entry >= first) & (entry < first + HD) & (entry < PART)).astype(F32).astype(BF16)


def split_dot(dot, values, members):
    high = values.astype(BF16)
    low = (values - high.astype(F32)).astype(BF16)
    return dot(high, members) + dot(low, members)


def window(head):
    start = head * HD // 128 * 128
    end = -(-(head + 1) * HD // 128) * 128
    column = lax.broadcasted_iota(jnp.int32, (BLOCK, end - start), 1) + start
    return start, end, (column >= head * HD) & (column < (head + 1) * HD)


def keep(values, mask):
    return jnp.where(mask, values, jnp.zeros_like(values))


def same_token():
    row = lax.broadcasted_iota(jnp.int32, (BLOCK, BLOCK), 0) % 16
    column = lax.broadcasted_iota(jnp.int32, (BLOCK, BLOCK), 1) % 16
    return row == column


def probabilities(q_hat, k_hat, same):
    scores = nt(q_hat, k_hat) * TEMPER
    exps = jnp.where(same, jnp.exp(scores), 0.0)
    return exps / jnp.sum(exps, axis=-1, keepdims=True)


def gather_rows(refs):
    return jnp.concatenate(
        [ref[:, first : first + 16, :].reshape(ZS * 16, D) for first in (0, 16) for ref in refs], axis=0
    )


def fetch_weights(block_refs, w_ref, sem):
    copies = [
        pltpu.make_async_copy(ref, w_ref.at[pl.ds(PART * step, PART), :], sem.at[step])
        for step, ref in enumerate(block_refs)
    ]
    for copy in copies:
        copy.start()
    return copies


def widen(values):
    return jnp.concatenate([values, jnp.zeros((values.shape[0], WIDE - PART), values.dtype)], axis=1)


def chip_forward(*refs):
    row_refs, block_refs, (tab_ref, q_ref, k_ref, v_ref, qh_ref, kh_ref, qf_ref, kf_ref, att_ref, w_ref, sem) = (
        refs[:4], refs[4:8], refs[8:]
    )
    copies = fetch_weights(block_refs, w_ref, sem)
    modded = gather_rows(row_refs)
    members = head_members()
    for copy in copies:
        copy.wait()
    packed = nn(modded, w_ref[:, : 7 * 128])
    for place, (raw_ref, hat_ref, factor_ref) in enumerate(((q_ref, qh_ref, qf_ref), (k_ref, kh_ref, kf_ref))):
        raw = widen(packed[:, place * PART : (place + 1) * PART])
        raw_ref[...] = raw.astype(BF16)
        raw = raw_ref[...].astype(F32)
        factor = lax.rsqrt(split_dot(nn, raw * raw, members) / HD + EPS)
        factor_ref[...] = factor
        wide = split_dot(nt, factor, members)
        swapped = swap_pairs(raw)
        for half in range(2):
            rows = slice(half * BLOCK, (half + 1) * BLOCK)
            turned = raw[rows] * tab_ref[2 * place] + swapped[rows] * tab_ref[2 * place + 1]
            hat_ref[rows, :] = (wide[rows] * turned).astype(BF16)
    v_ref[...] = widen(packed[:, 2 * PART : 3 * PART]).astype(BF16)
    same = same_token()
    att_ref[...] = jnp.zeros_like(att_ref)
    for head in range(HEADS):
        start, end, mask = window(head)
        for half in range(2):
            rows = slice(half * BLOCK, (half + 1) * BLOCK)
            probs = probabilities(keep(qh_ref[rows, start:end], mask), kh_ref[rows, start:end], same).astype(BF16)
            found = nn(probs, v_ref[rows, start:end]).astype(BF16)
            att_ref[rows, start:end] = jnp.where(mask, found, att_ref[rows, start:end])


def chip_term(*refs):
    row_refs, (att_ref, part_ref) = refs[:4], refs[4:]
    part_ref[...] = tn(att_ref[...], gather_rows(row_refs))[:PART].astype(BF16)


def chip_backward(*refs):
    row_refs, block_refs = refs[:4], refs[4:8]
    (
        wo_ref, tab_ref, q_ref, k_ref, v_ref, qh_ref, kh_ref, qf_ref, kf_ref,
        mine_ref, theirs_ref, do_ref, dv_ref, dqh_ref, dkh_ref, dqkv_ref, wide_ref, w_ref, sem,
    ) = refs[8:]
    copies = fetch_weights(block_refs, w_ref, sem)
    for place in range(4):
        wide_ref[:, place * PART : (place + 1) * PART] = wo_ref[place].astype(F32)
    do_ref[...] = widen(nt(gather_rows(row_refs), wide_ref[...].astype(BF16))).astype(BF16)
    same = same_token()
    members = head_members()
    for ref in (dv_ref, dqh_ref, dkh_ref):
        ref[...] = jnp.zeros_like(ref)
    for head in range(HEADS):
        start, end, mask = window(head)
        for half in range(2):
            rows = slice(half * BLOCK, (half + 1) * BLOCK)
            q_hat, k_hat = qh_ref[rows, start:end], kh_ref[rows, start:end]
            probs = probabilities(keep(q_hat, mask), k_hat, same)
            d_out = do_ref[rows, start:end]
            d_probs = nt(keep(d_out, mask), v_ref[rows, start:end])
            d_value = tn(probs.astype(BF16), d_out)
            spread = probs * d_probs
            d_scores = ((spread - probs * jnp.sum(spread, axis=-1, keepdims=True)) * TEMPER).astype(BF16)
            d_q = nn(d_scores, k_hat)
            d_k = tn(d_scores, q_hat)
            dv_ref[rows, start:end] = jnp.where(mask, d_value, dv_ref[rows, start:end])
            dqh_ref[rows, start:end] = jnp.where(mask, d_q, dqh_ref[rows, start:end])
            dkh_ref[rows, start:end] = jnp.where(mask, d_k, dkh_ref[rows, start:end])
    dqkv_ref[:, 3 * PART :] = jnp.zeros((ALL, 7 * 128 - 3 * PART), F32)
    dqkv_ref[:, 2 * PART : 3 * PART] = dv_ref[:, :PART]
    for place, (raw_ref, factor_ref, turned_ref) in enumerate(
        ((q_ref, qf_ref, dqh_ref), (k_ref, kf_ref, dkh_ref))
    ):
        raw = raw_ref[...].astype(F32)
        factor = factor_ref[...]
        turned = turned_ref[...]
        swapped = swap_pairs(turned)
        scaled = jnp.concatenate(
            [
                turned[first : first + BLOCK] * tab_ref[2 * place]
                + swapped[first : first + BLOCK] * tab_ref[2 * place + 1]
                for first in (0, BLOCK)
            ],
            axis=0,
        )
        inner = split_dot(nn, raw * scaled, members) / HD
        wide = split_dot(nt, factor, members)
        pulled = split_dot(nt, factor * factor * factor * inner, members)
        dqkv_ref[:, place * PART : (place + 1) * PART] = (wide * scaled - raw * pulled)[:, :PART]
    for copy in copies:
        copy.wait()
    total = nt(dqkv_ref[...].astype(BF16), w_ref[:, : 7 * 128])
    for half in range(2):
        for device in range(4):
            first = half * BLOCK + device * ZS * 16
            rows = total[first : first + ZS * 16].reshape(ZS, 16, D)
            out_ref = theirs_ref if device % 2 else mine_ref
            out_ref[device // 2, :, half * 16 : half * 16 + 16, :] = rows.astype(out_ref.dtype)


def turn_tables(qk_gain, yl, core):
    level = 2 * jnp.arange(ZS, dtype=jnp.int32)
    position = jnp.concatenate(
        [8 * y + level + c for y in (yl, 1 - yl) for c in (core, 1 - core)]
    ).astype(F32)
    column = jnp.arange(HD, dtype=jnp.int32)
    frequency = jnp.power(10000.0, -((2 * (column // 2)).astype(F32) / HD))
    angles = position[:, None] * frequency[None, :]
    cosine, sine = jnp.cos(angles), jnp.sin(angles)
    even = column % 2 == 0
    swapped = qk_gain.reshape(2, HD // 2, 2)[:, :, ::-1].reshape(2, HD)

    def spread(table):
        table = jnp.pad(jnp.tile(table, (1, 1, HEADS)), ((0, 0), (0, 0), (0, WIDE - PART)))
        return jnp.broadcast_to(table[:, :, None, :], (4, 16, 16, WIDE)).reshape(4, BLOCK, WIDE)

    straight = [qk_gain[i] * cosine for i in range(2)]
    ahead = [jnp.where(even, -sine, sine) * swapped[i] for i in range(2)]
    back = [jnp.where(even, sine, -sine) * qk_gain[i] for i in range(2)]
    return (
        spread(jnp.stack([straight[0], ahead[0], straight[1], ahead[1]])),
        spread(jnp.stack([straight[0], back[0], straight[1], back[1]])),
    )


def on_device(hidden, exponent, modulation, out_grad, w_qkv, w_out, qk_gain):
    core, yl, x = lax.axis_index("c"), lax.axis_index("yl"), lax.axis_index("x")
    rows, cotangent = hidden[0, 0], out_grad[0, 0]
    shift_by = exponent[0, 0]
    power = jnp.stack(
        [
            lax.shift_left(jnp.int32(1), shift_by).astype(F32),
            lax.shift_left(jnp.int32(1), 24 - shift_by).astype(F32) * 2.0**-24,
        ]
    )
    mod = lax.dynamic_index_in_dim(modulation[0], lax.axis_index("yh"), 0, keepdims=False)
    x_place = x[None]
    smem = pl.BlockSpec(memory_space=pltpu.SMEM)
    vmem = pl.BlockSpec(memory_space=pltpu.VMEM)
    hbm = pl.BlockSpec(memory_space=pl.ANY)
    four = pltpu.SemaphoreType.DMA((4,))

    unit = pl.pallas_call(
        pick_weights,
        out_shape=jax.ShapeDtypeStruct((4, HD, 4 * PART), BF16),
        in_specs=[smem, vmem, vmem],
        out_specs=vmem,
        scratch_shapes=[pltpu.VMEM((HD, 4 * PART), F32)],
        compiler_params=PARAMS,
        cost_estimate=cost(10**6, 2 * 10**6),
    )((2 * yl + core)[None], w_qkv, w_out)
    block = lax.all_to_all(unit, "zl", 0, 0, tiled=True).reshape(PART, 4 * PART)
    blocks = [block] + [
        lax.ppermute(block, "x", [(i, (i + 4 - step) % 4) for i in range(4)]) for step in (1, 2, 3)
    ]

    sent, sent_branch = pl.pallas_call(
        home_forward,
        out_shape=[jax.ShapeDtypeStruct((ZS, TOK, D), BF16)] * 2,
        in_specs=[smem, smem, vmem, vmem, vmem],
        out_specs=[vmem, vmem],
        scratch_shapes=[pltpu.VMEM((ROWS, D), F32)],
        compiler_params=PARAMS,
        cost_estimate=cost(20 * ROWS * D, 8 * ROWS * D),
    )(power, x_place, rows, cotangent, mod)

    def other_core(values):
        return lax.ppermute(values, "c", [(0, 1), (1, 0)])

    def other_y(values):
        return lax.ppermute(values, "yl", [(0, 1), (1, 0)])

    def from_frames(values):
        own = lax.all_to_all(values, "zh", 0, 0, tiled=True)
        across = other_y(own)
        return [own, other_core(own), across, other_core(across)]

    modded = from_frames(sent)
    branch = from_frames(sent_branch)
    w_back = pl.pallas_call(
        out_rows,
        out_shape=jax.ShapeDtypeStruct((4, PART, PART), BF16),
        in_specs=[smem] + [hbm] * 4,
        out_specs=vmem,
        scratch_shapes=[pltpu.VMEM((4, PART, 384), BF16), four],
        compiler_params=PARAMS,
        cost_estimate=cost(10**6, 2 * 10**6),
    )(x_place, *blocks)
    w_back = lax.all_to_all(w_back, ("yl", "c"), 0, 0, tiled=True)

    tables, tables_back = turn_tables(qk_gain, yl, core)
    wide = jax.ShapeDtypeStruct((ALL, WIDE), BF16)
    factors = jax.ShapeDtypeStruct((ALL, 128), F32)
    *kept, attended = pl.pallas_call(
        chip_forward,
        out_shape=[wide] * 5 + [factors] * 2 + [wide],
        in_specs=[vmem] * 4 + [hbm] * 4 + [vmem],
        out_specs=[vmem] * 8,
        scratch_shapes=[pltpu.VMEM((D, D), BF16), four],
        compiler_params=PARAMS,
        cost_estimate=cost(2 * ALL * D * 4 * PART, 12 * 10**6),
    )(*modded, *blocks, tables)
    part = pl.pallas_call(
        chip_term,
        out_shape=jax.ShapeDtypeStruct((PART, D), BF16),
        in_specs=[vmem] * 5,
        out_specs=vmem,
        compiler_params=PARAMS,
        cost_estimate=cost(2 * ALL * D * PART, 2 * 10**6),
    )(*branch, attended)

    plane = lax.all_to_all(part.reshape(8, 36, D), ("yh", "x"), 0, 0, tiled=True)
    plane = jnp.sum(plane.astype(F32), axis=0).astype(BF16)
    plane = jnp.pad(plane, ((0, 12), (0, 0))).reshape(16, 3, D)

    mine, theirs = pl.pallas_call(
        chip_backward,
        out_shape=[jax.ShapeDtypeStruct((2, ZS, TOK, D), F32), jax.ShapeDtypeStruct((2, ZS, TOK, D), BF16)],
        in_specs=[vmem] * 4 + [hbm] * 4 + [vmem] * 9,
        out_specs=[vmem] * 2,
        scratch_shapes=[
            pltpu.VMEM((ALL, WIDE), BF16),
            pltpu.VMEM((ALL, WIDE), F32),
            pltpu.VMEM((ALL, WIDE), F32),
            pltpu.VMEM((ALL, WIDE), F32),
            pltpu.VMEM((ALL, 7 * 128), F32),
            pltpu.VMEM((PART, D), F32),
            pltpu.VMEM((D, D), BF16),
            four,
        ],
        compiler_params=PARAMS,
        cost_estimate=cost(2 * ALL * D * 4 * PART, 14 * 10**6),
    )(*branch, *blocks, w_back, tables_back, *kept)
    arrived = other_core(theirs)
    across = (mine[1] + arrived[1].astype(F32)).astype(BF16)
    summed = (mine[0] + arrived[0].astype(F32) + other_y(across).astype(F32)).astype(BF16)
    back = lax.all_to_all(summed, "zh", 0, 0, tiled=True).reshape(ROWS, D)
    d_hidden = pl.pallas_call(
        home_backward,
        out_shape=jax.ShapeDtypeStruct((ROWS, D), BF16),
        in_specs=[smem, smem, vmem, vmem, vmem, vmem],
        out_specs=vmem,
        scratch_shapes=[pltpu.VMEM((ROWS, D), F32)],
        compiler_params=PARAMS,
        cost_estimate=cost(30 * ROWS * D, 8 * ROWS * D),
    )(power, x_place, rows, cotangent, mod, back)

    levels = lax.all_to_all(plane, ("zh", "zl"), 0, 0, tiled=True)
    level = jnp.sum(levels.astype(F32), axis=0).astype(BF16)
    spread = lax.all_to_all(jnp.broadcast_to(level[None], (8, 3, D)), ("c", "x"), 0, 0, tiled=True)
    wanted = lax.dynamic_index_in_dim(spread.reshape(4, 2, 3, D), core, 1, keepdims=False)
    wanted = jnp.broadcast_to(wanted[:, None], (4, 4, 3, D)).reshape(16, 3, D)
    final = lax.all_to_all(wanted, ("zh", "zl"), 0, 0, tiled=True).reshape(48, D)[:36]
    return d_hidden[None, None], final.astype(F32) / 32.0


def solution(mesh):
    fine = Mesh(mesh.devices.reshape([size for _, size in FINE]), [name for name, _ in FINE])
    placed = (
        P(CLIP, SEQ, None, None),
        P(CLIP, SEQ),
        P(CLIP, None, None, None),
        P(CLIP, SEQ, None, None),
        P(CLIP, None),
        P(CLIP, None),
        P(),
    )
    return jax.shard_map(
        on_device,
        mesh=fine,
        in_specs=placed,
        out_specs=(P(CLIP, SEQ, None, None), P(SEQ, None)),
        check_vma=False,
    )
```

```python
import jax
import jax.numpy as jnp
from jax import lax
from jax.experimental import pallas as pl
from jax.experimental.pallas import tpu as pltpu
from jax.sharding import Mesh
from jax.sharding import PartitionSpec as P

FINE = (("yh", 2), ("yl", 2), ("zh", 4), ("c", 2), ("zl", 4), ("x", 4))
SEQ = ("yh", "yl", "zh", "c")
CLIP = ("zl", "x")
D = 1152
HD = 72
PART = 288
WIDE = 384
HEADS = 4
ZS = 4
TOK = 32
ROWS = ZS * TOK
ALL = 4 * ROWS
BLOCK = 256
F32 = jnp.float32
BF16 = jnp.bfloat16
EPS = 1e-06
TEMPER = HD ** (-0.5)
PARAMS = pltpu.CompilerParams(vmem_limit_bytes=56 * 1024 * 1024)


def cost(flops, nbytes):
    return pl.CostEstimate(flops=flops, bytes_accessed=nbytes, transcendentals=0)


def normalise(hidden, power, inverse):
    scaled = jnp.clip(hidden.astype(F32) * power, -448.0, 448.0)
    rows = scaled * inverse
    centred = rows - jnp.mean(rows, axis=-1, keepdims=True)
    factor = lax.rsqrt(jnp.mean(centred * centred, axis=-1, keepdims=True) + EPS)
    return centred * factor, factor


def home_forward(power_ref, x_ref, hidden_ref, grad_ref, mod_ref, out_ref, branch_ref, turned_ref):
    normed, _ = normalise(hidden_ref[...], power_ref[0], power_ref[1])
    modded = normed * (1.0 + mod_ref[1:2, :]) + mod_ref[0:1, :]
    for x in range(4):

        @pl.when(x_ref[0] == x)
        def _(x=x):
            for place, block in enumerate(block_order(x)):
                turned_ref[:, place * HD : (place + 1) * HD] = modded[:, block * HD : (block + 1) * HD]

    out_ref[...] = turned_ref[...].astype(BF16).reshape(ZS, TOK, D)
    branch_ref[...] = (mod_ref[2:3, :] * grad_ref[...].astype(F32)).astype(BF16).reshape(ZS, TOK, D)


def home_backward(power_ref, x_ref, level_ref, hidden_ref, grad_ref, mod_ref, *refs):
    *back_refs, out_ref, turned_ref, back_ref = refs
    for step, piece_ref in enumerate(back_refs):
        back_ref[lax.rem(level_ref[0] + ZS - step, ZS)] = piece_ref[...].astype(F32)
    normed, factor = normalise(hidden_ref[...], power_ref[0], power_ref[1])
    back = back_ref[...].reshape(ROWS, D)
    for x in range(4):

        @pl.when(x_ref[0] == x)
        def _(x=x):
            for place, block in enumerate(block_order(x)):
                turned_ref[:, block * HD : (block + 1) * HD] = back[:, place * HD : (place + 1) * HD]

    d_normed = turned_ref[...] * (1.0 + mod_ref[1:2, :])
    d_rows = factor * (
        d_normed
        - jnp.mean(d_normed, axis=-1, keepdims=True)
        - normed * jnp.mean(d_normed * normed, axis=-1, keepdims=True)
    )
    out_ref[...] = (grad_ref[...].astype(F32) + d_rows.astype(BF16).astype(F32)).astype(BF16)


def block_order(x):
    return [4 * zl + (x + step) % 4 for step in range(4) for zl in range(4)]


def pick_weights(place_ref, w_qkv_ref, w_out_ref, out_ref, unit_ref):
    qkv = w_qkv_ref[...].astype(F32)
    out = w_out_ref[...].astype(F32)
    for place in range(4):

        @pl.when(place_ref[0] == place)
        def _(place=place):
            yl, core = place // 2, place % 2
            for part in range(3):
                for high in range(2):
                    first = part * D + HD * (4 * (2 * high + yl) + 2 * core)
                    to = part * PART + high * 2 * HD
                    unit_ref[:, to : to + 2 * HD] = qkv[:, first : first + 2 * HD]
            unit_ref[:, 3 * PART :] = out[:, place * PART : (place + 1) * PART]

    unit = unit_ref[...].astype(BF16)
    for copy in range(4):
        out_ref[copy] = unit


def out_rows(x_ref, *refs):
    *block_refs, send_ref, rows_ref, sem = refs
    copies = [
        pltpu.make_async_copy(ref.at[:, pl.ds(768, 384)], rows_ref.at[step], sem.at[step])
        for step, ref in enumerate(block_refs)
    ]
    for copy in copies:
        copy.start()
    for copy in copies:
        copy.wait()
    blocks = [rows_ref[step].astype(F32)[:, 96:384] for step in range(4)]
    for x in range(4):

        @pl.when(x_ref[0] == x)
        def _(x=x):
            for place in range(4):
                yl, core = place // 2, place % 2
                pieces = []
                for high in range(2):
                    for low in range(2):
                        first = (2 * high + yl) * HD
                        pieces.append(blocks[(2 * core + low - x) % 4][first : first + HD])
                send_ref[place] = jnp.concatenate(pieces, axis=0).astype(BF16)


def nt(left, right):
    return lax.dot_general(left, right, (((1,), (1,)), ((), ())), preferred_element_type=F32)


def nn(left, right):
    return lax.dot_general(left, right, (((1,), (0,)), ((), ())), preferred_element_type=F32)


def tn(left, right):
    return lax.dot_general(left, right, (((0,), (0,)), ((), ())), preferred_element_type=F32)


def swap_pairs(values):
    parity = lax.broadcasted_iota(jnp.int32, (values.shape[0], 128), 1) % 2
    tiles = []
    for start in range(0, values.shape[1], 128):
        tile = values[:, start : start + 128]
        tiles.append(jnp.where(parity == 0, pltpu.roll(tile, 127, 1), pltpu.roll(tile, 1, 1)))
    return jnp.concatenate(tiles, axis=1)


def head_members():
    entry = lax.broadcasted_iota(jnp.int32, (WIDE, 128), 0)
    first = lax.broadcasted_iota(jnp.int32, (WIDE, 128), 1) * HD
    return ((entry >= first) & (entry < first + HD) & (entry < PART)).astype(F32).astype(BF16)


def split_dot(dot, values, members):
    high = values.astype(BF16)
    low = (values - high.astype(F32)).astype(BF16)
    return dot(high, members) + dot(low, members)


def window(head):
    start = head * HD // 128 * 128
    end = -(-(head + 1) * HD // 128) * 128
    column = lax.broadcasted_iota(jnp.int32, (BLOCK, end - start), 1) + start
    return start, end, (column >= head * HD) & (column < (head + 1) * HD)


def keep(values, mask):
    return jnp.where(mask, values, jnp.zeros_like(values))


def same_token():
    row = lax.broadcasted_iota(jnp.int32, (BLOCK, BLOCK), 0) % 16
    column = lax.broadcasted_iota(jnp.int32, (BLOCK, BLOCK), 1) % 16
    return row == column


def probabilities(q_hat, k_hat, same):
    scores = nt(q_hat, k_hat) * TEMPER
    exps = jnp.where(same, jnp.exp(scores), 0.0)
    return exps / jnp.sum(exps, axis=-1, keepdims=True)


def gather_rows(refs):
    return jnp.concatenate(
        [ref[:, first : first + 16, :].reshape(ZS * 16, D) for first in (0, 16) for ref in refs], axis=0
    )


def fetch_weights(block_refs, w_ref, sem):
    copies = [
        pltpu.make_async_copy(ref, w_ref.at[pl.ds(PART * step, PART), :], sem.at[step])
        for step, ref in enumerate(block_refs)
    ]
    for copy in copies:
        copy.start()
    return copies


def by_token(table):
    return jnp.broadcast_to(table[:, None, :], (16, 16, WIDE)).reshape(BLOCK, WIDE)


def widen(values):
    return jnp.concatenate([values, jnp.zeros((values.shape[0], WIDE - PART), values.dtype)], axis=1)


def chip_forward(*refs):
    row_refs, block_refs, (tab_ref, q_ref, k_ref, v_ref, qh_ref, kh_ref, qf_ref, kf_ref, att_ref, w_ref, sem) = (
        refs[:4], refs[4:8], refs[8:]
    )
    copies = fetch_weights(block_refs, w_ref, sem)
    modded = gather_rows(row_refs)
    members = head_members()
    for copy in copies:
        copy.wait()
    packed = nn(modded, w_ref[:, : 7 * 128])
    for place, (raw_ref, hat_ref, factor_ref) in enumerate(((q_ref, qh_ref, qf_ref), (k_ref, kh_ref, kf_ref))):
        raw = widen(packed[:, place * PART : (place + 1) * PART])
        raw_ref[...] = raw.astype(BF16)
        raw = raw_ref[...].astype(F32)
        factor = lax.rsqrt(split_dot(nn, raw * raw, members) / HD + EPS)
        factor_ref[...] = factor
        wide = split_dot(nt, factor, members)
        swapped = swap_pairs(raw)
        straight, ahead = by_token(tab_ref[2 * place]), by_token(tab_ref[2 * place + 1])
        for half in range(2):
            rows = slice(half * BLOCK, (half + 1) * BLOCK)
            turned = raw[rows] * straight + swapped[rows] * ahead
            hat_ref[rows, :] = (wide[rows] * turned).astype(BF16)
    v_ref[...] = widen(packed[:, 2 * PART : 3 * PART]).astype(BF16)
    same = same_token()
    att_ref[...] = jnp.zeros_like(att_ref)
    for head in range(HEADS):
        start, end, mask = window(head)
        for half in range(2):
            rows = slice(half * BLOCK, (half + 1) * BLOCK)
            probs = probabilities(keep(qh_ref[rows, start:end], mask), kh_ref[rows, start:end], same).astype(BF16)
            found = nn(probs, v_ref[rows, start:end]).astype(BF16)
            att_ref[rows, start:end] = jnp.where(mask, found, att_ref[rows, start:end])


def chip_term(*refs):
    row_refs, (att_ref, part_ref) = refs[:4], refs[4:]
    total = tn(att_ref[...], gather_rows(row_refs))
    for piece in range(8):
        part_ref[piece] = total[36 * piece : 36 * (piece + 1)].astype(BF16)


def chip_backward(*refs):
    row_refs, block_refs = refs[:4], refs[4:8]
    (
        wo_ref, tab_ref, q_ref, k_ref, v_ref, qh_ref, kh_ref, qf_ref, kf_ref,
        mine_ref, theirs_ref, do_ref, dv_ref, dqh_ref, dkh_ref, dqkv_ref, wide_ref, w_ref, sem,
    ) = refs[8:]
    copies = fetch_weights(block_refs, w_ref, sem)
    for place in range(4):
        wide_ref[:, place * PART : (place + 1) * PART] = wo_ref[place].astype(F32)
    do_ref[...] = widen(nt(gather_rows(row_refs), wide_ref[...].astype(BF16))).astype(BF16)
    same = same_token()
    members = head_members()
    for ref in (dv_ref, dqh_ref, dkh_ref):
        ref[...] = jnp.zeros_like(ref)
    for head in range(HEADS):
        start, end, mask = window(head)
        for half in range(2):
            rows = slice(half * BLOCK, (half + 1) * BLOCK)
            q_hat, k_hat = qh_ref[rows, start:end], kh_ref[rows, start:end]
            probs = probabilities(keep(q_hat, mask), k_hat, same)
            d_out = do_ref[rows, start:end]
            d_probs = nt(keep(d_out, mask), v_ref[rows, start:end])
            d_value = tn(probs.astype(BF16), d_out)
            spread = probs * d_probs
            d_scores = ((spread - probs * jnp.sum(spread, axis=-1, keepdims=True)) * TEMPER).astype(BF16)
            d_q = nn(d_scores, k_hat)
            d_k = tn(d_scores, q_hat)
            dv_ref[rows, start:end] = jnp.where(mask, d_value, dv_ref[rows, start:end])
            dqh_ref[rows, start:end] = jnp.where(mask, d_q, dqh_ref[rows, start:end])
            dkh_ref[rows, start:end] = jnp.where(mask, d_k, dkh_ref[rows, start:end])
    dqkv_ref[:, 3 * PART :] = jnp.zeros((ALL, 7 * 128 - 3 * PART), F32)
    dqkv_ref[:, 2 * PART : 3 * PART] = dv_ref[:, :PART]
    for place, (raw_ref, factor_ref, turned_ref) in enumerate(
        ((q_ref, qf_ref, dqh_ref), (k_ref, kf_ref, dkh_ref))
    ):
        raw = raw_ref[...].astype(F32)
        factor = factor_ref[...]
        turned = turned_ref[...]
        swapped = swap_pairs(turned)
        straight, back = by_token(tab_ref[2 * place]), by_token(tab_ref[2 * place + 1])
        scaled = jnp.concatenate(
            [
                turned[first : first + BLOCK] * straight + swapped[first : first + BLOCK] * back
                for first in (0, BLOCK)
            ],
            axis=0,
        )
        inner = split_dot(nn, raw * scaled, members) / HD
        wide = split_dot(nt, factor, members)
        pulled = split_dot(nt, factor * factor * factor * inner, members)
        dqkv_ref[:, place * PART : (place + 1) * PART] = (wide * scaled - raw * pulled)[:, :PART]
    for copy in copies:
        copy.wait()
    total = nt(dqkv_ref[...].astype(BF16), w_ref[:, : 7 * 128])
    for half in range(2):
        for device in range(4):
            first = half * BLOCK + device * ZS * 16
            rows = total[first : first + ZS * 16].reshape(ZS, 16, D)
            out_ref = theirs_ref if device % 2 else mine_ref
            out_ref[device // 2, :, half * 16 : half * 16 + 16, :] = rows.astype(out_ref.dtype)


def turn_tables(qk_gain, yl, core):
    level = 2 * jnp.arange(ZS, dtype=jnp.int32)
    position = jnp.concatenate(
        [8 * y + level + c for y in (yl, 1 - yl) for c in (core, 1 - core)]
    ).astype(F32)
    column = jnp.arange(HD, dtype=jnp.int32)
    frequency = jnp.power(10000.0, -((2 * (column // 2)).astype(F32) / HD))
    angles = position[:, None] * frequency[None, :]
    cosine, sine = jnp.cos(angles), jnp.sin(angles)
    even = column % 2 == 0
    swapped = qk_gain.reshape(2, HD // 2, 2)[:, :, ::-1].reshape(2, HD)

    def spread(table):
        return jnp.pad(jnp.tile(table, (1, 1, HEADS)), ((0, 0), (0, 0), (0, WIDE - PART)))

    straight = [qk_gain[i] * cosine for i in range(2)]
    ahead = [jnp.where(even, -sine, sine) * swapped[i] for i in range(2)]
    back = [jnp.where(even, sine, -sine) * qk_gain[i] for i in range(2)]
    return (
        spread(jnp.stack([straight[0], ahead[0], straight[1], ahead[1]])),
        spread(jnp.stack([straight[0], back[0], straight[1], back[1]])),
    )


def on_device(hidden, exponent, modulation, out_grad, w_qkv, w_out, qk_gain):
    core, yl, x = lax.axis_index("c"), lax.axis_index("yl"), lax.axis_index("x")
    rows, cotangent = hidden[0, 0], out_grad[0, 0]
    shift_by = exponent[0, 0]
    power = jnp.stack(
        [
            lax.shift_left(jnp.int32(1), shift_by).astype(F32),
            lax.shift_left(jnp.int32(1), 24 - shift_by).astype(F32) * 2.0**-24,
        ]
    )
    mod = lax.dynamic_index_in_dim(modulation[0], lax.axis_index("yh"), 0, keepdims=False)
    x_place = x[None]
    smem = pl.BlockSpec(memory_space=pltpu.SMEM)
    vmem = pl.BlockSpec(memory_space=pltpu.VMEM)
    hbm = pl.BlockSpec(memory_space=pl.ANY)
    four = pltpu.SemaphoreType.DMA((4,))

    unit = pl.pallas_call(
        pick_weights,
        out_shape=jax.ShapeDtypeStruct((4, HD, 4 * PART), BF16),
        in_specs=[smem, vmem, vmem],
        out_specs=vmem,
        scratch_shapes=[pltpu.VMEM((HD, 4 * PART), F32)],
        compiler_params=PARAMS,
        cost_estimate=cost(10**6, 2 * 10**6),
    )((2 * yl + core)[None], w_qkv, w_out)
    block = lax.all_to_all(unit, "zl", 0, 0, tiled=True).reshape(PART, 4 * PART)
    blocks = [block] + [
        lax.ppermute(block, "x", [(i, (i + 4 - step) % 4) for i in range(4)]) for step in (1, 2, 3)
    ]

    sent, sent_branch = pl.pallas_call(
        home_forward,
        out_shape=[jax.ShapeDtypeStruct((ZS, TOK, D), BF16)] * 2,
        in_specs=[smem, smem, vmem, vmem, vmem],
        out_specs=[vmem, vmem],
        scratch_shapes=[pltpu.VMEM((ROWS, D), F32)],
        compiler_params=PARAMS,
        cost_estimate=cost(20 * ROWS * D, 8 * ROWS * D),
    )(power, x_place, rows, cotangent, mod)

    def other_core(values):
        return lax.ppermute(values, "c", [(0, 1), (1, 0)])

    def other_y(values):
        return lax.ppermute(values, "yl", [(0, 1), (1, 0)])

    def exchange(values):
        return lax.all_to_all(values, "zh", 0, 0, tiled=True)

    def from_frames(own):
        across = other_y(own)
        return [own, other_core(own), across, other_core(across)]

    sent, _ = lax.optimization_barrier((sent, block))
    both = exchange(jnp.concatenate([sent, sent_branch], axis=1))
    modded = from_frames(both[:, :TOK])
    branch = from_frames(both[:, TOK:])
    w_back = pl.pallas_call(
        out_rows,
        out_shape=jax.ShapeDtypeStruct((4, PART, PART), BF16),
        in_specs=[smem] + [hbm] * 4,
        out_specs=vmem,
        scratch_shapes=[pltpu.VMEM((4, PART, 384), BF16), four],
        compiler_params=PARAMS,
        cost_estimate=cost(10**6, 2 * 10**6),
    )(x_place, *blocks)
    w_back = lax.all_to_all(w_back, ("yl", "c"), 0, 0, tiled=True)

    tables, tables_back = turn_tables(qk_gain, yl, core)
    wide = jax.ShapeDtypeStruct((ALL, WIDE), BF16)
    factors = jax.ShapeDtypeStruct((ALL, 128), F32)
    *kept, attended = pl.pallas_call(
        chip_forward,
        out_shape=[wide] * 5 + [factors] * 2 + [wide],
        in_specs=[vmem] * 4 + [hbm] * 4 + [vmem],
        out_specs=[vmem] * 8,
        scratch_shapes=[pltpu.VMEM((D, D), BF16), four],
        compiler_params=PARAMS,
        cost_estimate=cost(2 * ALL * D * 4 * PART, 12 * 10**6),
    )(*modded, *blocks, tables)
    part = pl.pallas_call(
        chip_term,
        out_shape=jax.ShapeDtypeStruct((8, 36, D), BF16),
        in_specs=[vmem] * 5,
        out_specs=vmem,
        compiler_params=PARAMS,
        cost_estimate=cost(2 * ALL * D * PART, 2 * 10**6),
    )(*branch, attended)

    w_back, part = lax.optimization_barrier((w_back, part))

    plane = lax.all_to_all(part, ("yh", "x"), 0, 0, tiled=True)
    plane = jnp.sum(plane.astype(F32), axis=0).astype(BF16)
    plane = jnp.pad(plane, ((0, 12), (0, 0))).reshape(16, 3, D)

    mine, theirs = pl.pallas_call(
        chip_backward,
        out_shape=[jax.ShapeDtypeStruct((2, ZS, TOK, D), F32), jax.ShapeDtypeStruct((2, ZS, TOK, D), BF16)],
        in_specs=[vmem] * 4 + [hbm] * 4 + [vmem] * 9,
        out_specs=[vmem] * 2,
        scratch_shapes=[
            pltpu.VMEM((ALL, WIDE), BF16),
            pltpu.VMEM((ALL, WIDE), F32),
            pltpu.VMEM((ALL, WIDE), F32),
            pltpu.VMEM((ALL, WIDE), F32),
            pltpu.VMEM((ALL, 7 * 128), F32),
            pltpu.VMEM((PART, D), F32),
            pltpu.VMEM((D, D), BF16),
            four,
        ],
        compiler_params=PARAMS,
        cost_estimate=cost(2 * ALL * D * 4 * PART, 14 * 10**6),
    )(*branch, *blocks, w_back, tables_back, *kept)
    theirs, _ = lax.optimization_barrier((theirs, plane))
    arrived = other_core(theirs)
    across = (mine[1] + arrived[1].astype(F32)).astype(BF16)
    summed = (mine[0] + arrived[0].astype(F32) + other_y(across).astype(F32)).astype(BF16)
    level = lax.axis_index("zh")
    pieces = [lax.dynamic_index_in_dim(summed, level, 0, keepdims=False)]
    for step in range(1, ZS):
        piece = lax.dynamic_index_in_dim(summed, lax.rem(level + step, ZS), 0, keepdims=False)
        pieces.append(lax.ppermute(piece, "zh", [(i, (i + step) % ZS) for i in range(ZS)]))
    level = level[None]
    d_hidden = pl.pallas_call(
        home_backward,
        out_shape=jax.ShapeDtypeStruct((ROWS, D), BF16),
        in_specs=[smem, smem, smem] + [vmem] * 7,
        out_specs=vmem,
        scratch_shapes=[pltpu.VMEM((ROWS, D), F32), pltpu.VMEM((ZS, TOK, D), F32)],
        compiler_params=PARAMS,
        cost_estimate=cost(30 * ROWS * D, 8 * ROWS * D),
    )(power, x_place, level, rows, cotangent, mod, *pieces)

    levels = lax.all_to_all(plane, ("zh", "zl"), 0, 0, tiled=True)
    level = jnp.sum(levels.astype(F32), axis=0).astype(BF16)
    spread = lax.all_to_all(jnp.broadcast_to(level[None], (8, 3, D)), ("c", "x"), 0, 0, tiled=True)
    wanted = lax.dynamic_index_in_dim(spread.reshape(4, 2, 3, D), core, 1, keepdims=False)
    wanted = jnp.broadcast_to(wanted[:, None], (4, 4, 3, D)).reshape(16, 3, D)
    final = lax.all_to_all(wanted, ("zh", "zl"), 0, 0, tiled=True).reshape(48, D)[:36]
    return d_hidden[None, None], final.astype(F32) / 32.0


def solution(mesh):
    fine = Mesh(mesh.devices.reshape([size for _, size in FINE]), [name for name, _ in FINE])
    placed = (
        P(CLIP, SEQ, None, None),
        P(CLIP, SEQ),
        P(CLIP, None, None, None),
        P(CLIP, SEQ, None, None),
        P(CLIP, None),
        P(CLIP, None),
        P(),
    )
    return jax.shard_map(
        on_device,
        mesh=fine,
        in_specs=placed,
        out_specs=(P(CLIP, SEQ, None, None), P(SEQ, None)),
        check_vma=False,
    )
```

```python
import jax
import jax.numpy as jnp
from jax import lax
from jax.experimental import pallas as pl
from jax.experimental.pallas import tpu as pltpu
from jax.sharding import Mesh
from jax.sharding import PartitionSpec as P

FINE = (("yh", 2), ("yl", 2), ("zh", 4), ("c", 2), ("zl", 4), ("x", 4))
SEQ = ("yh", "yl", "zh", "c")
CLIP = ("zl", "x")
D = 1152
HD = 72
PART = 288
WIDE = 384
HEADS = 4
ZS = 4
TOK = 32
ROWS = ZS * TOK
ALL = 4 * ROWS
BLOCK = 256
F32 = jnp.float32
BF16 = jnp.bfloat16
EPS = 1e-06
TEMPER = HD ** (-0.5)
PARAMS = pltpu.CompilerParams(vmem_limit_bytes=56 * 1024 * 1024)


def cost(flops, nbytes):
    return pl.CostEstimate(flops=flops, bytes_accessed=nbytes, transcendentals=0)


def normalise(hidden, power, inverse):
    scaled = jnp.clip(hidden.astype(F32) * power, -448.0, 448.0)
    rows = scaled * inverse
    centred = rows - jnp.mean(rows, axis=-1, keepdims=True)
    factor = lax.rsqrt(jnp.mean(centred * centred, axis=-1, keepdims=True) + EPS)
    return centred * factor, factor


def home_forward(power_ref, x_ref, hidden_ref, grad_ref, mod_ref, out_ref, turned_ref):
    normed, _ = normalise(hidden_ref[...], power_ref[0], power_ref[1])
    modded = normed * (1.0 + mod_ref[1:2, :]) + mod_ref[0:1, :]
    for x in range(4):

        @pl.when(x_ref[0] == x)
        def _(x=x):
            for place, block in enumerate(block_order(x)):
                turned_ref[:, place * HD : (place + 1) * HD] = modded[:, block * HD : (block + 1) * HD]

    out_ref[:, :TOK, :] = turned_ref[...].astype(BF16).reshape(ZS, TOK, D)
    out_ref[:, TOK:, :] = (mod_ref[2:3, :] * grad_ref[...].astype(F32)).astype(BF16).reshape(ZS, TOK, D)


def home_backward(power_ref, x_ref, hidden_ref, grad_ref, mod_ref, back_ref, out_ref, turned_ref):
    normed, factor = normalise(hidden_ref[...], power_ref[0], power_ref[1])
    back = back_ref[:, :TOK, :].reshape(ROWS, D).astype(F32)
    for x in range(4):

        @pl.when(x_ref[0] == x)
        def _(x=x):
            for place, block in enumerate(block_order(x)):
                turned_ref[:, block * HD : (block + 1) * HD] = back[:, place * HD : (place + 1) * HD]

    d_normed = turned_ref[...] * (1.0 + mod_ref[1:2, :])
    d_rows = factor * (
        d_normed
        - jnp.mean(d_normed, axis=-1, keepdims=True)
        - normed * jnp.mean(d_normed * normed, axis=-1, keepdims=True)
    )
    out_ref[...] = (grad_ref[...].astype(F32) + d_rows.astype(BF16).astype(F32)).astype(BF16)


def block_order(x):
    return [4 * zl + (x + step) % 4 for step in range(4) for zl in range(4)]


def pick_weights(place_ref, w_qkv_ref, w_out_ref, out_ref, unit_ref):
    qkv = w_qkv_ref[...].astype(F32)
    out = w_out_ref[...].astype(F32)
    for place in range(4):

        @pl.when(place_ref[0] == place)
        def _(place=place):
            yl, core = place // 2, place % 2
            for part in range(3):
                for high in range(2):
                    first = part * D + HD * (4 * (2 * high + yl) + 2 * core)
                    to = part * PART + high * 2 * HD
                    unit_ref[:, to : to + 2 * HD] = qkv[:, first : first + 2 * HD]
            unit_ref[:, 3 * PART :] = out[:, place * PART : (place + 1) * PART]

    unit = unit_ref[...].astype(BF16)
    for copy in range(4):
        out_ref[copy] = unit


def out_rows(x_ref, *refs):
    *block_refs, send_ref, rows_ref, sem = refs
    copies = [
        pltpu.make_async_copy(ref.at[:, pl.ds(768, 384)], rows_ref.at[step], sem.at[step])
        for step, ref in enumerate(block_refs)
    ]
    for copy in copies:
        copy.start()
    for copy in copies:
        copy.wait()
    blocks = [rows_ref[step].astype(F32)[:, 96:384] for step in range(4)]
    for x in range(4):

        @pl.when(x_ref[0] == x)
        def _(x=x):
            for place in range(4):
                yl, core = place // 2, place % 2
                pieces = []
                for high in range(2):
                    for low in range(2):
                        first = (2 * high + yl) * HD
                        pieces.append(blocks[(2 * core + low - x) % 4][first : first + HD])
                send_ref[place] = jnp.concatenate(pieces, axis=0).astype(BF16)


def nt(left, right):
    return lax.dot_general(left, right, (((1,), (1,)), ((), ())), preferred_element_type=F32)


def nn(left, right):
    return lax.dot_general(left, right, (((1,), (0,)), ((), ())), preferred_element_type=F32)


def tn(left, right):
    return lax.dot_general(left, right, (((0,), (0,)), ((), ())), preferred_element_type=F32)


def swap_pairs(values):
    parity = lax.broadcasted_iota(jnp.int32, (values.shape[0], 128), 1) % 2
    tiles = []
    for start in range(0, values.shape[1], 128):
        tile = values[:, start : start + 128]
        tiles.append(jnp.where(parity == 0, pltpu.roll(tile, 127, 1), pltpu.roll(tile, 1, 1)))
    return jnp.concatenate(tiles, axis=1)


def head_members():
    entry = lax.broadcasted_iota(jnp.int32, (WIDE, 128), 0)
    first = lax.broadcasted_iota(jnp.int32, (WIDE, 128), 1) * HD
    return ((entry >= first) & (entry < first + HD) & (entry < PART)).astype(F32).astype(BF16)


def split_dot(dot, values, members):
    high = values.astype(BF16)
    low = (values - high.astype(F32)).astype(BF16)
    return dot(high, members) + dot(low, members)


def window(head):
    start = head * HD // 128 * 128
    end = -(-(head + 1) * HD // 128) * 128
    column = lax.broadcasted_iota(jnp.int32, (BLOCK, end - start), 1) + start
    return start, end, (column >= head * HD) & (column < (head + 1) * HD)


def keep(values, mask):
    return jnp.where(mask, values, jnp.zeros_like(values))


def same_token():
    row = lax.broadcasted_iota(jnp.int32, (BLOCK, BLOCK), 0) % 16
    column = lax.broadcasted_iota(jnp.int32, (BLOCK, BLOCK), 1) % 16
    return row == column


def probabilities(q_hat, k_hat, same):
    scores = nt(q_hat, k_hat) * TEMPER
    exps = jnp.where(same, jnp.exp(scores), 0.0)
    return exps / jnp.sum(exps, axis=-1, keepdims=True)


def gather_rows(refs, start):
    return jnp.concatenate(
        [ref[:, first : first + 16, :].reshape(ZS * 16, D) for first in (start, start + 16) for ref in refs], axis=0
    )


def fetch_weights(block_refs, w_ref, sem):
    copies = [
        pltpu.make_async_copy(ref, w_ref.at[pl.ds(PART * step, PART), :], sem.at[step])
        for step, ref in enumerate(block_refs)
    ]
    for copy in copies:
        copy.start()
    return copies


def by_token(table):
    return jnp.broadcast_to(table[:, None, :], (16, 16, WIDE)).reshape(BLOCK, WIDE)


def widen(values):
    return jnp.concatenate([values, jnp.zeros((values.shape[0], WIDE - PART), values.dtype)], axis=1)


def chip_forward(*refs):
    row_refs, block_refs, (tab_ref, q_ref, k_ref, v_ref, qh_ref, kh_ref, qf_ref, kf_ref, att_ref, w_ref, sem) = (
        refs[:4], refs[4:8], refs[8:]
    )
    copies = fetch_weights(block_refs, w_ref, sem)
    modded = gather_rows(row_refs, 0)
    members = head_members()
    for copy in copies:
        copy.wait()
    packed = nn(modded, w_ref[:, : 7 * 128])
    for place, (raw_ref, hat_ref, factor_ref) in enumerate(((q_ref, qh_ref, qf_ref), (k_ref, kh_ref, kf_ref))):
        raw = widen(packed[:, place * PART : (place + 1) * PART])
        raw_ref[...] = raw.astype(BF16)
        raw = raw_ref[...].astype(F32)
        factor = lax.rsqrt(split_dot(nn, raw * raw, members) / HD + EPS)
        factor_ref[...] = factor
        wide = split_dot(nt, factor, members)
        swapped = swap_pairs(raw)
        straight, ahead = by_token(tab_ref[2 * place]), by_token(tab_ref[2 * place + 1])
        for half in range(2):
            rows = slice(half * BLOCK, (half + 1) * BLOCK)
            turned = raw[rows] * straight + swapped[rows] * ahead
            hat_ref[rows, :] = (wide[rows] * turned).astype(BF16)
    v_ref[...] = widen(packed[:, 2 * PART : 3 * PART]).astype(BF16)
    same = same_token()
    att_ref[...] = jnp.zeros_like(att_ref)
    for head in range(HEADS):
        start, end, mask = window(head)
        for half in range(2):
            rows = slice(half * BLOCK, (half + 1) * BLOCK)
            probs = probabilities(keep(qh_ref[rows, start:end], mask), kh_ref[rows, start:end], same).astype(BF16)
            found = nn(probs, v_ref[rows, start:end]).astype(BF16)
            att_ref[rows, start:end] = jnp.where(mask, found, att_ref[rows, start:end])


def chip_term(*refs):
    row_refs, (att_ref, part_ref) = refs[:4], refs[4:]
    total = tn(att_ref[...], gather_rows(row_refs, TOK))
    for piece in range(8):
        part_ref[piece] = total[36 * piece : 36 * (piece + 1)].astype(BF16)


def chip_backward(*refs):
    row_refs, block_refs = refs[:4], refs[4:8]
    (
        wo_ref, tab_ref, q_ref, k_ref, v_ref, qh_ref, kh_ref, qf_ref, kf_ref,
        mine_ref, theirs_ref, do_ref, dv_ref, dqh_ref, dkh_ref, dqkv_ref, wide_ref, w_ref, sem,
    ) = refs[8:]
    copies = fetch_weights(block_refs, w_ref, sem)
    for place in range(4):
        wide_ref[:, place * PART : (place + 1) * PART] = wo_ref[place].astype(F32)
    do_ref[...] = widen(nt(gather_rows(row_refs, TOK), wide_ref[...].astype(BF16))).astype(BF16)
    same = same_token()
    members = head_members()
    for ref in (dv_ref, dqh_ref, dkh_ref):
        ref[...] = jnp.zeros_like(ref)
    for head in range(HEADS):
        start, end, mask = window(head)
        for half in range(2):
            rows = slice(half * BLOCK, (half + 1) * BLOCK)
            q_hat, k_hat = qh_ref[rows, start:end], kh_ref[rows, start:end]
            probs = probabilities(keep(q_hat, mask), k_hat, same)
            d_out = do_ref[rows, start:end]
            d_probs = nt(keep(d_out, mask), v_ref[rows, start:end])
            d_value = tn(probs.astype(BF16), d_out)
            spread = probs * d_probs
            d_scores = ((spread - probs * jnp.sum(spread, axis=-1, keepdims=True)) * TEMPER).astype(BF16)
            d_q = nn(d_scores, k_hat)
            d_k = tn(d_scores, q_hat)
            dv_ref[rows, start:end] = jnp.where(mask, d_value, dv_ref[rows, start:end])
            dqh_ref[rows, start:end] = jnp.where(mask, d_q, dqh_ref[rows, start:end])
            dkh_ref[rows, start:end] = jnp.where(mask, d_k, dkh_ref[rows, start:end])
    dqkv_ref[:, 3 * PART :] = jnp.zeros((ALL, 7 * 128 - 3 * PART), F32)
    dqkv_ref[:, 2 * PART : 3 * PART] = dv_ref[:, :PART]
    for place, (raw_ref, factor_ref, turned_ref) in enumerate(
        ((q_ref, qf_ref, dqh_ref), (k_ref, kf_ref, dkh_ref))
    ):
        raw = raw_ref[...].astype(F32)
        factor = factor_ref[...]
        turned = turned_ref[...]
        swapped = swap_pairs(turned)
        straight, back = by_token(tab_ref[2 * place]), by_token(tab_ref[2 * place + 1])
        scaled = jnp.concatenate(
            [
                turned[first : first + BLOCK] * straight + swapped[first : first + BLOCK] * back
                for first in (0, BLOCK)
            ],
            axis=0,
        )
        inner = split_dot(nn, raw * scaled, members) / HD
        wide = split_dot(nt, factor, members)
        pulled = split_dot(nt, factor * factor * factor * inner, members)
        dqkv_ref[:, place * PART : (place + 1) * PART] = (wide * scaled - raw * pulled)[:, :PART]
    for copy in copies:
        copy.wait()
    total = nt(dqkv_ref[...].astype(BF16), w_ref[:, : 7 * 128])
    for half in range(2):
        for device in range(4):
            first = half * BLOCK + device * ZS * 16
            rows = total[first : first + ZS * 16].reshape(ZS, 16, D)
            out_ref = theirs_ref if device % 2 else mine_ref
            out_ref[device // 2, :, half * 16 : half * 16 + 16, :] = rows.astype(out_ref.dtype)


def turn_tables(qk_gain, yl, core):
    level = 2 * jnp.arange(ZS, dtype=jnp.int32)
    position = jnp.concatenate(
        [8 * y + level + c for y in (yl, 1 - yl) for c in (core, 1 - core)]
    ).astype(F32)
    column = jnp.arange(HD, dtype=jnp.int32)
    frequency = jnp.power(10000.0, -((2 * (column // 2)).astype(F32) / HD))
    angles = position[:, None] * frequency[None, :]
    cosine, sine = jnp.cos(angles), jnp.sin(angles)
    even = column % 2 == 0
    swapped = qk_gain.reshape(2, HD // 2, 2)[:, :, ::-1].reshape(2, HD)

    def spread(table):
        return jnp.pad(jnp.tile(table, (1, 1, HEADS)), ((0, 0), (0, 0), (0, WIDE - PART)))

    straight = [qk_gain[i] * cosine for i in range(2)]
    ahead = [jnp.where(even, -sine, sine) * swapped[i] for i in range(2)]
    back = [jnp.where(even, sine, -sine) * qk_gain[i] for i in range(2)]
    return (
        spread(jnp.stack([straight[0], ahead[0], straight[1], ahead[1]])),
        spread(jnp.stack([straight[0], back[0], straight[1], back[1]])),
    )


def on_device(hidden, exponent, modulation, out_grad, w_qkv, w_out, qk_gain):
    core, yl, x = lax.axis_index("c"), lax.axis_index("yl"), lax.axis_index("x")
    rows, cotangent = hidden[0, 0], out_grad[0, 0]
    shift_by = exponent[0, 0]
    power = jnp.stack(
        [
            lax.shift_left(jnp.int32(1), shift_by).astype(F32),
            lax.shift_left(jnp.int32(1), 24 - shift_by).astype(F32) * 2.0**-24,
        ]
    )
    mod = lax.dynamic_index_in_dim(modulation[0], lax.axis_index("yh"), 0, keepdims=False)
    x_place = x[None]
    smem = pl.BlockSpec(memory_space=pltpu.SMEM)
    vmem = pl.BlockSpec(memory_space=pltpu.VMEM)
    hbm = pl.BlockSpec(memory_space=pl.ANY)
    four = pltpu.SemaphoreType.DMA((4,))

    unit = pl.pallas_call(
        pick_weights,
        out_shape=jax.ShapeDtypeStruct((4, HD, 4 * PART), BF16),
        in_specs=[smem, vmem, vmem],
        out_specs=vmem,
        scratch_shapes=[pltpu.VMEM((HD, 4 * PART), F32)],
        compiler_params=PARAMS,
        cost_estimate=cost(10**6, 2 * 10**6),
    )((2 * yl + core)[None], w_qkv, w_out)
    block = lax.all_to_all(unit, "zl", 0, 0, tiled=True).reshape(PART, 4 * PART)
    blocks = [block] + [
        lax.ppermute(block, "x", [(i, (i + 4 - step) % 4) for i in range(4)]) for step in (1, 2, 3)
    ]

    sent = pl.pallas_call(
        home_forward,
        out_shape=jax.ShapeDtypeStruct((ZS, 2 * TOK, D), BF16),
        in_specs=[smem, smem, vmem, vmem, vmem],
        out_specs=vmem,
        scratch_shapes=[pltpu.VMEM((ROWS, D), F32)],
        compiler_params=PARAMS,
        cost_estimate=cost(20 * ROWS * D, 8 * ROWS * D),
    )(power, x_place, rows, cotangent, mod)

    def other_core(values):
        return lax.ppermute(values, "c", [(0, 1), (1, 0)])

    def other_y(values):
        return lax.ppermute(values, "yl", [(0, 1), (1, 0)])

    def exchange(values):
        return lax.all_to_all(values, "zh", 0, 0, tiled=True)

    tables, tables_back = turn_tables(qk_gain, yl, core)
    sent, _, tables, tables_back = lax.optimization_barrier((sent, block, tables, tables_back))
    own = exchange(sent)
    across = other_y(own)
    near = other_core(own)
    w_back = pl.pallas_call(
        out_rows,
        out_shape=jax.ShapeDtypeStruct((4, PART, PART), BF16),
        in_specs=[smem] + [hbm] * 4,
        out_specs=vmem,
        scratch_shapes=[pltpu.VMEM((4, PART, 384), BF16), four],
        compiler_params=PARAMS,
        cost_estimate=cost(10**6, 2 * 10**6),
    )(x_place, *blocks)
    across, w_back = lax.optimization_barrier((across, w_back))
    arrays = [own, near, across, other_core(across)]
    w_back = lax.all_to_all(w_back, ("yl", "c"), 0, 0, tiled=True)

    wide = jax.ShapeDtypeStruct((ALL, WIDE), BF16)
    factors = jax.ShapeDtypeStruct((ALL, 128), F32)
    *kept, attended = pl.pallas_call(
        chip_forward,
        out_shape=[wide] * 5 + [factors] * 2 + [wide],
        in_specs=[vmem] * 4 + [hbm] * 4 + [vmem],
        out_specs=[vmem] * 8,
        scratch_shapes=[pltpu.VMEM((D, D), BF16), four],
        compiler_params=PARAMS,
        cost_estimate=cost(2 * ALL * D * 4 * PART, 12 * 10**6),
    )(*arrays, *blocks, tables)
    part = pl.pallas_call(
        chip_term,
        out_shape=jax.ShapeDtypeStruct((8, 36, D), BF16),
        in_specs=[vmem] * 5,
        out_specs=vmem,
        compiler_params=PARAMS,
        cost_estimate=cost(2 * ALL * D * PART, 2 * 10**6),
    )(*arrays, attended)

    w_back, part = lax.optimization_barrier((w_back, part))

    plane = lax.all_to_all(part, ("yh", "x"), 0, 0, tiled=True)

    mine, theirs = pl.pallas_call(
        chip_backward,
        out_shape=[jax.ShapeDtypeStruct((2, ZS, TOK, D), F32), jax.ShapeDtypeStruct((2, ZS, TOK, D), BF16)],
        in_specs=[vmem] * 4 + [hbm] * 4 + [vmem] * 9,
        out_specs=[vmem] * 2,
        scratch_shapes=[
            pltpu.VMEM((ALL, WIDE), BF16),
            pltpu.VMEM((ALL, WIDE), F32),
            pltpu.VMEM((ALL, WIDE), F32),
            pltpu.VMEM((ALL, WIDE), F32),
            pltpu.VMEM((ALL, 7 * 128), F32),
            pltpu.VMEM((PART, D), F32),
            pltpu.VMEM((D, D), BF16),
            four,
        ],
        compiler_params=PARAMS,
        cost_estimate=cost(2 * ALL * D * 4 * PART, 14 * 10**6),
    )(*arrays, *blocks, w_back, tables_back, *kept)
    theirs, plane = lax.optimization_barrier((theirs, plane))
    plane = jnp.sum(plane.astype(F32), axis=0).astype(BF16)
    plane = plane.reshape(4, 9, D)
    arrived = other_core(theirs)
    across = (mine[1] + arrived[1].astype(F32)).astype(BF16)
    from_y = other_y(across)
    summed = (mine[0] + arrived[0].astype(F32) + from_y.astype(F32)).astype(BF16)

    levels = lax.all_to_all(plane, "zl", 0, 0, tiled=True)
    level = jnp.sum(levels.astype(F32), axis=0).astype(BF16)
    level, summed = lax.optimization_barrier((level, summed))
    spread = lax.all_to_all(jnp.broadcast_to(level[None], (8, 9, D)), ("c", "x"), 0, 0, tiled=True)
    wanted = lax.dynamic_index_in_dim(spread.reshape(4, 2, 9, D), core, 1, keepdims=False)
    joined = jnp.concatenate([summed, jnp.pad(wanted, ((0, 0), (0, 7), (0, 0)))], axis=1)
    joined = exchange(joined)
    d_hidden = pl.pallas_call(
        home_backward,
        out_shape=jax.ShapeDtypeStruct((ROWS, D), BF16),
        in_specs=[smem, smem, vmem, vmem, vmem, vmem],
        out_specs=vmem,
        scratch_shapes=[pltpu.VMEM((ROWS, D), F32)],
        compiler_params=PARAMS,
        cost_estimate=cost(30 * ROWS * D, 8 * ROWS * D),
    )(power, x_place, rows, cotangent, mod, joined)
    share = jnp.sum(joined[:, TOK : TOK + 9].astype(F32), axis=0).astype(BF16)
    final = lax.all_to_all(jnp.broadcast_to(share[None], (4, 9, D)), "zl", 0, 0, tiled=True).reshape(36, D)
    return d_hidden[None, None], final.astype(F32) / 32.0


def solution(mesh):
    fine = Mesh(mesh.devices.reshape([size for _, size in FINE]), [name for name, _ in FINE])
    placed = (
        P(CLIP, SEQ, None, None),
        P(CLIP, SEQ),
        P(CLIP, None, None, None),
        P(CLIP, SEQ, None, None),
        P(CLIP, None),
        P(CLIP, None),
        P(),
    )
    return jax.shard_map(
        on_device,
        mesh=fine,
        in_specs=placed,
        out_specs=(P(CLIP, SEQ, None, None), P(SEQ, None)),
        check_vma=False,
    )
```

```python
import jax
import jax.numpy as jnp
from jax import lax
from jax.experimental import pallas as pl
from jax.experimental.pallas import tpu as pltpu
from jax.sharding import Mesh
from jax.sharding import PartitionSpec as P

FINE = (("yh", 2), ("yl", 2), ("zh", 4), ("c", 2), ("zl", 4), ("x", 4))
SEQ = ("yh", "yl", "zh", "c")
CLIP = ("zl", "x")
D = 1152
HD = 72
PART = 288
WIDE = 384
SPAN = 896
HEADS = 4
ZS = 4
TOK = 32
ROWS = ZS * TOK
ALL = 4 * ROWS
BLOCK = 256
F32 = jnp.float32
BF16 = jnp.bfloat16
EPS = 1e-06
TEMPER = HD ** (-0.5)
PARAMS = pltpu.CompilerParams(vmem_limit_bytes=56 * 1024 * 1024)


def cost(flops, nbytes):
    return pl.CostEstimate(flops=flops, bytes_accessed=nbytes, transcendentals=0)


def normalise(hidden, power, inverse):
    scaled = jnp.clip(hidden.astype(F32) * power, -448.0, 448.0)
    rows = scaled * inverse
    centred = rows - jnp.mean(rows, axis=-1, keepdims=True)
    factor = lax.rsqrt(jnp.mean(centred * centred, axis=-1, keepdims=True) + EPS)
    return centred * factor, factor


def home_forward(power_ref, x_ref, hidden_ref, grad_ref, mod_ref, out_ref, turned_ref):
    normed, _ = normalise(hidden_ref[...], power_ref[0], power_ref[1])
    modded = normed * (1.0 + mod_ref[1:2, :]) + mod_ref[0:1, :]
    for x in range(4):

        @pl.when(x_ref[0] == x)
        def _(x=x):
            for place, block in enumerate(block_order(x)):
                turned_ref[:, place * HD : (place + 1) * HD] = modded[:, block * HD : (block + 1) * HD]

    out_ref[:, :TOK, :] = turned_ref[...].astype(BF16).reshape(ZS, TOK, D)
    out_ref[:, TOK:, :] = (mod_ref[2:3, :] * grad_ref[...].astype(F32)).astype(BF16).reshape(ZS, TOK, D)


def home_backward(power_ref, x_ref, hidden_ref, grad_ref, mod_ref, back_ref, out_ref, turned_ref):
    normed, factor = normalise(hidden_ref[...], power_ref[0], power_ref[1])
    back = back_ref[:, :TOK, :].reshape(ROWS, D).astype(F32)
    for x in range(4):

        @pl.when(x_ref[0] == x)
        def _(x=x):
            for place, block in enumerate(block_order(x)):
                turned_ref[:, block * HD : (block + 1) * HD] = back[:, place * HD : (place + 1) * HD]

    d_normed = turned_ref[...] * (1.0 + mod_ref[1:2, :])
    d_rows = factor * (
        d_normed
        - jnp.mean(d_normed, axis=-1, keepdims=True)
        - normed * jnp.mean(d_normed * normed, axis=-1, keepdims=True)
    )
    out_ref[...] = (grad_ref[...].astype(F32) + d_rows.astype(BF16).astype(F32)).astype(BF16)


def block_order(x):
    return [4 * zl + (x + step) % 4 for step in range(4) for zl in range(4)]


def pick_weights(place_ref, w_qkv_ref, w_out_ref, out_ref, unit_ref):
    qkv = w_qkv_ref[...].astype(F32)
    out = w_out_ref[...].astype(F32)
    for place in range(4):

        @pl.when(place_ref[0] == place)
        def _(place=place):
            yl, core = place // 2, place % 2
            for part in range(3):
                for high in range(2):
                    first = part * D + HD * (4 * (2 * high + yl) + 2 * core)
                    to = part * PART + high * 2 * HD
                    unit_ref[:, to : to + 2 * HD] = qkv[:, first : first + 2 * HD]
            unit_ref[:, 3 * PART :] = out[:, place * PART : (place + 1) * PART]

    unit = unit_ref[...].astype(BF16)
    for copy in range(4):
        out_ref[copy] = unit


def out_rows(x_ref, *refs):
    *block_refs, send_ref, rows_ref, sem = refs
    copies = [
        pltpu.make_async_copy(ref.at[:, pl.ds(768, 384)], rows_ref.at[step], sem.at[step])
        for step, ref in enumerate(block_refs)
    ]
    for copy in copies:
        copy.start()
    for copy in copies:
        copy.wait()
    blocks = [rows_ref[step].astype(F32)[:, 96:384] for step in range(4)]
    for x in range(4):

        @pl.when(x_ref[0] == x)
        def _(x=x):
            for place in range(4):
                yl, core = place // 2, place % 2
                pieces = []
                for high in range(2):
                    for low in range(2):
                        first = (2 * high + yl) * HD
                        pieces.append(blocks[(2 * core + low - x) % 4][first : first + HD])
                send_ref[place] = jnp.concatenate(pieces, axis=0).astype(BF16)


def nt(left, right):
    return lax.dot_general(left, right, (((1,), (1,)), ((), ())), preferred_element_type=F32)


def nn(left, right):
    return lax.dot_general(left, right, (((1,), (0,)), ((), ())), preferred_element_type=F32)


def tn(left, right):
    return lax.dot_general(left, right, (((0,), (0,)), ((), ())), preferred_element_type=F32)


def swap_pairs(values):
    parity = lax.broadcasted_iota(jnp.int32, (values.shape[0], 128), 1) % 2
    tiles = []
    for start in range(0, values.shape[1], 128):
        tile = values[:, start : start + 128]
        tiles.append(jnp.where(parity == 0, pltpu.roll(tile, 127, 1), pltpu.roll(tile, 1, 1)))
    return jnp.concatenate(tiles, axis=1)


def head_members():
    entry = lax.broadcasted_iota(jnp.int32, (WIDE, 128), 0)
    first = lax.broadcasted_iota(jnp.int32, (WIDE, 128), 1) * HD
    return ((entry >= first) & (entry < first + HD) & (entry < PART)).astype(F32).astype(BF16)


def split_dot(dot, values, members):
    high = values.astype(BF16)
    low = (values - high.astype(F32)).astype(BF16)
    return dot(high, members) + dot(low, members)


def window(head):
    start = head * HD // 128 * 128
    end = -(-(head + 1) * HD // 128) * 128
    column = lax.broadcasted_iota(jnp.int32, (BLOCK, end - start), 1) + start
    return start, end, (column >= head * HD) & (column < (head + 1) * HD)


def keep(values, mask):
    return jnp.where(mask, values, jnp.zeros_like(values))


def same_token():
    row = lax.broadcasted_iota(jnp.int32, (BLOCK, BLOCK), 0) % 16
    column = lax.broadcasted_iota(jnp.int32, (BLOCK, BLOCK), 1) % 16
    return row == column


def probabilities(q_hat, k_hat, same):
    scores = nt(q_hat, k_hat) * TEMPER
    exps = jnp.where(same, jnp.exp(scores), 0.0)
    return exps / jnp.sum(exps, axis=-1, keepdims=True)


def gather_rows(refs, start):
    return jnp.concatenate(
        [ref[:, first : first + 16, :].reshape(ZS * 16, D) for first in (start, start + 16) for ref in refs], axis=0
    )


def fetch_weights(block_refs, w_ref, sem):
    copies = [
        pltpu.make_async_copy(ref.at[:, pl.ds(0, SPAN)], w_ref.at[pl.ds(PART * step, PART), :], sem.at[step])
        for step, ref in enumerate(block_refs)
    ]
    for copy in copies:
        copy.start()
    return copies


def by_token(table):
    return jnp.broadcast_to(table[:, None, :], (16, 16, WIDE)).reshape(BLOCK, WIDE)


def widen(values):
    return jnp.concatenate([values, jnp.zeros((values.shape[0], WIDE - PART), values.dtype)], axis=1)


def chip_forward(*refs):
    row_refs, block_refs, (tab_ref, q_ref, k_ref, v_ref, qh_ref, kh_ref, qf_ref, kf_ref, part_ref, att_ref, w_ref, sem) = (
        refs[:4], refs[4:8], refs[8:]
    )
    copies = fetch_weights(block_refs, w_ref, sem)
    modded = gather_rows(row_refs, 0)
    members = head_members()
    for copy in copies:
        copy.wait()
    packed = nn(modded, w_ref[...])
    for place, (raw_ref, hat_ref, factor_ref) in enumerate(((q_ref, qh_ref, qf_ref), (k_ref, kh_ref, kf_ref))):
        raw = widen(packed[:, place * PART : (place + 1) * PART])
        raw_ref[...] = raw.astype(BF16)
        raw = raw_ref[...].astype(F32)
        factor = lax.rsqrt(split_dot(nn, raw * raw, members) / HD + EPS)
        factor_ref[...] = factor
        wide = split_dot(nt, factor, members)
        swapped = swap_pairs(raw)
        straight, ahead = by_token(tab_ref[2 * place]), by_token(tab_ref[2 * place + 1])
        for half in range(2):
            rows = slice(half * BLOCK, (half + 1) * BLOCK)
            turned = raw[rows] * straight + swapped[rows] * ahead
            hat_ref[rows, :] = (wide[rows] * turned).astype(BF16)
    v_ref[...] = widen(packed[:, 2 * PART : 3 * PART]).astype(BF16)
    same = same_token()
    att_ref[...] = jnp.zeros_like(att_ref)
    for head in range(HEADS):
        start, end, mask = window(head)
        for half in range(2):
            rows = slice(half * BLOCK, (half + 1) * BLOCK)
            probs = probabilities(keep(qh_ref[rows, start:end], mask), kh_ref[rows, start:end], same).astype(BF16)
            found = nn(probs, v_ref[rows, start:end]).astype(BF16)
            att_ref[rows, start:end] = jnp.where(mask, found, att_ref[rows, start:end])

    total = tn(att_ref[...], gather_rows(row_refs, TOK))
    for piece in range(8):
        part_ref[piece] = total[36 * piece : 36 * (piece + 1)].astype(BF16)


def chip_backward(*refs):
    row_refs, block_refs = refs[:4], refs[4:8]
    (
        wo_ref, tab_ref, q_ref, k_ref, v_ref, qh_ref, kh_ref, qf_ref, kf_ref,
        mine_ref, theirs_ref, do_ref, dv_ref, dqh_ref, dkh_ref, dqkv_ref, wide_ref, w_ref, sem,
    ) = refs[8:]
    copies = fetch_weights(block_refs, w_ref, sem)
    for place in range(4):
        wide_ref[:, place * PART : (place + 1) * PART] = wo_ref[place].astype(F32)
    do_ref[...] = widen(nt(gather_rows(row_refs, TOK), wide_ref[...].astype(BF16))).astype(BF16)
    same = same_token()
    members = head_members()
    for ref in (dv_ref, dqh_ref, dkh_ref):
        ref[...] = jnp.zeros_like(ref)
    for head in range(HEADS):
        start, end, mask = window(head)
        for half in range(2):
            rows = slice(half * BLOCK, (half + 1) * BLOCK)
            q_hat, k_hat = qh_ref[rows, start:end], kh_ref[rows, start:end]
            probs = probabilities(keep(q_hat, mask), k_hat, same)
            d_out = do_ref[rows, start:end]
            d_probs = nt(keep(d_out, mask), v_ref[rows, start:end])
            d_value = tn(probs.astype(BF16), d_out)
            spread = probs * d_probs
            d_scores = ((spread - probs * jnp.sum(spread, axis=-1, keepdims=True)) * TEMPER).astype(BF16)
            d_q = nn(d_scores, k_hat)
            d_k = tn(d_scores, q_hat)
            dv_ref[rows, start:end] = jnp.where(mask, d_value, dv_ref[rows, start:end])
            dqh_ref[rows, start:end] = jnp.where(mask, d_q, dqh_ref[rows, start:end])
            dkh_ref[rows, start:end] = jnp.where(mask, d_k, dkh_ref[rows, start:end])
    dqkv_ref[:, 3 * PART :] = jnp.zeros((ALL, SPAN - 3 * PART), F32)
    dqkv_ref[:, 2 * PART : 3 * PART] = dv_ref[:, :PART]
    for place, (raw_ref, factor_ref, turned_ref) in enumerate(
        ((q_ref, qf_ref, dqh_ref), (k_ref, kf_ref, dkh_ref))
    ):
        raw = raw_ref[...].astype(F32)
        factor = factor_ref[...]
        turned = turned_ref[...]
        swapped = swap_pairs(turned)
        straight, back = by_token(tab_ref[2 * place]), by_token(tab_ref[2 * place + 1])
        scaled = jnp.concatenate(
            [
                turned[first : first + BLOCK] * straight + swapped[first : first + BLOCK] * back
                for first in (0, BLOCK)
            ],
            axis=0,
        )
        inner = split_dot(nn, raw * scaled, members) / HD
        wide = split_dot(nt, factor, members)
        pulled = split_dot(nt, factor * factor * factor * inner, members)
        dqkv_ref[:, place * PART : (place + 1) * PART] = (wide * scaled - raw * pulled)[:, :PART]
    for copy in copies:
        copy.wait()
    total = nt(dqkv_ref[...].astype(BF16), w_ref[...])
    for half in range(2):
        for device in range(4):
            first = half * BLOCK + device * ZS * 16
            rows = total[first : first + ZS * 16].reshape(ZS, 16, D)
            out_ref = theirs_ref if device % 2 else mine_ref
            out_ref[device // 2, :, half * 16 : half * 16 + 16, :] = rows.astype(out_ref.dtype)


def turn_tables(qk_gain, yl, core):
    level = 2 * jnp.arange(ZS, dtype=jnp.int32)
    position = jnp.concatenate(
        [8 * y + level + c for y in (yl, 1 - yl) for c in (core, 1 - core)]
    ).astype(F32)
    column = jnp.arange(HD, dtype=jnp.int32)
    frequency = jnp.power(10000.0, -((2 * (column // 2)).astype(F32) / HD))
    angles = position[:, None] * frequency[None, :]
    cosine, sine = jnp.cos(angles), jnp.sin(angles)
    even = column % 2 == 0
    swapped = qk_gain.reshape(2, HD // 2, 2)[:, :, ::-1].reshape(2, HD)

    def spread(table):
        return jnp.pad(jnp.tile(table, (1, 1, HEADS)), ((0, 0), (0, 0), (0, WIDE - PART)))

    straight = [qk_gain[i] * cosine for i in range(2)]
    ahead = [jnp.where(even, -sine, sine) * swapped[i] for i in range(2)]
    back = [jnp.where(even, sine, -sine) * qk_gain[i] for i in range(2)]
    return (
        spread(jnp.stack([straight[0], ahead[0], straight[1], ahead[1]])),
        spread(jnp.stack([straight[0], back[0], straight[1], back[1]])),
    )


def on_device(hidden, exponent, modulation, out_grad, w_qkv, w_out, qk_gain):
    core, yl, x = lax.axis_index("c"), lax.axis_index("yl"), lax.axis_index("x")
    rows, cotangent = hidden[0, 0], out_grad[0, 0]
    shift_by = exponent[0, 0]
    power = jnp.stack(
        [
            lax.shift_left(jnp.int32(1), shift_by).astype(F32),
            lax.shift_left(jnp.int32(1), 24 - shift_by).astype(F32) * 2.0**-24,
        ]
    )
    mod = lax.dynamic_index_in_dim(modulation[0], lax.axis_index("yh"), 0, keepdims=False)
    x_place = x[None]
    smem = pl.BlockSpec(memory_space=pltpu.SMEM)
    vmem = pl.BlockSpec(memory_space=pltpu.VMEM)
    hbm = pl.BlockSpec(memory_space=pl.ANY)
    four = pltpu.SemaphoreType.DMA((4,))

    unit = pl.pallas_call(
        pick_weights,
        out_shape=jax.ShapeDtypeStruct((4, HD, 4 * PART), BF16),
        in_specs=[smem, vmem, vmem],
        out_specs=vmem,
        scratch_shapes=[pltpu.VMEM((HD, 4 * PART), F32)],
        compiler_params=PARAMS,
        cost_estimate=cost(10**6, 2 * 10**6),
    )((2 * yl + core)[None], w_qkv, w_out)
    block = lax.all_to_all(unit, "zl", 0, 0, tiled=True).reshape(PART, 4 * PART)
    blocks = [block] + [
        lax.ppermute(block, "x", [(i, (i + 4 - step) % 4) for i in range(4)]) for step in (1, 2, 3)
    ]

    sent = pl.pallas_call(
        home_forward,
        out_shape=jax.ShapeDtypeStruct((ZS, 2 * TOK, D), BF16),
        in_specs=[smem, smem, vmem, vmem, vmem],
        out_specs=vmem,
        scratch_shapes=[pltpu.VMEM((ROWS, D), F32)],
        compiler_params=PARAMS,
        cost_estimate=cost(20 * ROWS * D, 8 * ROWS * D),
    )(power, x_place, rows, cotangent, mod)

    def other_core(values):
        return lax.ppermute(values, "c", [(0, 1), (1, 0)])

    def other_y(values):
        return lax.ppermute(values, "yl", [(0, 1), (1, 0)])

    def exchange(values):
        return lax.all_to_all(values, "zh", 0, 0, tiled=True)

    tables, tables_back = turn_tables(qk_gain, yl, core)
    sent, _, tables, tables_back = lax.optimization_barrier((sent, block, tables, tables_back))
    own = exchange(sent)
    across = other_y(own)
    near = other_core(own)
    w_back = pl.pallas_call(
        out_rows,
        out_shape=jax.ShapeDtypeStruct((4, PART, PART), BF16),
        in_specs=[smem] + [hbm] * 4,
        out_specs=vmem,
        scratch_shapes=[pltpu.VMEM((4, PART, 384), BF16), four],
        compiler_params=PARAMS,
        cost_estimate=cost(10**6, 2 * 10**6),
    )(x_place, *blocks)
    across, w_back = lax.optimization_barrier((across, w_back))
    arrays = [own, near, across, other_core(across)]
    w_back = lax.all_to_all(w_back, ("yl", "c"), 0, 0, tiled=True)

    wide = jax.ShapeDtypeStruct((ALL, WIDE), BF16)
    factors = jax.ShapeDtypeStruct((ALL, 128), F32)
    *kept, part = pl.pallas_call(
        chip_forward,
        out_shape=[wide] * 5 + [factors] * 2 + [jax.ShapeDtypeStruct((8, 36, D), BF16)],
        in_specs=[vmem] * 4 + [hbm] * 4 + [vmem],
        out_specs=[vmem] * 8,
        scratch_shapes=[pltpu.VMEM((ALL, WIDE), BF16), pltpu.VMEM((D, SPAN), BF16), four],
        compiler_params=PARAMS,
        cost_estimate=cost(2 * ALL * D * 5 * PART, 12 * 10**6),
    )(*arrays, *blocks, tables)
    w_back, part = lax.optimization_barrier((w_back, part))

    plane = lax.all_to_all(part, ("yh", "x"), 0, 0, tiled=True)

    mine, theirs = pl.pallas_call(
        chip_backward,
        out_shape=[jax.ShapeDtypeStruct((2, ZS, TOK, D), F32), jax.ShapeDtypeStruct((2, ZS, TOK, D), BF16)],
        in_specs=[vmem] * 4 + [hbm] * 4 + [vmem] * 9,
        out_specs=[vmem] * 2,
        scratch_shapes=[
            pltpu.VMEM((ALL, WIDE), BF16),
            pltpu.VMEM((ALL, WIDE), F32),
            pltpu.VMEM((ALL, WIDE), F32),
            pltpu.VMEM((ALL, WIDE), F32),
            pltpu.VMEM((ALL, SPAN), F32),
            pltpu.VMEM((PART, D), F32),
            pltpu.VMEM((D, SPAN), BF16),
            four,
        ],
        compiler_params=PARAMS,
        cost_estimate=cost(2 * ALL * D * 4 * PART, 14 * 10**6),
    )(*arrays, *blocks, w_back, tables_back, *kept)
    theirs, plane = lax.optimization_barrier((theirs, plane))
    plane = jnp.sum(plane.astype(F32), axis=0).astype(BF16)
    plane = plane.reshape(4, 9, D)
    arrived = other_core(theirs)
    across = (mine[1] + arrived[1].astype(F32)).astype(BF16)
    from_y = other_y(across)
    summed = (mine[0] + arrived[0].astype(F32) + from_y.astype(F32)).astype(BF16)

    levels = lax.all_to_all(plane, "zl", 0, 0, tiled=True)
    level = jnp.sum(levels.astype(F32), axis=0).astype(BF16)
    level, summed = lax.optimization_barrier((level, summed))
    quarters = jnp.broadcast_to(jnp.pad(level, ((0, 3), (0, 0))).reshape(1, 4, 3, D), (2, 4, 3, D)).reshape(8, 3, D)
    spread = lax.all_to_all(quarters, ("c", "x"), 0, 0, tiled=True)
    wanted = lax.dynamic_index_in_dim(spread.reshape(4, 2, 3, D), core, 1, keepdims=False)
    joined = jnp.concatenate([summed, jnp.pad(wanted, ((0, 0), (0, 5), (0, 0)))], axis=1)
    joined = exchange(joined)
    d_hidden = pl.pallas_call(
        home_backward,
        out_shape=jax.ShapeDtypeStruct((ROWS, D), BF16),
        in_specs=[smem, smem, vmem, vmem, vmem, vmem],
        out_specs=vmem,
        scratch_shapes=[pltpu.VMEM((ROWS, D), F32)],
        compiler_params=PARAMS,
        cost_estimate=cost(30 * ROWS * D, 8 * ROWS * D),
    )(power, x_place, rows, cotangent, mod, joined)
    share = jnp.sum(joined[:, TOK : TOK + 3].astype(F32), axis=0).astype(BF16)
    final = lax.all_to_all(jnp.broadcast_to(share[None], (16, 3, D)), CLIP, 0, 0, tiled=True)
    final = final.reshape(4, 12, D)[:, :9].reshape(36, D)
    return d_hidden[None, None], final.astype(F32) / 32.0


def solution(mesh):
    fine = Mesh(mesh.devices.reshape([size for _, size in FINE]), [name for name, _ in FINE])
    placed = (
        P(CLIP, SEQ, None, None),
        P(CLIP, SEQ),
        P(CLIP, None, None, None),
        P(CLIP, SEQ, None, None),
        P(CLIP, None),
        P(CLIP, None),
        P(),
    )
    return jax.shard_map(
        on_device,
        mesh=fine,
        in_specs=placed,
        out_specs=(P(CLIP, SEQ, None, None), P(SEQ, None)),
        check_vma=False,
    )
```

```python
import jax
import jax.numpy as jnp
from jax import lax
from jax.experimental import pallas as pl
from jax.experimental.pallas import tpu as pltpu
from jax.sharding import Mesh
from jax.sharding import PartitionSpec as P

FINE = (("yh", 2), ("yl", 2), ("zh", 4), ("c", 2), ("zl", 4), ("x", 4))
SEQ = ("yh", "yl", "zh", "c")
CLIP = ("zl", "x")
D = 1152
HD = 72
PART = 288
WIDE = 384
SPAN = 896
HEADS = 4
ZS = 4
TOK = 32
ROWS = ZS * TOK
ALL = 4 * ROWS
BLOCK = 256
F32 = jnp.float32
BF16 = jnp.bfloat16
EPS = 1e-06
TEMPER = HD ** (-0.5)
PARAMS = pltpu.CompilerParams(vmem_limit_bytes=56 * 1024 * 1024)


SMALL = pltpu.CompilerParams(vmem_limit_bytes=24 * 1024 * 1024)


def cost(flops, nbytes):
    return pl.CostEstimate(flops=flops, bytes_accessed=nbytes, transcendentals=0)


def normalise(hidden, power, inverse):
    scaled = jnp.clip(hidden.astype(F32) * power, -448.0, 448.0)
    rows = scaled * inverse
    centred = rows - jnp.mean(rows, axis=-1, keepdims=True)
    factor = lax.rsqrt(jnp.mean(centred * centred, axis=-1, keepdims=True) + EPS)
    return centred * factor, factor


def home_forward(power_ref, x_ref, hidden_ref, grad_ref, mod_ref, out_ref, turned_ref):
    normed, _ = normalise(hidden_ref[...], power_ref[0], power_ref[1])
    modded = normed * (1.0 + mod_ref[1:2, :]) + mod_ref[0:1, :]
    for x in range(4):

        @pl.when(x_ref[0] == x)
        def _(x=x):
            for place, block in enumerate(block_order(x)):
                turned_ref[:, place * HD : (place + 1) * HD] = modded[:, block * HD : (block + 1) * HD]

    out_ref[:, :TOK, :] = turned_ref[...].astype(BF16).reshape(ZS, TOK, D)
    out_ref[:, TOK:, :] = (mod_ref[2:3, :] * grad_ref[...].astype(F32)).astype(BF16).reshape(ZS, TOK, D)


def home_backward(power_ref, x_ref, hidden_ref, grad_ref, mod_ref, back_ref, out_ref, turned_ref):
    normed, factor = normalise(hidden_ref[...], power_ref[0], power_ref[1])
    back = back_ref[:, :TOK, :].reshape(ROWS, D).astype(F32)
    for x in range(4):

        @pl.when(x_ref[0] == x)
        def _(x=x):
            for place, block in enumerate(block_order(x)):
                turned_ref[:, block * HD : (block + 1) * HD] = back[:, place * HD : (place + 1) * HD]

    d_normed = turned_ref[...] * (1.0 + mod_ref[1:2, :])
    d_rows = factor * (
        d_normed
        - jnp.mean(d_normed, axis=-1, keepdims=True)
        - normed * jnp.mean(d_normed * normed, axis=-1, keepdims=True)
    )
    out_ref[...] = (grad_ref[...].astype(F32) + d_rows.astype(BF16).astype(F32)).astype(BF16)


def block_order(x):
    return [4 * zl + (x + step) % 4 for step in range(4) for zl in range(4)]


def pick_weights(place_ref, w_qkv_ref, w_out_ref, out_ref, unit_ref):
    qkv = w_qkv_ref[...].astype(F32)
    out = w_out_ref[...].astype(F32)
    for place in range(4):

        @pl.when(place_ref[0] == place)
        def _(place=place):
            yl, core = place // 2, place % 2
            for part in range(3):
                for high in range(2):
                    first = part * D + HD * (4 * (2 * high + yl) + 2 * core)
                    to = part * PART + high * 2 * HD
                    unit_ref[:, to : to + 2 * HD] = qkv[:, first : first + 2 * HD]
            unit_ref[:, 3 * PART :] = out[:, place * PART : (place + 1) * PART]

    unit = unit_ref[...].astype(BF16)
    for copy in range(4):
        out_ref[copy] = unit


def out_rows(x_ref, *refs):
    *block_refs, send_ref, rows_ref, sem = refs
    copies = [
        pltpu.make_async_copy(ref.at[:, pl.ds(768, 384)], rows_ref.at[step], sem.at[step])
        for step, ref in enumerate(block_refs)
    ]
    for copy in copies:
        copy.start()
    for copy in copies:
        copy.wait()
    blocks = [rows_ref[step].astype(F32)[:, 96:384] for step in range(4)]
    for x in range(4):

        @pl.when(x_ref[0] == x)
        def _(x=x):
            for place in range(4):
                yl, core = place // 2, place % 2
                pieces = []
                for high in range(2):
                    for low in range(2):
                        first = (2 * high + yl) * HD
                        pieces.append(blocks[(2 * core + low - x) % 4][first : first + HD])
                send_ref[place] = jnp.concatenate(pieces, axis=0).astype(BF16)


def nt(left, right):
    return lax.dot_general(left, right, (((1,), (1,)), ((), ())), preferred_element_type=F32)


def nn(left, right):
    return lax.dot_general(left, right, (((1,), (0,)), ((), ())), preferred_element_type=F32)


def tn(left, right):
    return lax.dot_general(left, right, (((0,), (0,)), ((), ())), preferred_element_type=F32)


def swap_pairs(values):
    parity = lax.broadcasted_iota(jnp.int32, (values.shape[0], 128), 1) % 2
    tiles = []
    for start in range(0, values.shape[1], 128):
        tile = values[:, start : start + 128]
        tiles.append(jnp.where(parity == 0, pltpu.roll(tile, 127, 1), pltpu.roll(tile, 1, 1)))
    return jnp.concatenate(tiles, axis=1)


def head_members():
    entry = lax.broadcasted_iota(jnp.int32, (WIDE, 128), 0)
    first = lax.broadcasted_iota(jnp.int32, (WIDE, 128), 1) * HD
    return ((entry >= first) & (entry < first + HD) & (entry < PART)).astype(F32).astype(BF16)


def split_dot(dot, values, members):
    high = values.astype(BF16)
    low = (values - high.astype(F32)).astype(BF16)
    return dot(high, members) + dot(low, members)


def window(head):
    start = head * HD // 128 * 128
    end = -(-(head + 1) * HD // 128) * 128
    column = lax.broadcasted_iota(jnp.int32, (BLOCK, end - start), 1) + start
    return start, end, (column >= head * HD) & (column < (head + 1) * HD)


def keep(values, mask):
    return jnp.where(mask, values, jnp.zeros_like(values))


def same_token():
    row = lax.broadcasted_iota(jnp.int32, (BLOCK, BLOCK), 0) % 16
    column = lax.broadcasted_iota(jnp.int32, (BLOCK, BLOCK), 1) % 16
    return row == column


def probabilities(q_hat, k_hat, same):
    scores = nt(q_hat, k_hat) * TEMPER
    exps = jnp.where(same, jnp.exp(scores), 0.0)
    return exps / jnp.sum(exps, axis=-1, keepdims=True)


def gather_rows(refs, start):
    return jnp.concatenate(
        [ref[:, first : first + 16, :].reshape(ZS * 16, D) for first in (start, start + 16) for ref in refs], axis=0
    )


def fetch_weights(block_refs, w_ref, sem):
    copies = [
        pltpu.make_async_copy(ref.at[:, pl.ds(0, SPAN)], w_ref.at[pl.ds(PART * step, PART), :], sem.at[step])
        for step, ref in enumerate(block_refs)
    ]
    for copy in copies:
        copy.start()
    return copies


def by_token(table):
    return jnp.broadcast_to(table[:, None, :], (16, 16, WIDE)).reshape(BLOCK, WIDE)


def widen(values):
    return jnp.concatenate([values, jnp.zeros((values.shape[0], WIDE - PART), values.dtype)], axis=1)


def chip_forward(*refs):
    row_refs, block_refs, (tab_ref, q_ref, k_ref, v_ref, qh_ref, kh_ref, qf_ref, kf_ref, part_ref, att_ref, w_ref, sem) = (
        refs[:4], refs[4:8], refs[8:]
    )
    copies = fetch_weights(block_refs, w_ref, sem)
    modded = gather_rows(row_refs, 0)
    members = head_members()
    for copy in copies:
        copy.wait()
    packed = nn(modded, w_ref[...])
    for place, (raw_ref, hat_ref, factor_ref) in enumerate(((q_ref, qh_ref, qf_ref), (k_ref, kh_ref, kf_ref))):
        raw = widen(packed[:, place * PART : (place + 1) * PART])
        raw_ref[...] = raw.astype(BF16)
        raw = raw_ref[...].astype(F32)
        factor = lax.rsqrt(split_dot(nn, raw * raw, members) / HD + EPS)
        factor_ref[...] = factor
        wide = split_dot(nt, factor, members)
        swapped = swap_pairs(raw)
        straight, ahead = by_token(tab_ref[2 * place]), by_token(tab_ref[2 * place + 1])
        for half in range(2):
            rows = slice(half * BLOCK, (half + 1) * BLOCK)
            turned = raw[rows] * straight + swapped[rows] * ahead
            hat_ref[rows, :] = (wide[rows] * turned).astype(BF16)
    v_ref[...] = widen(packed[:, 2 * PART : 3 * PART]).astype(BF16)
    same = same_token()
    att_ref[...] = jnp.zeros_like(att_ref)
    for head in range(HEADS):
        start, end, mask = window(head)
        for half in range(2):
            rows = slice(half * BLOCK, (half + 1) * BLOCK)
            probs = probabilities(keep(qh_ref[rows, start:end], mask), kh_ref[rows, start:end], same).astype(BF16)
            found = nn(probs, v_ref[rows, start:end]).astype(BF16)
            att_ref[rows, start:end] = jnp.where(mask, found, att_ref[rows, start:end])

    total = tn(att_ref[...], gather_rows(row_refs, TOK))
    for piece in range(8):
        part_ref[piece] = total[36 * piece : 36 * (piece + 1)].astype(BF16)


def chip_backward(*refs):
    row_refs, block_refs = refs[:4], refs[4:8]
    (
        wo_ref, tab_ref, q_ref, k_ref, v_ref, qh_ref, kh_ref, qf_ref, kf_ref,
        mine_ref, theirs_ref, do_ref, dv_ref, dqh_ref, dkh_ref, dqkv_ref, wide_ref, w_ref, sem,
    ) = refs[8:]
    copies = fetch_weights(block_refs, w_ref, sem)
    for place in range(4):
        wide_ref[:, place * PART : (place + 1) * PART] = wo_ref[place].astype(F32)
    do_ref[...] = widen(nt(gather_rows(row_refs, TOK), wide_ref[...].astype(BF16))).astype(BF16)
    same = same_token()
    members = head_members()
    for ref in (dv_ref, dqh_ref, dkh_ref):
        ref[...] = jnp.zeros_like(ref)
    for head in range(HEADS):
        start, end, mask = window(head)
        for half in range(2):
            rows = slice(half * BLOCK, (half + 1) * BLOCK)
            q_hat, k_hat = qh_ref[rows, start:end], kh_ref[rows, start:end]
            probs = probabilities(keep(q_hat, mask), k_hat, same)
            d_out = do_ref[rows, start:end]
            d_probs = nt(keep(d_out, mask), v_ref[rows, start:end])
            d_value = tn(probs.astype(BF16), d_out)
            spread = probs * d_probs
            d_scores = ((spread - probs * jnp.sum(spread, axis=-1, keepdims=True)) * TEMPER).astype(BF16)
            d_q = nn(d_scores, k_hat)
            d_k = tn(d_scores, q_hat)
            dv_ref[rows, start:end] = jnp.where(mask, d_value, dv_ref[rows, start:end])
            dqh_ref[rows, start:end] = jnp.where(mask, d_q, dqh_ref[rows, start:end])
            dkh_ref[rows, start:end] = jnp.where(mask, d_k, dkh_ref[rows, start:end])
    dqkv_ref[:, 3 * PART :] = jnp.zeros((ALL, SPAN - 3 * PART), F32)
    dqkv_ref[:, 2 * PART : 3 * PART] = dv_ref[:, :PART]
    for place, (raw_ref, factor_ref, turned_ref) in enumerate(
        ((q_ref, qf_ref, dqh_ref), (k_ref, kf_ref, dkh_ref))
    ):
        raw = raw_ref[...].astype(F32)
        factor = factor_ref[...]
        turned = turned_ref[...]
        swapped = swap_pairs(turned)
        straight, back = by_token(tab_ref[2 * place]), by_token(tab_ref[2 * place + 1])
        scaled = jnp.concatenate(
            [
                turned[first : first + BLOCK] * straight + swapped[first : first + BLOCK] * back
                for first in (0, BLOCK)
            ],
            axis=0,
        )
        inner = split_dot(nn, raw * scaled, members) / HD
        wide = split_dot(nt, factor, members)
        pulled = split_dot(nt, factor * factor * factor * inner, members)
        dqkv_ref[:, place * PART : (place + 1) * PART] = (wide * scaled - raw * pulled)[:, :PART]
    for copy in copies:
        copy.wait()
    total = nt(dqkv_ref[...].astype(BF16), w_ref[...])
    for half in range(2):
        for device in range(4):
            first = half * BLOCK + device * ZS * 16
            rows = total[first : first + ZS * 16].reshape(ZS, 16, D)
            out_ref = theirs_ref if device % 2 else mine_ref
            out_ref[device // 2, :, half * 16 : half * 16 + 16, :] = rows.astype(out_ref.dtype)


def turn_tables(qk_gain, yl, core):
    level = 2 * jnp.arange(ZS, dtype=jnp.int32)
    position = jnp.concatenate(
        [8 * y + level + c for y in (yl, 1 - yl) for c in (core, 1 - core)]
    ).astype(F32)
    column = jnp.arange(HD, dtype=jnp.int32)
    frequency = jnp.power(10000.0, -((2 * (column // 2)).astype(F32) / HD))
    angles = position[:, None] * frequency[None, :]
    cosine, sine = jnp.cos(angles), jnp.sin(angles)
    even = column % 2 == 0
    swapped = qk_gain.reshape(2, HD // 2, 2)[:, :, ::-1].reshape(2, HD)

    def spread(table):
        return jnp.pad(jnp.tile(table, (1, 1, HEADS)), ((0, 0), (0, 0), (0, WIDE - PART)))

    straight = [qk_gain[i] * cosine for i in range(2)]
    ahead = [jnp.where(even, -sine, sine) * swapped[i] for i in range(2)]
    back = [jnp.where(even, sine, -sine) * qk_gain[i] for i in range(2)]
    return (
        spread(jnp.stack([straight[0], ahead[0], straight[1], ahead[1]])),
        spread(jnp.stack([straight[0], back[0], straight[1], back[1]])),
    )


def on_device(hidden, exponent, modulation, out_grad, w_qkv, w_out, qk_gain):
    core, yl, x = lax.axis_index("c"), lax.axis_index("yl"), lax.axis_index("x")
    rows, cotangent = hidden[0, 0], out_grad[0, 0]
    shift_by = exponent[0, 0]
    power = jnp.stack(
        [
            lax.shift_left(jnp.int32(1), shift_by).astype(F32),
            lax.shift_left(jnp.int32(1), 24 - shift_by).astype(F32) * 2.0**-24,
        ]
    )
    mod = lax.dynamic_index_in_dim(modulation[0], lax.axis_index("yh"), 0, keepdims=False)
    x_place = x[None]
    smem = pl.BlockSpec(memory_space=pltpu.SMEM)
    vmem = pl.BlockSpec(memory_space=pltpu.VMEM)
    hbm = pl.BlockSpec(memory_space=pl.ANY)
    four = pltpu.SemaphoreType.DMA((4,))

    unit = pl.pallas_call(
        pick_weights,
        out_shape=jax.ShapeDtypeStruct((4, HD, 4 * PART), BF16),
        in_specs=[smem, vmem, vmem],
        out_specs=vmem,
        scratch_shapes=[pltpu.VMEM((HD, 4 * PART), F32)],
        compiler_params=PARAMS,
        cost_estimate=cost(10**6, 2 * 10**6),
    )((2 * yl + core)[None], w_qkv, w_out)
    block = lax.all_to_all(unit, "zl", 0, 0, tiled=True).reshape(PART, 4 * PART)
    blocks = [block] + [
        lax.ppermute(block, "x", [(i, (i + 4 - step) % 4) for i in range(4)]) for step in (1, 2, 3)
    ]

    sent = pl.pallas_call(
        home_forward,
        out_shape=jax.ShapeDtypeStruct((ZS, 2 * TOK, D), BF16),
        in_specs=[smem, smem, vmem, vmem, vmem],
        out_specs=vmem,
        scratch_shapes=[pltpu.VMEM((ROWS, D), F32)],
        compiler_params=SMALL,
        cost_estimate=cost(20 * ROWS * D, 8 * ROWS * D),
    )(power, x_place, rows, cotangent, mod)

    def other_core(values):
        return lax.ppermute(values, "c", [(0, 1), (1, 0)])

    def other_y(values):
        return lax.ppermute(values, "yl", [(0, 1), (1, 0)])

    def exchange(values):
        return lax.all_to_all(values, "zh", 0, 0, tiled=True)

    tables, tables_back = turn_tables(qk_gain, yl, core)
    sent, _, tables, tables_back = lax.optimization_barrier((sent, block, tables, tables_back))
    own = exchange(sent)
    across = other_y(own)
    near = other_core(own)
    w_back = pl.pallas_call(
        out_rows,
        out_shape=jax.ShapeDtypeStruct((4, PART, PART), BF16),
        in_specs=[smem] + [hbm] * 4,
        out_specs=vmem,
        scratch_shapes=[pltpu.VMEM((4, PART, 384), BF16), four],
        compiler_params=PARAMS,
        cost_estimate=cost(10**6, 2 * 10**6),
    )(x_place, *blocks)
    across, w_back = lax.optimization_barrier((across, w_back))
    arrays = [own, near, across, other_core(across)]
    w_back = lax.all_to_all(w_back, ("yl", "c"), 0, 0, tiled=True)

    wide = jax.ShapeDtypeStruct((ALL, WIDE), BF16)
    factors = jax.ShapeDtypeStruct((ALL, 128), F32)
    *kept, part = pl.pallas_call(
        chip_forward,
        out_shape=[wide] * 5 + [factors] * 2 + [jax.ShapeDtypeStruct((8, 36, D), BF16)],
        in_specs=[vmem] * 4 + [hbm] * 4 + [vmem],
        out_specs=[vmem] * 8,
        scratch_shapes=[pltpu.VMEM((ALL, WIDE), BF16), pltpu.VMEM((D, SPAN), BF16), four],
        compiler_params=PARAMS,
        cost_estimate=cost(2 * ALL * D * 5 * PART, 12 * 10**6),
    )(*arrays, *blocks, tables)
    w_back, part = lax.optimization_barrier((w_back, part))

    plane = lax.all_to_all(part, ("yh", "x"), 0, 0, tiled=True)

    mine, theirs = pl.pallas_call(
        chip_backward,
        out_shape=[jax.ShapeDtypeStruct((2, ZS, TOK, D), F32), jax.ShapeDtypeStruct((2, ZS, TOK, D), BF16)],
        in_specs=[vmem] * 4 + [hbm] * 4 + [vmem] * 9,
        out_specs=[vmem] * 2,
        scratch_shapes=[
            pltpu.VMEM((ALL, WIDE), BF16),
            pltpu.VMEM((ALL, WIDE), F32),
            pltpu.VMEM((ALL, WIDE), F32),
            pltpu.VMEM((ALL, WIDE), F32),
            pltpu.VMEM((ALL, SPAN), F32),
            pltpu.VMEM((PART, D), F32),
            pltpu.VMEM((D, SPAN), BF16),
            four,
        ],
        compiler_params=PARAMS,
        cost_estimate=cost(2 * ALL * D * 4 * PART, 14 * 10**6),
    )(*arrays, *blocks, w_back, tables_back, *kept)
    theirs, plane = lax.optimization_barrier((theirs, plane))
    plane = jnp.sum(plane.astype(F32), axis=0).astype(BF16)
    plane = plane.reshape(4, 9, D)
    arrived = other_core(theirs)
    across = (mine[1] + arrived[1].astype(F32)).astype(BF16)

    levels = lax.all_to_all(plane, "zl", 0, 0, tiled=True)
    across, levels = lax.optimization_barrier((across, levels))
    from_y = other_y(across)
    summed = (mine[0] + arrived[0].astype(F32) + from_y.astype(F32)).astype(BF16)
    level = jnp.sum(levels.astype(F32), axis=0).astype(BF16)
    quarters = jnp.broadcast_to(jnp.pad(level, ((0, 3), (0, 0))).reshape(1, 4, 3, D), (2, 4, 3, D)).reshape(8, 3, D)
    spread = lax.all_to_all(quarters, ("c", "x"), 0, 0, tiled=True)
    wanted = lax.dynamic_index_in_dim(spread.reshape(4, 2, 3, D), core, 1, keepdims=False)
    joined = jnp.concatenate([summed, jnp.pad(wanted, ((0, 0), (0, 5), (0, 0)))], axis=1)
    joined = exchange(joined)
    d_hidden = pl.pallas_call(
        home_backward,
        out_shape=jax.ShapeDtypeStruct((ROWS, D), BF16),
        in_specs=[smem, smem, vmem, vmem, vmem, vmem],
        out_specs=vmem,
        scratch_shapes=[pltpu.VMEM((ROWS, D), F32)],
        compiler_params=SMALL,
        cost_estimate=cost(30 * ROWS * D, 8 * ROWS * D),
    )(power, x_place, rows, cotangent, mod, joined)
    share = jnp.sum(joined[:, TOK : TOK + 3].astype(F32), axis=0).astype(BF16)
    final = lax.all_to_all(jnp.broadcast_to(share[None], (16, 3, D)), CLIP, 0, 0, tiled=True)
    final = final.reshape(4, 12, D)[:, :9].reshape(36, D)
    return d_hidden[None, None], final.astype(F32) / 32.0


def solution(mesh):
    fine = Mesh(mesh.devices.reshape([size for _, size in FINE]), [name for name, _ in FINE])
    placed = (
        P(CLIP, SEQ, None, None),
        P(CLIP, SEQ),
        P(CLIP, None, None, None),
        P(CLIP, SEQ, None, None),
        P(CLIP, None),
        P(CLIP, None),
        P(),
    )
    return jax.shard_map(
        on_device,
        mesh=fine,
        in_specs=placed,
        out_specs=(P(CLIP, SEQ, None, None), P(SEQ, None)),
        check_vma=False,
    )
```

```python
import jax
import jax.numpy as jnp
from jax import lax
from jax.experimental import pallas as pl
from jax.experimental.pallas import tpu as pltpu
from jax.sharding import Mesh
from jax.sharding import PartitionSpec as P

FINE = (("yh", 2), ("yl", 2), ("zh", 4), ("c", 2), ("zl", 4), ("x", 4))
SEQ = ("yh", "yl", "zh", "c")
CLIP = ("zl", "x")
D = 1152
HD = 72
PART = 288
WIDE = 384
SPAN = 896
HEADS = 4
ZS = 4
TOK = 32
ROWS = ZS * TOK
ALL = 4 * ROWS
BLOCK = 256
F32 = jnp.float32
BF16 = jnp.bfloat16
EPS = 1e-06
TEMPER = HD ** (-0.5)
PARAMS = pltpu.CompilerParams(vmem_limit_bytes=56 * 1024 * 1024)


SMALL = pltpu.CompilerParams(vmem_limit_bytes=24 * 1024 * 1024)


def cost(flops, nbytes):
    return pl.CostEstimate(flops=flops, bytes_accessed=nbytes, transcendentals=0)


def normalise(hidden, power, inverse):
    scaled = jnp.clip(hidden.astype(F32) * power, -448.0, 448.0)
    rows = scaled * inverse
    centred = rows - jnp.mean(rows, axis=-1, keepdims=True)
    factor = lax.rsqrt(jnp.mean(centred * centred, axis=-1, keepdims=True) + EPS)
    return centred * factor, factor


def block_at(place, spot_ref):
    return 4 * lax.rem(spot_ref[1] + place % 4, 4) + lax.rem(spot_ref[0] + place // 4, 4)


def home_forward(power_ref, spot_ref, hidden_ref, grad_ref, mod_ref, out_ref, turned_ref, block_ref):
    normed, _ = normalise(hidden_ref[...], power_ref[0], power_ref[1])
    modded = normed * (1.0 + mod_ref[1:2, :]) + mod_ref[0:1, :]
    for block in range(16):
        block_ref[block] = modded[:, block * HD : (block + 1) * HD]
    for place in range(16):
        turned_ref[:, place * HD : (place + 1) * HD] = block_ref[block_at(place, spot_ref)]
    out_ref[:, :TOK, :] = turned_ref[...].astype(BF16).reshape(ZS, TOK, D)
    out_ref[:, TOK:, :] = (mod_ref[2:3, :] * grad_ref[...].astype(F32)).astype(BF16).reshape(ZS, TOK, D)


def home_backward(power_ref, spot_ref, hidden_ref, grad_ref, mod_ref, back_ref, out_ref, turned_ref, block_ref):
    normed, factor = normalise(hidden_ref[...], power_ref[0], power_ref[1])
    back = back_ref[:, :TOK, :].reshape(ROWS, D).astype(F32)
    for place in range(16):
        block_ref[block_at(place, spot_ref)] = back[:, place * HD : (place + 1) * HD]
    for block in range(16):
        turned_ref[:, block * HD : (block + 1) * HD] = block_ref[block]
    d_normed = turned_ref[...] * (1.0 + mod_ref[1:2, :])
    d_rows = factor * (
        d_normed
        - jnp.mean(d_normed, axis=-1, keepdims=True)
        - normed * jnp.mean(d_normed * normed, axis=-1, keepdims=True)
    )
    out_ref[...] = (grad_ref[...].astype(F32) + d_rows.astype(BF16).astype(F32)).astype(BF16)


def pick_weights(place_ref, w_qkv_ref, w_out_ref, out_ref, unit_ref):
    qkv = w_qkv_ref[...].astype(F32)
    out = w_out_ref[...].astype(F32)
    for place in range(4):

        @pl.when(place_ref[0] == place)
        def _(place=place):
            yl, core = place // 2, place % 2
            for part in range(3):
                for high in range(2):
                    first = part * D + HD * (4 * (2 * high + yl) + 2 * core)
                    to = part * PART + high * 2 * HD
                    unit_ref[:, to : to + 2 * HD] = qkv[:, first : first + 2 * HD]
            unit_ref[:, 3 * PART :] = out[:, place * PART : (place + 1) * PART]

    out_ref[...] = unit_ref[...].astype(BF16)


def out_rows(spot_ref, *refs):
    *block_refs, send_ref, rows_ref, head_ref, sem = refs
    copies = [
        pltpu.make_async_copy(ref.at[:, pl.ds(768, 384)], rows_ref.at[step], sem.at[step])
        for step, ref in enumerate(block_refs)
    ]
    for copy in copies:
        copy.start()
    for step, copy in enumerate(copies):
        copy.wait()
        rows = rows_ref[step].astype(F32)[:, 96:384]
        for level in range(4):
            head_ref[4 * step + level] = rows[level * HD : (level + 1) * HD]
    for place in range(4):
        yl, core = place // 2, place % 2
        pieces = [
            head_ref[4 * lax.rem(2 * core + low + 4 - spot_ref[0], 4) + lax.rem(2 * high + yl + 4 - spot_ref[1], 4)]
            for high in range(2)
            for low in range(2)
        ]
        send_ref[place] = jnp.concatenate(pieces, axis=0).astype(BF16)


def nt(left, right):
    return lax.dot_general(left, right, (((1,), (1,)), ((), ())), preferred_element_type=F32)


def nn(left, right):
    return lax.dot_general(left, right, (((1,), (0,)), ((), ())), preferred_element_type=F32)


def tn(left, right):
    return lax.dot_general(left, right, (((0,), (0,)), ((), ())), preferred_element_type=F32)


def swap_pairs(values):
    parity = lax.broadcasted_iota(jnp.int32, (values.shape[0], 128), 1) % 2
    tiles = []
    for start in range(0, values.shape[1], 128):
        tile = values[:, start : start + 128]
        tiles.append(jnp.where(parity == 0, pltpu.roll(tile, 127, 1), pltpu.roll(tile, 1, 1)))
    return jnp.concatenate(tiles, axis=1)


def head_members():
    entry = lax.broadcasted_iota(jnp.int32, (WIDE, 128), 0)
    first = lax.broadcasted_iota(jnp.int32, (WIDE, 128), 1) * HD
    return ((entry >= first) & (entry < first + HD) & (entry < PART)).astype(F32).astype(BF16)


def split_dot(dot, values, members):
    high = values.astype(BF16)
    low = (values - high.astype(F32)).astype(BF16)
    return dot(high, members) + dot(low, members)


def window(head):
    start = head * HD // 128 * 128
    end = -(-(head + 1) * HD // 128) * 128
    column = lax.broadcasted_iota(jnp.int32, (BLOCK, end - start), 1) + start
    return start, end, (column >= head * HD) & (column < (head + 1) * HD)


def keep(values, mask):
    return jnp.where(mask, values, jnp.zeros_like(values))


def same_token():
    row = lax.broadcasted_iota(jnp.int32, (BLOCK, BLOCK), 0) % 16
    column = lax.broadcasted_iota(jnp.int32, (BLOCK, BLOCK), 1) % 16
    return row == column


def probabilities(q_hat, k_hat, same):
    scores = nt(q_hat, k_hat) * TEMPER
    exps = jnp.where(same, jnp.exp(scores), 0.0)
    return exps / jnp.sum(exps, axis=-1, keepdims=True)


def gather_rows(refs, start):
    return jnp.concatenate(
        [ref[:, first : first + 16, :].reshape(ZS * 16, D) for first in (start, start + 16) for ref in refs], axis=0
    )


def fetch_weights(block_refs, w_ref, sem):
    copies = [
        pltpu.make_async_copy(ref.at[:, pl.ds(0, SPAN)], w_ref.at[pl.ds(PART * step, PART), :], sem.at[step])
        for step, ref in enumerate(block_refs)
    ]
    for copy in copies:
        copy.start()
    return copies


def by_token(table):
    return jnp.broadcast_to(table[:, None, :], (16, 16, WIDE)).reshape(BLOCK, WIDE)


def widen(values):
    return jnp.concatenate([values, jnp.zeros((values.shape[0], WIDE - PART), values.dtype)], axis=1)


def chip_forward(*refs):
    row_refs, block_refs, (tab_ref, q_ref, k_ref, v_ref, qh_ref, kh_ref, qf_ref, kf_ref, part_ref, att_ref, w_ref, sem) = (
        refs[:4], refs[4:8], refs[8:]
    )
    copies = fetch_weights(block_refs, w_ref, sem)
    modded = gather_rows(row_refs, 0)
    members = head_members()
    for copy in copies:
        copy.wait()
    packed = nn(modded, w_ref[...])
    for place, (raw_ref, hat_ref, factor_ref) in enumerate(((q_ref, qh_ref, qf_ref), (k_ref, kh_ref, kf_ref))):
        raw = widen(packed[:, place * PART : (place + 1) * PART])
        raw_ref[...] = raw.astype(BF16)
        raw = raw_ref[...].astype(F32)
        factor = lax.rsqrt(split_dot(nn, raw * raw, members) / HD + EPS)
        factor_ref[...] = factor
        wide = split_dot(nt, factor, members)
        swapped = swap_pairs(raw)
        straight, ahead = by_token(tab_ref[2 * place]), by_token(tab_ref[2 * place + 1])
        for half in range(2):
            rows = slice(half * BLOCK, (half + 1) * BLOCK)
            turned = raw[rows] * straight + swapped[rows] * ahead
            hat_ref[rows, :] = (wide[rows] * turned).astype(BF16)
    v_ref[...] = widen(packed[:, 2 * PART : 3 * PART]).astype(BF16)
    same = same_token()
    att_ref[...] = jnp.zeros_like(att_ref)
    for head in range(HEADS):
        start, end, mask = window(head)
        for half in range(2):
            rows = slice(half * BLOCK, (half + 1) * BLOCK)
            probs = probabilities(keep(qh_ref[rows, start:end], mask), kh_ref[rows, start:end], same).astype(BF16)
            found = nn(probs, v_ref[rows, start:end]).astype(BF16)
            att_ref[rows, start:end] = jnp.where(mask, found, att_ref[rows, start:end])

    total = tn(att_ref[...], gather_rows(row_refs, TOK))
    for piece in range(8):
        part_ref[piece] = total[36 * piece : 36 * (piece + 1)].astype(BF16)


def chip_backward(*refs):
    row_refs, block_refs = refs[:4], refs[4:8]
    (
        wo_ref, tab_ref, q_ref, k_ref, v_ref, qh_ref, kh_ref, qf_ref, kf_ref,
        mine_ref, theirs_ref, do_ref, dv_ref, dqh_ref, dkh_ref, dqkv_ref, wide_ref, w_ref, sem,
    ) = refs[8:]
    copies = fetch_weights(block_refs, w_ref, sem)
    for place in range(4):
        wide_ref[:, place * PART : (place + 1) * PART] = wo_ref[place].astype(F32)
    do_ref[...] = widen(nt(gather_rows(row_refs, TOK), wide_ref[...].astype(BF16))).astype(BF16)
    same = same_token()
    members = head_members()
    for ref in (dv_ref, dqh_ref, dkh_ref):
        ref[...] = jnp.zeros_like(ref)
    for head in range(HEADS):
        start, end, mask = window(head)
        for half in range(2):
            rows = slice(half * BLOCK, (half + 1) * BLOCK)
            q_hat, k_hat = qh_ref[rows, start:end], kh_ref[rows, start:end]
            probs = probabilities(keep(q_hat, mask), k_hat, same)
            d_out = do_ref[rows, start:end]
            d_probs = nt(keep(d_out, mask), v_ref[rows, start:end])
            d_value = tn(probs.astype(BF16), d_out)
            spread = probs * d_probs
            d_scores = ((spread - probs * jnp.sum(spread, axis=-1, keepdims=True)) * TEMPER).astype(BF16)
            d_q = nn(d_scores, k_hat)
            d_k = tn(d_scores, q_hat)
            dv_ref[rows, start:end] = jnp.where(mask, d_value, dv_ref[rows, start:end])
            dqh_ref[rows, start:end] = jnp.where(mask, d_q, dqh_ref[rows, start:end])
            dkh_ref[rows, start:end] = jnp.where(mask, d_k, dkh_ref[rows, start:end])
    dqkv_ref[:, 3 * PART :] = jnp.zeros((ALL, SPAN - 3 * PART), F32)
    dqkv_ref[:, 2 * PART : 3 * PART] = dv_ref[:, :PART]
    for place, (raw_ref, factor_ref, turned_ref) in enumerate(
        ((q_ref, qf_ref, dqh_ref), (k_ref, kf_ref, dkh_ref))
    ):
        raw = raw_ref[...].astype(F32)
        factor = factor_ref[...]
        turned = turned_ref[...]
        swapped = swap_pairs(turned)
        straight, back = by_token(tab_ref[2 * place]), by_token(tab_ref[2 * place + 1])
        scaled = jnp.concatenate(
            [
                turned[first : first + BLOCK] * straight + swapped[first : first + BLOCK] * back
                for first in (0, BLOCK)
            ],
            axis=0,
        )
        inner = split_dot(nn, raw * scaled, members) / HD
        wide = split_dot(nt, factor, members)
        pulled = split_dot(nt, factor * factor * factor * inner, members)
        dqkv_ref[:, place * PART : (place + 1) * PART] = (wide * scaled - raw * pulled)[:, :PART]
    for copy in copies:
        copy.wait()
    total = nt(dqkv_ref[...].astype(BF16), w_ref[...])
    for half in range(2):
        for device in range(4):
            first = half * BLOCK + device * ZS * 16
            rows = total[first : first + ZS * 16].reshape(ZS, 16, D)
            out_ref = theirs_ref if device % 2 else mine_ref
            out_ref[device // 2, :, half * 16 : half * 16 + 16, :] = rows.astype(out_ref.dtype)


def turn_tables(qk_gain, yl, core):
    level = 2 * jnp.arange(ZS, dtype=jnp.int32)
    position = jnp.concatenate(
        [8 * y + level + c for y in (yl, 1 - yl) for c in (core, 1 - core)]
    ).astype(F32)
    column = jnp.arange(HD, dtype=jnp.int32)
    frequency = jnp.power(10000.0, -((2 * (column // 2)).astype(F32) / HD))
    angles = position[:, None] * frequency[None, :]
    cosine, sine = jnp.cos(angles), jnp.sin(angles)
    even = column % 2 == 0
    swapped = qk_gain.reshape(2, HD // 2, 2)[:, :, ::-1].reshape(2, HD)

    def spread(table):
        return jnp.pad(jnp.tile(table, (1, 1, HEADS)), ((0, 0), (0, 0), (0, WIDE - PART)))

    straight = [qk_gain[i] * cosine for i in range(2)]
    ahead = [jnp.where(even, -sine, sine) * swapped[i] for i in range(2)]
    back = [jnp.where(even, sine, -sine) * qk_gain[i] for i in range(2)]
    return (
        spread(jnp.stack([straight[0], ahead[0], straight[1], ahead[1]])),
        spread(jnp.stack([straight[0], back[0], straight[1], back[1]])),
    )


def on_device(hidden, exponent, modulation, out_grad, w_qkv, w_out, qk_gain):
    core, yl, x = lax.axis_index("c"), lax.axis_index("yl"), lax.axis_index("x")
    rows, cotangent = hidden[0, 0], out_grad[0, 0]
    shift_by = exponent[0, 0]
    power = jnp.stack(
        [
            lax.shift_left(jnp.int32(1), shift_by).astype(F32),
            lax.shift_left(jnp.int32(1), 24 - shift_by).astype(F32) * 2.0**-24,
        ]
    )
    mod = lax.dynamic_index_in_dim(modulation[0], lax.axis_index("yh"), 0, keepdims=False)
    spot = jnp.stack([x, lax.axis_index("zl")])
    smem = pl.BlockSpec(memory_space=pltpu.SMEM)
    vmem = pl.BlockSpec(memory_space=pltpu.VMEM)
    hbm = pl.BlockSpec(memory_space=pl.ANY)
    four = pltpu.SemaphoreType.DMA((4,))

    unit = pl.pallas_call(
        pick_weights,
        out_shape=jax.ShapeDtypeStruct((HD, 4 * PART), BF16),
        in_specs=[smem, vmem, vmem],
        out_specs=vmem,
        scratch_shapes=[pltpu.VMEM((HD, 4 * PART), F32)],
        compiler_params=PARAMS,
        cost_estimate=cost(10**6, 2 * 10**6),
    )((2 * yl + core)[None], w_qkv, w_out)
    block = jnp.concatenate(
        [unit]
        + [lax.ppermute(unit, ("zh", "zl"), [(i, (i + 16 - step) % 16) for i in range(16)]) for step in (1, 2, -1)]
    )
    blocks = [block] + [
        lax.ppermute(block, "x", [(i, (i + 4 - step) % 4) for i in range(4)]) for step in (1, 2, 3)
    ]

    sent = pl.pallas_call(
        home_forward,
        out_shape=jax.ShapeDtypeStruct((ZS, 2 * TOK, D), BF16),
        in_specs=[smem, smem, vmem, vmem, vmem],
        out_specs=vmem,
        scratch_shapes=[pltpu.VMEM((ROWS, D), F32), pltpu.VMEM((16, ROWS, HD), F32)],
        compiler_params=SMALL,
        cost_estimate=cost(20 * ROWS * D, 8 * ROWS * D),
    )(power, spot, rows, cotangent, mod)

    def other_core(values):
        return lax.ppermute(values, "c", [(0, 1), (1, 0)])

    def other_y(values):
        return lax.ppermute(values, "yl", [(0, 1), (1, 0)])

    def exchange(values):
        return lax.all_to_all(values, "zh", 0, 0, tiled=True)

    tables, tables_back = turn_tables(qk_gain, yl, core)
    sent, _ = lax.optimization_barrier((sent, block))
    own = exchange(sent)
    own, tables, tables_back = lax.optimization_barrier((own, tables, tables_back))
    across = other_y(own)
    near = other_core(own)
    w_back = pl.pallas_call(
        out_rows,
        out_shape=jax.ShapeDtypeStruct((4, PART, PART), BF16),
        in_specs=[smem] + [hbm] * 4,
        out_specs=vmem,
        scratch_shapes=[pltpu.VMEM((4, PART, 384), BF16), pltpu.VMEM((16, HD, PART), F32), four],
        compiler_params=PARAMS,
        cost_estimate=cost(10**6, 2 * 10**6),
    )(spot, *blocks)
    across, w_back = lax.optimization_barrier((across, w_back))
    arrays = [own, near, across, other_core(across)]
    w_back = lax.all_to_all(w_back, ("yl", "c"), 0, 0, tiled=True)

    wide = jax.ShapeDtypeStruct((ALL, WIDE), BF16)
    factors = jax.ShapeDtypeStruct((ALL, 128), F32)
    *kept, part = pl.pallas_call(
        chip_forward,
        out_shape=[wide] * 5 + [factors] * 2 + [jax.ShapeDtypeStruct((8, 36, D), BF16)],
        in_specs=[vmem] * 4 + [hbm] * 4 + [vmem],
        out_specs=[vmem] * 8,
        scratch_shapes=[pltpu.VMEM((ALL, WIDE), BF16), pltpu.VMEM((D, SPAN), BF16), four],
        compiler_params=PARAMS,
        cost_estimate=cost(2 * ALL * D * 5 * PART, 12 * 10**6),
    )(*arrays, *blocks, tables)
    w_back, part = lax.optimization_barrier((w_back, part))

    plane = lax.all_to_all(part, ("yh", "x"), 0, 0, tiled=True)

    mine, theirs = pl.pallas_call(
        chip_backward,
        out_shape=[jax.ShapeDtypeStruct((2, ZS, TOK, D), F32), jax.ShapeDtypeStruct((2, ZS, TOK, D), BF16)],
        in_specs=[vmem] * 4 + [hbm] * 4 + [vmem] * 9,
        out_specs=[vmem] * 2,
        scratch_shapes=[
            pltpu.VMEM((ALL, WIDE), BF16),
            pltpu.VMEM((ALL, WIDE), F32),
            pltpu.VMEM((ALL, WIDE), F32),
            pltpu.VMEM((ALL, WIDE), F32),
            pltpu.VMEM((ALL, SPAN), F32),
            pltpu.VMEM((PART, D), F32),
            pltpu.VMEM((D, SPAN), BF16),
            four,
        ],
        compiler_params=PARAMS,
        cost_estimate=cost(2 * ALL * D * 4 * PART, 14 * 10**6),
    )(*arrays, *blocks, w_back, tables_back, *kept)
    theirs, plane = lax.optimization_barrier((theirs, plane))
    plane = jnp.sum(plane.astype(F32), axis=0).astype(BF16)
    plane = plane.reshape(4, 9, D)
    arrived = other_core(theirs)
    across = (mine[1] + arrived[1].astype(F32)).astype(BF16)

    levels = lax.all_to_all(plane, "zl", 0, 0, tiled=True)
    across, levels = lax.optimization_barrier((across, levels))
    from_y = other_y(across)
    summed = (mine[0] + arrived[0].astype(F32) + from_y.astype(F32)).astype(BF16)
    level = jnp.sum(levels.astype(F32), axis=0).astype(BF16)
    quarters = jnp.broadcast_to(jnp.pad(level, ((0, 3), (0, 0))).reshape(1, 4, 3, D), (2, 4, 3, D)).reshape(8, 3, D)
    spread = lax.all_to_all(quarters, ("c", "x"), 0, 0, tiled=True)
    wanted = lax.dynamic_index_in_dim(spread.reshape(4, 2, 3, D), core, 1, keepdims=False)
    joined = jnp.concatenate([summed, jnp.pad(wanted, ((0, 0), (0, 5), (0, 0)))], axis=1)
    joined = exchange(joined)
    d_hidden = pl.pallas_call(
        home_backward,
        out_shape=jax.ShapeDtypeStruct((ROWS, D), BF16),
        in_specs=[smem, smem, vmem, vmem, vmem, vmem],
        out_specs=vmem,
        scratch_shapes=[pltpu.VMEM((ROWS, D), F32), pltpu.VMEM((16, ROWS, HD), F32)],
        compiler_params=SMALL,
        cost_estimate=cost(30 * ROWS * D, 8 * ROWS * D),
    )(power, spot, rows, cotangent, mod, joined)
    share = jnp.sum(joined[:, TOK : TOK + 3].astype(F32), axis=0).astype(BF16)
    final = lax.all_to_all(jnp.broadcast_to(share[None], (16, 3, D)), CLIP, 0, 0, tiled=True)
    final = final.reshape(4, 12, D)[:, :9].reshape(36, D)
    return d_hidden[None, None], final.astype(F32) / 32.0


def solution(mesh):
    fine = Mesh(mesh.devices.reshape([size for _, size in FINE]), [name for name, _ in FINE])
    placed = (
        P(CLIP, SEQ, None, None),
        P(CLIP, SEQ),
        P(CLIP, None, None, None),
        P(CLIP, SEQ, None, None),
        P(CLIP, None),
        P(CLIP, None),
        P(),
    )
    return jax.shard_map(
        on_device,
        mesh=fine,
        in_specs=placed,
        out_specs=(P(CLIP, SEQ, None, None), P(SEQ, None)),
        check_vma=False,
    )
```

```python
import jax
import jax.numpy as jnp
from jax import lax
from jax.experimental import pallas as pl
from jax.experimental.pallas import tpu as pltpu
from jax.sharding import Mesh
from jax.sharding import PartitionSpec as P

FINE = (("yh", 2), ("yl", 2), ("zh", 4), ("c", 2), ("zl", 4), ("x", 4))
SEQ = ("yh", "yl", "zh", "c")
CLIP = ("zl", "x")
D = 1152
HD = 72
PART = 288
WIDE = 384
SPAN = 896
HEADS = 4
ZS = 4
TOK = 32
ROWS = ZS * TOK
ALL = 4 * ROWS
BLOCK = 256
F32 = jnp.float32
BF16 = jnp.bfloat16
EPS = 1e-06
TEMPER = HD ** (-0.5)
PARAMS = pltpu.CompilerParams(vmem_limit_bytes=56 * 1024 * 1024)


SMALL = pltpu.CompilerParams(vmem_limit_bytes=24 * 1024 * 1024)


def cost(flops, nbytes):
    return pl.CostEstimate(flops=flops, bytes_accessed=nbytes, transcendentals=0)


def normalise(hidden, power, inverse):
    scaled = jnp.clip(hidden.astype(F32) * power, -448.0, 448.0)
    rows = scaled * inverse
    centred = rows - jnp.mean(rows, axis=-1, keepdims=True)
    factor = lax.rsqrt(jnp.mean(centred * centred, axis=-1, keepdims=True) + EPS)
    return centred * factor, factor


def block_at(place, spot_ref):
    return 4 * lax.rem(spot_ref[1] + place % 4, 4) + lax.rem(spot_ref[0] + place // 4, 4)


def home_forward(power_ref, spot_ref, hidden_ref, grad_ref, mod_ref, out_ref, turned_ref, block_ref):
    normed, _ = normalise(hidden_ref[...], power_ref[0], power_ref[1])
    modded = normed * (1.0 + mod_ref[1:2, :]) + mod_ref[0:1, :]
    for block in range(16):
        block_ref[block] = modded[:, block * HD : (block + 1) * HD]
    for place in range(16):
        turned_ref[:, place * HD : (place + 1) * HD] = block_ref[block_at(place, spot_ref)]
    out_ref[:, :TOK, :] = turned_ref[...].astype(BF16).reshape(ZS, TOK, D)
    out_ref[:, TOK:, :] = (mod_ref[2:3, :] * grad_ref[...].astype(F32)).astype(BF16).reshape(ZS, TOK, D)


def home_backward(power_ref, spot_ref, hidden_ref, grad_ref, mod_ref, back_ref, out_ref, turned_ref, block_ref):
    normed, factor = normalise(hidden_ref[...], power_ref[0], power_ref[1])
    back = back_ref[:, :TOK, :].reshape(ROWS, D).astype(F32)
    for place in range(16):
        block_ref[block_at(place, spot_ref)] = back[:, place * HD : (place + 1) * HD]
    for block in range(16):
        turned_ref[:, block * HD : (block + 1) * HD] = block_ref[block]
    d_normed = turned_ref[...] * (1.0 + mod_ref[1:2, :])
    d_rows = factor * (
        d_normed
        - jnp.mean(d_normed, axis=-1, keepdims=True)
        - normed * jnp.mean(d_normed * normed, axis=-1, keepdims=True)
    )
    out_ref[...] = (grad_ref[...].astype(F32) + d_rows.astype(BF16).astype(F32)).astype(BF16)


def pick_weights(place_ref, w_qkv_ref, w_out_ref, out_ref, unit_ref):
    qkv = w_qkv_ref[...].astype(F32)
    out = w_out_ref[...].astype(F32)
    for place in range(4):

        @pl.when(place_ref[0] == place)
        def _(place=place):
            yl, core = place // 2, place % 2
            for part in range(3):
                for high in range(2):
                    first = part * D + HD * (4 * (2 * high + yl) + 2 * core)
                    to = part * PART + high * 2 * HD
                    unit_ref[:, to : to + 2 * HD] = qkv[:, first : first + 2 * HD]
            unit_ref[:, 3 * PART :] = out[:, place * PART : (place + 1) * PART]

    out_ref[...] = unit_ref[...].astype(BF16)


def out_rows(spot_ref, *refs):
    *block_refs, send_ref, rows_ref, head_ref, sem = refs
    copies = [
        pltpu.make_async_copy(ref.at[:, pl.ds(768, 384)], rows_ref.at[step], sem.at[step])
        for step, ref in enumerate(block_refs)
    ]
    for copy in copies:
        copy.start()
    for step, copy in enumerate(copies):
        copy.wait()
        rows = rows_ref[step].astype(F32)[:, 96:384]
        for level in range(4):
            head_ref[4 * step + level] = rows[level * HD : (level + 1) * HD]
    for place in range(4):
        yl, core = place // 2, place % 2
        pieces = [
            head_ref[4 * lax.rem(2 * core + low + 4 - spot_ref[0], 4) + lax.rem(2 * high + yl + 4 - spot_ref[1], 4)]
            for high in range(2)
            for low in range(2)
        ]
        send_ref[place] = jnp.concatenate(pieces, axis=0).astype(BF16)


def nt(left, right):
    return lax.dot_general(left, right, (((1,), (1,)), ((), ())), preferred_element_type=F32)


def nn(left, right):
    return lax.dot_general(left, right, (((1,), (0,)), ((), ())), preferred_element_type=F32)


def tn(left, right):
    return lax.dot_general(left, right, (((0,), (0,)), ((), ())), preferred_element_type=F32)


def swap_pairs(values):
    parity = lax.broadcasted_iota(jnp.int32, (values.shape[0], 128), 1) % 2
    tiles = []
    for start in range(0, values.shape[1], 128):
        tile = values[:, start : start + 128]
        tiles.append(jnp.where(parity == 0, pltpu.roll(tile, 127, 1), pltpu.roll(tile, 1, 1)))
    return jnp.concatenate(tiles, axis=1)


def head_members():
    entry = lax.broadcasted_iota(jnp.int32, (WIDE, 128), 0)
    first = lax.broadcasted_iota(jnp.int32, (WIDE, 128), 1) * HD
    return ((entry >= first) & (entry < first + HD) & (entry < PART)).astype(F32).astype(BF16)


def split_dot(dot, values, members):
    high = values.astype(BF16)
    low = (values - high.astype(F32)).astype(BF16)
    return dot(high, members) + dot(low, members)


def window(head):
    start = head * HD // 128 * 128
    end = -(-(head + 1) * HD // 128) * 128
    column = lax.broadcasted_iota(jnp.int32, (BLOCK, end - start), 1) + start
    return start, end, (column >= head * HD) & (column < (head + 1) * HD)


def keep(values, mask):
    return jnp.where(mask, values, jnp.zeros_like(values))


def same_token():
    row = lax.broadcasted_iota(jnp.int32, (BLOCK, BLOCK), 0) % 16
    column = lax.broadcasted_iota(jnp.int32, (BLOCK, BLOCK), 1) % 16
    return row == column


def probabilities(q_hat, k_hat, same):
    scores = nt(q_hat, k_hat) * TEMPER
    exps = jnp.where(same, jnp.exp(scores), 0.0)
    return exps / jnp.sum(exps, axis=-1, keepdims=True)


def gather_rows(refs, start):
    return jnp.concatenate(
        [ref[:, first : first + 16, :].reshape(ZS * 16, D) for first in (start, start + 16) for ref in refs], axis=0
    )


def fetch_weights(block_refs, w_ref, sem):
    copies = [
        pltpu.make_async_copy(ref.at[:, pl.ds(0, SPAN)], w_ref.at[pl.ds(PART * step, PART), :], sem.at[step])
        for step, ref in enumerate(block_refs)
    ]
    for copy in copies:
        copy.start()
    return copies


def by_token(table):
    return jnp.broadcast_to(table[:, None, :], (16, 16, WIDE)).reshape(BLOCK, WIDE)


def widen(values):
    return jnp.concatenate([values, jnp.zeros((values.shape[0], WIDE - PART), values.dtype)], axis=1)


def chip_forward(*refs):
    row_refs, block_refs, (tab_ref, q_ref, k_ref, v_ref, qh_ref, kh_ref, qf_ref, kf_ref, part_ref, att_ref, w_ref, sem) = (
        refs[:4], refs[4:8], refs[8:]
    )
    copies = fetch_weights(block_refs, w_ref, sem)
    modded = gather_rows(row_refs, 0)
    members = head_members()
    for copy in copies:
        copy.wait()
    packed = nn(modded, w_ref[...])
    for place, (raw_ref, hat_ref, factor_ref) in enumerate(((q_ref, qh_ref, qf_ref), (k_ref, kh_ref, kf_ref))):
        raw = widen(packed[:, place * PART : (place + 1) * PART])
        raw_ref[...] = raw.astype(BF16)
        raw = raw_ref[...].astype(F32)
        factor = lax.rsqrt(split_dot(nn, raw * raw, members) / HD + EPS)
        factor_ref[...] = factor
        wide = split_dot(nt, factor, members)
        swapped = swap_pairs(raw)
        straight, ahead = by_token(tab_ref[2 * place]), by_token(tab_ref[2 * place + 1])
        for half in range(2):
            rows = slice(half * BLOCK, (half + 1) * BLOCK)
            turned = raw[rows] * straight + swapped[rows] * ahead
            hat_ref[rows, :] = (wide[rows] * turned).astype(BF16)
    v_ref[...] = widen(packed[:, 2 * PART : 3 * PART]).astype(BF16)
    same = same_token()
    att_ref[...] = jnp.zeros_like(att_ref)
    for head in range(HEADS):
        start, end, mask = window(head)
        for half in range(2):
            rows = slice(half * BLOCK, (half + 1) * BLOCK)
            probs = probabilities(keep(qh_ref[rows, start:end], mask), kh_ref[rows, start:end], same).astype(BF16)
            found = nn(probs, v_ref[rows, start:end]).astype(BF16)
            att_ref[rows, start:end] = jnp.where(mask, found, att_ref[rows, start:end])

    total = tn(att_ref[...], gather_rows(row_refs, TOK))
    for piece in range(8):
        part_ref[piece] = total[36 * piece : 36 * (piece + 1)].astype(BF16)


def chip_backward(*refs):
    row_refs, block_refs = refs[:4], refs[4:8]
    (
        wo_ref, tab_ref, q_ref, k_ref, v_ref, qh_ref, kh_ref, qf_ref, kf_ref,
        mine_ref, theirs_ref, do_ref, dv_ref, dqh_ref, dkh_ref, dqkv_ref, wide_ref, w_ref, sem,
    ) = refs[8:]
    copies = fetch_weights(block_refs, w_ref, sem)
    for place in range(4):
        wide_ref[:, place * PART : (place + 1) * PART] = wo_ref[place].astype(F32)
    do_ref[...] = widen(nt(gather_rows(row_refs, TOK), wide_ref[...].astype(BF16))).astype(BF16)
    same = same_token()
    members = head_members()
    for ref in (dv_ref, dqh_ref, dkh_ref):
        ref[...] = jnp.zeros_like(ref)
    for head in range(HEADS):
        start, end, mask = window(head)
        for half in range(2):
            rows = slice(half * BLOCK, (half + 1) * BLOCK)
            q_hat, k_hat = qh_ref[rows, start:end], kh_ref[rows, start:end]
            probs = probabilities(keep(q_hat, mask), k_hat, same)
            d_out = do_ref[rows, start:end]
            d_probs = nt(keep(d_out, mask), v_ref[rows, start:end])
            d_value = tn(probs.astype(BF16), d_out)
            spread = probs * d_probs
            d_scores = ((spread - probs * jnp.sum(spread, axis=-1, keepdims=True)) * TEMPER).astype(BF16)
            d_q = nn(d_scores, k_hat)
            d_k = tn(d_scores, q_hat)
            dv_ref[rows, start:end] = jnp.where(mask, d_value, dv_ref[rows, start:end])
            dqh_ref[rows, start:end] = jnp.where(mask, d_q, dqh_ref[rows, start:end])
            dkh_ref[rows, start:end] = jnp.where(mask, d_k, dkh_ref[rows, start:end])
    dqkv_ref[:, 3 * PART :] = jnp.zeros((ALL, SPAN - 3 * PART), F32)
    dqkv_ref[:, 2 * PART : 3 * PART] = dv_ref[:, :PART]
    for place, (raw_ref, factor_ref, turned_ref) in enumerate(
        ((q_ref, qf_ref, dqh_ref), (k_ref, kf_ref, dkh_ref))
    ):
        raw = raw_ref[...].astype(F32)
        factor = factor_ref[...]
        turned = turned_ref[...]
        swapped = swap_pairs(turned)
        straight, back = by_token(tab_ref[2 * place]), by_token(tab_ref[2 * place + 1])
        scaled = jnp.concatenate(
            [
                turned[first : first + BLOCK] * straight + swapped[first : first + BLOCK] * back
                for first in (0, BLOCK)
            ],
            axis=0,
        )
        inner = split_dot(nn, raw * scaled, members) / HD
        wide = split_dot(nt, factor, members)
        pulled = split_dot(nt, factor * factor * factor * inner, members)
        dqkv_ref[:, place * PART : (place + 1) * PART] = (wide * scaled - raw * pulled)[:, :PART]
    for copy in copies:
        copy.wait()
    total = nt(dqkv_ref[...].astype(BF16), w_ref[...])
    for half in range(2):
        for device in range(4):
            first = half * BLOCK + device * ZS * 16
            rows = total[first : first + ZS * 16].reshape(ZS, 16, D)
            out_ref = theirs_ref if device % 2 else mine_ref
            out_ref[device // 2, :, half * 16 : half * 16 + 16, :] = rows.astype(out_ref.dtype)


def turn_tables(qk_gain, yl, core):
    level = 2 * jnp.arange(ZS, dtype=jnp.int32)
    position = jnp.concatenate(
        [8 * y + level + c for y in (yl, 1 - yl) for c in (core, 1 - core)]
    ).astype(F32)
    column = jnp.arange(HD, dtype=jnp.int32)
    frequency = jnp.power(10000.0, -((2 * (column // 2)).astype(F32) / HD))
    angles = position[:, None] * frequency[None, :]
    cosine, sine = jnp.cos(angles), jnp.sin(angles)
    even = column % 2 == 0
    swapped = qk_gain.reshape(2, HD // 2, 2)[:, :, ::-1].reshape(2, HD)

    def spread(table):
        return jnp.pad(jnp.tile(table, (1, 1, HEADS)), ((0, 0), (0, 0), (0, WIDE - PART)))

    straight = [qk_gain[i] * cosine for i in range(2)]
    ahead = [jnp.where(even, -sine, sine) * swapped[i] for i in range(2)]
    back = [jnp.where(even, sine, -sine) * qk_gain[i] for i in range(2)]
    return (
        spread(jnp.stack([straight[0], ahead[0], straight[1], ahead[1]])),
        spread(jnp.stack([straight[0], back[0], straight[1], back[1]])),
    )


def on_device(hidden, exponent, modulation, out_grad, w_qkv, w_out, qk_gain):
    core, yl, x = lax.axis_index("c"), lax.axis_index("yl"), lax.axis_index("x")
    rows, cotangent = hidden[0, 0], out_grad[0, 0]
    shift_by = exponent[0, 0]
    power = jnp.stack(
        [
            lax.shift_left(jnp.int32(1), shift_by).astype(F32),
            lax.shift_left(jnp.int32(1), 24 - shift_by).astype(F32) * 2.0**-24,
        ]
    )
    mod = lax.dynamic_index_in_dim(modulation[0], lax.axis_index("yh"), 0, keepdims=False)
    spot = jnp.stack([x, lax.axis_index("zl")])
    smem = pl.BlockSpec(memory_space=pltpu.SMEM)
    vmem = pl.BlockSpec(memory_space=pltpu.VMEM)
    hbm = pl.BlockSpec(memory_space=pl.ANY)
    four = pltpu.SemaphoreType.DMA((4,))

    unit = pl.pallas_call(
        pick_weights,
        out_shape=jax.ShapeDtypeStruct((HD, 4 * PART), BF16),
        in_specs=[smem, vmem, vmem],
        out_specs=vmem,
        scratch_shapes=[pltpu.VMEM((HD, 4 * PART), F32)],
        compiler_params=PARAMS,
        cost_estimate=cost(10**6, 2 * 10**6),
    )((2 * yl + core)[None], w_qkv, w_out)
    block = jnp.concatenate(
        [unit]
        + [lax.ppermute(unit, ("zh", "zl"), [(i, (i + 16 - step) % 16) for i in range(16)]) for step in (1, 2, -1)]
    )
    blocks = [block] + [
        lax.ppermute(block, "x", [(i, (i + 4 - step) % 4) for i in range(4)]) for step in (1, 2, 3)
    ]

    sent = pl.pallas_call(
        home_forward,
        out_shape=jax.ShapeDtypeStruct((ZS, 2 * TOK, D), BF16),
        in_specs=[smem, smem, vmem, vmem, vmem],
        out_specs=vmem,
        scratch_shapes=[pltpu.VMEM((ROWS, D), F32), pltpu.VMEM((16, ROWS, HD), F32)],
        compiler_params=SMALL,
        cost_estimate=cost(20 * ROWS * D, 8 * ROWS * D),
    )(power, spot, rows, cotangent, mod)

    def other_core(values):
        return lax.ppermute(values, "c", [(0, 1), (1, 0)])

    def other_y(values):
        return lax.ppermute(values, "yl", [(0, 1), (1, 0)])

    def exchange(values):
        return lax.all_to_all(values, "zh", 0, 0, tiled=True)

    tables, tables_back = turn_tables(qk_gain, yl, core)
    sent, _, tables, tables_back = lax.optimization_barrier((sent, block, tables, tables_back))
    own = exchange(sent)
    across = other_y(own)
    near = other_core(own)
    w_back = pl.pallas_call(
        out_rows,
        out_shape=jax.ShapeDtypeStruct((4, PART, PART), BF16),
        in_specs=[smem] + [hbm] * 4,
        out_specs=vmem,
        scratch_shapes=[pltpu.VMEM((4, PART, 384), BF16), pltpu.VMEM((16, HD, PART), F32), four],
        compiler_params=PARAMS,
        cost_estimate=cost(10**6, 2 * 10**6),
    )(spot, *blocks)
    across, w_back = lax.optimization_barrier((across, w_back))
    arrays = [own, near, across, other_core(across)]
    w_back = lax.all_to_all(w_back, ("yl", "c"), 0, 0, tiled=True)

    wide = jax.ShapeDtypeStruct((ALL, WIDE), BF16)
    factors = jax.ShapeDtypeStruct((ALL, 128), F32)
    *kept, part = pl.pallas_call(
        chip_forward,
        out_shape=[wide] * 5 + [factors] * 2 + [jax.ShapeDtypeStruct((8, 36, D), BF16)],
        in_specs=[vmem] * 4 + [hbm] * 4 + [vmem],
        out_specs=[vmem] * 8,
        scratch_shapes=[pltpu.VMEM((ALL, WIDE), BF16), pltpu.VMEM((D, SPAN), BF16), four],
        compiler_params=PARAMS,
        cost_estimate=cost(2 * ALL * D * 5 * PART, 12 * 10**6),
    )(*arrays, *blocks, tables)
    w_back, part = lax.optimization_barrier((w_back, part))

    plane = lax.all_to_all(part, ("yh", "x"), 0, 0, tiled=True)

    mine, theirs = pl.pallas_call(
        chip_backward,
        out_shape=[jax.ShapeDtypeStruct((2, ZS, TOK, D), F32), jax.ShapeDtypeStruct((2, ZS, TOK, D), BF16)],
        in_specs=[vmem] * 4 + [hbm] * 4 + [vmem] * 9,
        out_specs=[vmem] * 2,
        scratch_shapes=[
            pltpu.VMEM((ALL, WIDE), BF16),
            pltpu.VMEM((ALL, WIDE), F32),
            pltpu.VMEM((ALL, WIDE), F32),
            pltpu.VMEM((ALL, WIDE), F32),
            pltpu.VMEM((ALL, SPAN), F32),
            pltpu.VMEM((PART, D), F32),
            pltpu.VMEM((D, SPAN), BF16),
            four,
        ],
        compiler_params=PARAMS,
        cost_estimate=cost(2 * ALL * D * 4 * PART, 14 * 10**6),
    )(*arrays, *blocks, w_back, tables_back, *kept)
    theirs, plane = lax.optimization_barrier((theirs, plane))
    plane = jnp.sum(plane.astype(F32), axis=0).astype(BF16)
    plane = plane.reshape(4, 9, D)
    arrived = other_core(theirs)
    across = (mine[1] + arrived[1].astype(F32)).astype(BF16)

    levels = lax.all_to_all(plane, "zl", 0, 0, tiled=True)
    across, levels = lax.optimization_barrier((across, levels))
    from_y = other_y(across)
    summed = (mine[0] + arrived[0].astype(F32) + from_y.astype(F32)).astype(BF16)
    level = jnp.sum(levels.astype(F32), axis=0).astype(BF16)
    quarters = jnp.broadcast_to(jnp.pad(level, ((0, 3), (0, 0))).reshape(1, 4, 3, D), (2, 4, 3, D)).reshape(8, 3, D)
    spread = lax.all_to_all(quarters, ("c", "x"), 0, 0, tiled=True)
    wanted = lax.dynamic_index_in_dim(spread.reshape(4, 2, 3, D), core, 1, keepdims=False)
    joined = jnp.concatenate([summed, jnp.pad(wanted, ((0, 0), (0, 5), (0, 0)))], axis=1)
    joined = exchange(joined)
    d_hidden = pl.pallas_call(
        home_backward,
        out_shape=jax.ShapeDtypeStruct((ROWS, D), BF16),
        in_specs=[smem, smem, vmem, vmem, vmem, vmem],
        out_specs=vmem,
        scratch_shapes=[pltpu.VMEM((ROWS, D), F32), pltpu.VMEM((16, ROWS, HD), F32)],
        compiler_params=SMALL,
        cost_estimate=cost(30 * ROWS * D, 8 * ROWS * D),
    )(power, spot, rows, cotangent, mod, joined)
    share = jnp.sum(joined[:, TOK : TOK + 3].astype(F32), axis=0).astype(BF16)
    final = lax.all_to_all(jnp.broadcast_to(share[None], (16, 3, D)), CLIP, 0, 0, tiled=True)
    final = final.reshape(4, 12, D)[:, :9].reshape(36, D)
    return d_hidden[None, None], final.astype(F32) / 32.0


def solution(mesh):
    fine = Mesh(mesh.devices.reshape([size for _, size in FINE]), [name for name, _ in FINE])
    placed = (
        P(CLIP, SEQ, None, None),
        P(CLIP, SEQ),
        P(CLIP, None, None, None),
        P(CLIP, SEQ, None, None),
        P(CLIP, None),
        P(CLIP, None),
        P(),
    )
    return jax.shard_map(
        on_device,
        mesh=fine,
        in_specs=placed,
        out_specs=(P(CLIP, SEQ, None, None), P(SEQ, None)),
        check_vma=False,
    )
```

```python
import jax
import jax.numpy as jnp
from jax import lax
from jax.experimental import pallas as pl
from jax.experimental.pallas import tpu as pltpu
from jax.sharding import Mesh
from jax.sharding import PartitionSpec as P

FINE = (("yh", 2), ("yl", 2), ("zh", 4), ("c", 2), ("zl", 4), ("x", 4))
SEQ = ("yh", "yl", "zh", "c")
CLIP = ("zl", "x")
D = 1152
HD = 72
PART = 288
WIDE = 384
SPAN = 896
HEADS = 4
ZS = 4
TOK = 32
ROWS = ZS * TOK
ALL = 4 * ROWS
BLOCK = 256
F32 = jnp.float32
BF16 = jnp.bfloat16
EPS = 1e-06
TEMPER = HD ** (-0.5)
PARAMS = pltpu.CompilerParams(vmem_limit_bytes=56 * 1024 * 1024)


SMALL = pltpu.CompilerParams(vmem_limit_bytes=24 * 1024 * 1024)


def cost(flops, nbytes):
    return pl.CostEstimate(flops=flops, bytes_accessed=nbytes, transcendentals=0)


def normalise(hidden, power, inverse):
    scaled = jnp.clip(hidden.astype(F32) * power, -448.0, 448.0)
    rows = scaled * inverse
    centred = rows - jnp.mean(rows, axis=-1, keepdims=True)
    factor = lax.rsqrt(jnp.mean(centred * centred, axis=-1, keepdims=True) + EPS)
    return centred * factor, factor


def block_at(place, spot_ref):
    return 4 * lax.rem(spot_ref[1] + place % 4, 4) + lax.rem(spot_ref[0] + place // 4, 4)


def home_forward(power_ref, spot_ref, hidden_ref, grad_ref, mod_ref, out_ref, turned_ref, block_ref):
    normed, _ = normalise(hidden_ref[...], power_ref[0], power_ref[1])
    modded = normed * (1.0 + mod_ref[1:2, :]) + mod_ref[0:1, :]
    for block in range(16):
        block_ref[block] = modded[:, block * HD : (block + 1) * HD]
    for place in range(16):
        turned_ref[:, place * HD : (place + 1) * HD] = block_ref[block_at(place, spot_ref)]
    out_ref[:, :TOK, :] = turned_ref[...].astype(BF16).reshape(ZS, TOK, D)
    out_ref[:, TOK:, :] = (mod_ref[2:3, :] * grad_ref[...].astype(F32)).astype(BF16).reshape(ZS, TOK, D)


def home_backward(power_ref, spot_ref, hidden_ref, grad_ref, mod_ref, back_ref, out_ref, turned_ref, block_ref):
    normed, factor = normalise(hidden_ref[...], power_ref[0], power_ref[1])
    back = back_ref[:, :TOK, :].reshape(ROWS, D).astype(F32)
    for place in range(16):
        block_ref[block_at(place, spot_ref)] = back[:, place * HD : (place + 1) * HD]
    for block in range(16):
        turned_ref[:, block * HD : (block + 1) * HD] = block_ref[block]
    d_normed = turned_ref[...] * (1.0 + mod_ref[1:2, :])
    d_rows = factor * (
        d_normed
        - jnp.mean(d_normed, axis=-1, keepdims=True)
        - normed * jnp.mean(d_normed * normed, axis=-1, keepdims=True)
    )
    out_ref[...] = (grad_ref[...].astype(F32) + d_rows.astype(BF16).astype(F32)).astype(BF16)


def pick_weights(place_ref, w_qkv_ref, w_out_ref, out_ref, unit_ref):
    qkv = w_qkv_ref[...].astype(F32)
    out = w_out_ref[...].astype(F32)
    for place in range(4):

        @pl.when(place_ref[0] == place)
        def _(place=place):
            yl, core = place // 2, place % 2
            for part in range(3):
                for high in range(2):
                    first = part * D + HD * (4 * (2 * high + yl) + 2 * core)
                    to = part * PART + high * 2 * HD
                    unit_ref[:, to : to + 2 * HD] = qkv[:, first : first + 2 * HD]
            unit_ref[:, 3 * PART :] = out[:, place * PART : (place + 1) * PART]

    out_ref[...] = unit_ref[...].astype(BF16)


def out_rows(spot_ref, *refs):
    *block_refs, send_ref, rows_ref, head_ref, sem = refs
    copies = [
        pltpu.make_async_copy(ref.at[:, pl.ds(768, 384)], rows_ref.at[step], sem.at[step])
        for step, ref in enumerate(block_refs)
    ]
    for copy in copies:
        copy.start()
    for step, copy in enumerate(copies):
        copy.wait()
        rows = rows_ref[step].astype(F32)[:, 96:384]
        for level in range(4):
            head_ref[4 * step + level] = rows[level * HD : (level + 1) * HD]
    for place in range(4):
        yl, core = place // 2, place % 2
        pieces = [
            head_ref[4 * lax.rem(2 * core + low + 4 - spot_ref[0], 4) + lax.rem(2 * high + yl + 4 - spot_ref[1], 4)]
            for high in range(2)
            for low in range(2)
        ]
        send_ref[place] = jnp.concatenate(pieces, axis=0).astype(BF16)


def nt(left, right):
    return lax.dot_general(left, right, (((1,), (1,)), ((), ())), preferred_element_type=F32)


def nn(left, right):
    return lax.dot_general(left, right, (((1,), (0,)), ((), ())), preferred_element_type=F32)


def tn(left, right):
    return lax.dot_general(left, right, (((0,), (0,)), ((), ())), preferred_element_type=F32)


def swap_pairs(values):
    parity = lax.broadcasted_iota(jnp.int32, (values.shape[0], 128), 1) % 2
    tiles = []
    for start in range(0, values.shape[1], 128):
        tile = values[:, start : start + 128]
        tiles.append(jnp.where(parity == 0, pltpu.roll(tile, 127, 1), pltpu.roll(tile, 1, 1)))
    return jnp.concatenate(tiles, axis=1)


def head_members():
    entry = lax.broadcasted_iota(jnp.int32, (WIDE, 128), 0)
    first = lax.broadcasted_iota(jnp.int32, (WIDE, 128), 1) * HD
    return ((entry >= first) & (entry < first + HD) & (entry < PART)).astype(F32).astype(BF16)


def split_dot(dot, values, members):
    high = values.astype(BF16)
    low = (values - high.astype(F32)).astype(BF16)
    return dot(high, members) + dot(low, members)


def window(head):
    start = head * HD // 128 * 128
    end = -(-(head + 1) * HD // 128) * 128
    column = lax.broadcasted_iota(jnp.int32, (BLOCK, end - start), 1) + start
    return start, end, (column >= head * HD) & (column < (head + 1) * HD)


def keep(values, mask):
    return jnp.where(mask, values, jnp.zeros_like(values))


def same_token():
    row = lax.broadcasted_iota(jnp.int32, (BLOCK, BLOCK), 0) % 16
    column = lax.broadcasted_iota(jnp.int32, (BLOCK, BLOCK), 1) % 16
    return row == column


def probabilities(q_hat, k_hat, same):
    scores = nt(q_hat, k_hat) * TEMPER
    exps = jnp.where(same, jnp.exp(scores), 0.0)
    return exps / jnp.sum(exps, axis=-1, keepdims=True)


def gather_rows(refs, start):
    return jnp.concatenate(
        [ref[:, first : first + 16, :].reshape(ZS * 16, D) for first in (start, start + 16) for ref in refs], axis=0
    )


def fetch_weights(block_refs, w_ref, sem):
    copies = [
        pltpu.make_async_copy(ref.at[:, pl.ds(0, SPAN)], w_ref.at[pl.ds(PART * step, PART), :], sem.at[step])
        for step, ref in enumerate(block_refs)
    ]
    for copy in copies:
        copy.start()
    return copies


def by_token(table):
    return jnp.broadcast_to(table[:, None, :], (16, 16, WIDE)).reshape(BLOCK, WIDE)


def widen(values):
    return jnp.concatenate([values, jnp.zeros((values.shape[0], WIDE - PART), values.dtype)], axis=1)


def chip_forward(*refs):
    row_refs, block_refs, (tab_ref, q_ref, k_ref, v_ref, qh_ref, kh_ref, qf_ref, kf_ref, part_ref, att_ref, w_ref, sem) = (
        refs[:4], refs[4:8], refs[8:]
    )
    copies = fetch_weights(block_refs, w_ref, sem)
    modded = gather_rows(row_refs, 0)
    members = head_members()
    for copy in copies:
        copy.wait()
    packed = nn(modded, w_ref[...])
    for place, (raw_ref, hat_ref, factor_ref) in enumerate(((q_ref, qh_ref, qf_ref), (k_ref, kh_ref, kf_ref))):
        raw = widen(packed[:, place * PART : (place + 1) * PART])
        raw_ref[...] = raw.astype(BF16)
        raw = raw_ref[...].astype(F32)
        factor = lax.rsqrt(split_dot(nn, raw * raw, members) / HD + EPS)
        factor_ref[...] = factor
        wide = split_dot(nt, factor, members)
        swapped = swap_pairs(raw)
        straight, ahead = by_token(tab_ref[2 * place]), by_token(tab_ref[2 * place + 1])
        for half in range(2):
            rows = slice(half * BLOCK, (half + 1) * BLOCK)
            turned = raw[rows] * straight + swapped[rows] * ahead
            hat_ref[rows, :] = (wide[rows] * turned).astype(BF16)
    v_ref[...] = widen(packed[:, 2 * PART : 3 * PART]).astype(BF16)
    same = same_token()
    att_ref[...] = jnp.zeros_like(att_ref)
    for head in range(HEADS):
        start, end, mask = window(head)
        for half in range(2):
            rows = slice(half * BLOCK, (half + 1) * BLOCK)
            probs = probabilities(keep(qh_ref[rows, start:end], mask), kh_ref[rows, start:end], same).astype(BF16)
            found = nn(probs, v_ref[rows, start:end]).astype(BF16)
            att_ref[rows, start:end] = jnp.where(mask, found, att_ref[rows, start:end])

    total = tn(att_ref[...], gather_rows(row_refs, TOK))
    for piece in range(8):
        part_ref[piece] = total[36 * piece : 36 * (piece + 1)].astype(BF16)


def chip_backward(*refs):
    row_refs, block_refs = refs[:4], refs[4:8]
    (
        wo_ref, tab_ref, q_ref, k_ref, v_ref, qh_ref, kh_ref, qf_ref, kf_ref,
        mine_ref, theirs_ref, do_ref, dv_ref, dqh_ref, dkh_ref, dqkv_ref, wide_ref, w_ref, sem,
    ) = refs[8:]
    copies = fetch_weights(block_refs, w_ref, sem)
    for place in range(4):
        wide_ref[:, place * PART : (place + 1) * PART] = wo_ref[place].astype(F32)
    do_ref[...] = widen(nt(gather_rows(row_refs, TOK), wide_ref[...].astype(BF16))).astype(BF16)
    same = same_token()
    members = head_members()
    for ref in (dv_ref, dqh_ref, dkh_ref):
        ref[...] = jnp.zeros_like(ref)
    for head in range(HEADS):
        start, end, mask = window(head)
        for half in range(2):
            rows = slice(half * BLOCK, (half + 1) * BLOCK)
            q_hat, k_hat = qh_ref[rows, start:end], kh_ref[rows, start:end]
            probs = probabilities(keep(q_hat, mask), k_hat, same)
            d_out = do_ref[rows, start:end]
            d_probs = nt(keep(d_out, mask), v_ref[rows, start:end])
            d_value = tn(probs.astype(BF16), d_out)
            spread = probs * d_probs
            d_scores = ((spread - probs * jnp.sum(spread, axis=-1, keepdims=True)) * TEMPER).astype(BF16)
            d_q = nn(d_scores, k_hat)
            d_k = tn(d_scores, q_hat)
            dv_ref[rows, start:end] = jnp.where(mask, d_value, dv_ref[rows, start:end])
            dqh_ref[rows, start:end] = jnp.where(mask, d_q, dqh_ref[rows, start:end])
            dkh_ref[rows, start:end] = jnp.where(mask, d_k, dkh_ref[rows, start:end])
    dqkv_ref[:, 3 * PART :] = jnp.zeros((ALL, SPAN - 3 * PART), F32)
    dqkv_ref[:, 2 * PART : 3 * PART] = dv_ref[:, :PART]
    for place, (raw_ref, factor_ref, turned_ref) in enumerate(
        ((q_ref, qf_ref, dqh_ref), (k_ref, kf_ref, dkh_ref))
    ):
        raw = raw_ref[...].astype(F32)
        factor = factor_ref[...]
        turned = turned_ref[...]
        swapped = swap_pairs(turned)
        straight, back = by_token(tab_ref[2 * place]), by_token(tab_ref[2 * place + 1])
        scaled = jnp.concatenate(
            [
                turned[first : first + BLOCK] * straight + swapped[first : first + BLOCK] * back
                for first in (0, BLOCK)
            ],
            axis=0,
        )
        inner = split_dot(nn, raw * scaled, members) / HD
        wide = split_dot(nt, factor, members)
        pulled = split_dot(nt, factor * factor * factor * inner, members)
        dqkv_ref[:, place * PART : (place + 1) * PART] = (wide * scaled - raw * pulled)[:, :PART]
    for copy in copies:
        copy.wait()
    total = nt(dqkv_ref[...].astype(BF16), w_ref[...])
    for half in range(2):
        for device in range(4):
            first = half * BLOCK + device * ZS * 16
            rows = total[first : first + ZS * 16].reshape(ZS, 16, D)
            out_ref = theirs_ref if device % 2 else mine_ref
            out_ref[device // 2, :, half * 16 : half * 16 + 16, :] = rows.astype(out_ref.dtype)


def turn_tables(qk_gain, yl, core):
    level = 2 * jnp.arange(ZS, dtype=jnp.int32)
    position = jnp.concatenate(
        [8 * y + level + c for y in (yl, 1 - yl) for c in (core, 1 - core)]
    ).astype(F32)
    column = jnp.arange(HD, dtype=jnp.int32)
    frequency = jnp.power(10000.0, -((2 * (column // 2)).astype(F32) / HD))
    angles = position[:, None] * frequency[None, :]
    cosine, sine = jnp.cos(angles), jnp.sin(angles)
    even = column % 2 == 0
    swapped = qk_gain.reshape(2, HD // 2, 2)[:, :, ::-1].reshape(2, HD)

    def spread(table):
        return jnp.pad(jnp.tile(table, (1, 1, HEADS)), ((0, 0), (0, 0), (0, WIDE - PART)))

    straight = [qk_gain[i] * cosine for i in range(2)]
    ahead = [jnp.where(even, -sine, sine) * swapped[i] for i in range(2)]
    back = [jnp.where(even, sine, -sine) * qk_gain[i] for i in range(2)]
    return (
        spread(jnp.stack([straight[0], ahead[0], straight[1], ahead[1]])),
        spread(jnp.stack([straight[0], back[0], straight[1], back[1]])),
    )


def on_device(hidden, exponent, modulation, out_grad, w_qkv, w_out, qk_gain):
    core, yl, x = lax.axis_index("c"), lax.axis_index("yl"), lax.axis_index("x")
    rows, cotangent = hidden[0, 0], out_grad[0, 0]
    shift_by = exponent[0, 0]
    power = jnp.stack(
        [
            lax.shift_left(jnp.int32(1), shift_by).astype(F32),
            lax.shift_left(jnp.int32(1), 24 - shift_by).astype(F32) * 2.0**-24,
        ]
    )
    mod = lax.dynamic_index_in_dim(modulation[0], lax.axis_index("yh"), 0, keepdims=False)
    spot = jnp.stack([x, lax.axis_index("zl")])
    smem = pl.BlockSpec(memory_space=pltpu.SMEM)
    vmem = pl.BlockSpec(memory_space=pltpu.VMEM)
    hbm = pl.BlockSpec(memory_space=pl.ANY)
    four = pltpu.SemaphoreType.DMA((4,))

    unit = pl.pallas_call(
        pick_weights,
        out_shape=jax.ShapeDtypeStruct((HD, 4 * PART), BF16),
        in_specs=[smem, vmem, vmem],
        out_specs=vmem,
        scratch_shapes=[pltpu.VMEM((HD, 4 * PART), F32)],
        compiler_params=SMALL,
        cost_estimate=cost(10**6, 2 * 10**6),
    )((2 * yl + core)[None], w_qkv, w_out)
    block = jnp.concatenate(
        [unit]
        + [lax.ppermute(unit, ("zh", "zl"), [(i, (i + 16 - step) % 16) for i in range(16)]) for step in (1, 2, -1)]
    )
    blocks = [block] + [
        lax.ppermute(block, "x", [(i, (i + 4 - step) % 4) for i in range(4)]) for step in (1, 2, 3)
    ]

    sent = pl.pallas_call(
        home_forward,
        out_shape=jax.ShapeDtypeStruct((ZS, 2 * TOK, D), BF16),
        in_specs=[smem, smem, vmem, vmem, vmem],
        out_specs=vmem,
        scratch_shapes=[pltpu.VMEM((ROWS, D), F32), pltpu.VMEM((16, ROWS, HD), F32)],
        compiler_params=SMALL,
        cost_estimate=cost(20 * ROWS * D, 8 * ROWS * D),
    )(power, spot, rows, cotangent, mod)

    def other_core(values):
        return lax.ppermute(values, "c", [(0, 1), (1, 0)])

    def other_y(values):
        return lax.ppermute(values, "yl", [(0, 1), (1, 0)])

    def exchange(values):
        return lax.all_to_all(values, "zh", 0, 0, tiled=True)

    tables, tables_back = turn_tables(qk_gain, yl, core)
    sent, _, tables, tables_back = lax.optimization_barrier((sent, block, tables, tables_back))
    own = exchange(sent)
    across = other_y(own)
    near = other_core(own)
    w_back = pl.pallas_call(
        out_rows,
        out_shape=jax.ShapeDtypeStruct((4, PART, PART), BF16),
        in_specs=[smem] + [hbm] * 4,
        out_specs=vmem,
        scratch_shapes=[pltpu.VMEM((4, PART, 384), BF16), pltpu.VMEM((16, HD, PART), F32), four],
        compiler_params=SMALL,
        cost_estimate=cost(10**6, 2 * 10**6),
    )(spot, *blocks)
    across, w_back = lax.optimization_barrier((across, w_back))
    arrays = [own, near, across, other_core(across)]
    w_back = lax.all_to_all(w_back, ("yl", "c"), 0, 0, tiled=True)

    wide = jax.ShapeDtypeStruct((ALL, WIDE), BF16)
    factors = jax.ShapeDtypeStruct((ALL, 128), F32)
    *kept, part = pl.pallas_call(
        chip_forward,
        out_shape=[wide] * 5 + [factors] * 2 + [jax.ShapeDtypeStruct((8, 36, D), BF16)],
        in_specs=[vmem] * 4 + [hbm] * 4 + [vmem],
        out_specs=[vmem] * 8,
        scratch_shapes=[pltpu.VMEM((ALL, WIDE), BF16), pltpu.VMEM((D, SPAN), BF16), four],
        compiler_params=PARAMS,
        cost_estimate=cost(2 * ALL * D * 5 * PART, 12 * 10**6),
    )(*arrays, *blocks, tables)
    w_back, part = lax.optimization_barrier((w_back, part))

    plane = lax.all_to_all(part, ("yh", "x"), 0, 0, tiled=True)

    mine, theirs = pl.pallas_call(
        chip_backward,
        out_shape=[jax.ShapeDtypeStruct((2, ZS, TOK, D), F32), jax.ShapeDtypeStruct((2, ZS, TOK, D), BF16)],
        in_specs=[vmem] * 4 + [hbm] * 4 + [vmem] * 9,
        out_specs=[vmem] * 2,
        scratch_shapes=[
            pltpu.VMEM((ALL, WIDE), BF16),
            pltpu.VMEM((ALL, WIDE), F32),
            pltpu.VMEM((ALL, WIDE), F32),
            pltpu.VMEM((ALL, WIDE), F32),
            pltpu.VMEM((ALL, SPAN), F32),
            pltpu.VMEM((PART, D), F32),
            pltpu.VMEM((D, SPAN), BF16),
            four,
        ],
        compiler_params=PARAMS,
        cost_estimate=cost(2 * ALL * D * 4 * PART, 14 * 10**6),
    )(*arrays, *blocks, w_back, tables_back, *kept)
    theirs, plane = lax.optimization_barrier((theirs, plane))
    plane = jnp.sum(plane.astype(F32), axis=0).astype(BF16)
    plane = plane.reshape(4, 9, D)
    arrived = other_core(theirs)
    across = (mine[1] + arrived[1].astype(F32)).astype(BF16)

    levels = lax.all_to_all(plane, "zl", 0, 0, tiled=True)
    across, levels = lax.optimization_barrier((across, levels))
    from_y = other_y(across)
    summed = (mine[0] + arrived[0].astype(F32) + from_y.astype(F32)).astype(BF16)
    level = jnp.sum(levels.astype(F32), axis=0).astype(BF16)
    quarters = jnp.broadcast_to(jnp.pad(level, ((0, 3), (0, 0))).reshape(1, 4, 3, D), (2, 4, 3, D)).reshape(8, 3, D)
    spread = lax.all_to_all(quarters, ("c", "x"), 0, 0, tiled=True)
    wanted = lax.dynamic_index_in_dim(spread.reshape(4, 2, 3, D), core, 1, keepdims=False)
    joined = jnp.concatenate([summed, jnp.pad(wanted, ((0, 0), (0, 5), (0, 0)))], axis=1)
    joined = exchange(joined)
    d_hidden = pl.pallas_call(
        home_backward,
        out_shape=jax.ShapeDtypeStruct((ROWS, D), BF16),
        in_specs=[smem, smem, vmem, vmem, vmem, vmem],
        out_specs=vmem,
        scratch_shapes=[pltpu.VMEM((ROWS, D), F32), pltpu.VMEM((16, ROWS, HD), F32)],
        compiler_params=SMALL,
        cost_estimate=cost(30 * ROWS * D, 8 * ROWS * D),
    )(power, spot, rows, cotangent, mod, joined)
    share = jnp.sum(joined[:, TOK : TOK + 3].astype(F32), axis=0).astype(BF16)
    final = lax.all_to_all(jnp.broadcast_to(share[None], (16, 3, D)), CLIP, 0, 0, tiled=True)
    final = final.reshape(4, 12, D)[:, :9].reshape(36, D)
    return d_hidden[None, None], final.astype(F32) / 32.0


def solution(mesh):
    fine = Mesh(mesh.devices.reshape([size for _, size in FINE]), [name for name, _ in FINE])
    placed = (
        P(CLIP, SEQ, None, None),
        P(CLIP, SEQ),
        P(CLIP, None, None, None),
        P(CLIP, SEQ, None, None),
        P(CLIP, None),
        P(CLIP, None),
        P(),
    )
    return jax.shard_map(
        on_device,
        mesh=fine,
        in_specs=placed,
        out_specs=(P(CLIP, SEQ, None, None), P(SEQ, None)),
        check_vma=False,
    )
```
